128 devices in a mesh: loc: 32 (over y, x, core), head: 4 (over z).
Axes of the slice: x: 4, y: 4, z: 4, core: 2. Of those that a mesh axis runs over, the one named last changes fastest.
Arguments:
- entities: bfloat16 [32768, 1024], P('loc', 'head'), may hold values from -9 to 9
- attn_gain: float32 [1024], replicated, may hold values from 0.25 to 1.75
- w_qkv: bfloat16 [3, 1024, 1024], P(None, None, 'head'), may hold values from -1 to 1
- w_out: bfloat16 [1024, 1024], P('head'), may hold values from -0.1875 to 0.1875
- mlp_gain: float32 [1024], replicated, may hold values from 0.25 to 1.75
- w_up: bfloat16 [1024, 4096], P(None, 'head'), may hold values from -0.1875 to 0.1875
- w_down: bfloat16 [4096, 1024], P('head'), may hold values from -0.09375 to 0.09375
- far_owner: int32 [256, 4], P('loc'), may hold values from 0 to 31, all different within a row; in each aligned block of 8 rows (0 to 7, 8 to 15, ...) at most 2 rows name the same one
- far_local: int32 [256, 4], P('loc'), may hold values from 0 to 7
- far_live: int32 [256, 4], P('loc'), may hold values 0 or 1
Outputs:
- encoded: bfloat16 [32768, 1024], P('loc', 'head')
The draws below stay inside these ranges and needn't reach their ends.
Inputs may be any that keep to these rules, and one draw needn't show every extreme that they name: `far_owner`: each row names 4 different owners; among the rows of one index of loc (aligned blocks of 8 rows) no owner is named more than 2 times, a bound that some block reaches.
All inputs are finite; a program needn't handle non-finite values. No bound on the sum of `far_live` on one device may be relied on, other than what follows from the above.
Results may differ from the reference program's by a relative error of at most 0.0065.
Values may be sent and summed in bfloat16 or wider, within the bound.
A program may use at most 128 MiB of HBM per device.

```python
import math
import jax
import jax.numpy as jnp
import numpy as np
from jax import lax

D = 1024
HEADS = 16
HD = 64
FF = 4096
BLK = 128
FAR = 4
NB_DEV = 8
NBLK = 256
ROWS = 32768
MOST = 2
N_LOC = 32


def feature_scale(low, high):
    place = jnp.arange(D, dtype=jnp.float32) / (D - 1)
    return low * jnp.exp(place * jnp.log(high / low))


def draw_entities(key, part):
    values = jnp.clip(jax.random.normal(jax.random.fold_in(key, 11), (ROWS, D), jnp.float32), -6.0, 6.0)
    values = values * feature_scale(0.5, 2.0)[None, :]
    values = jnp.clip(values, -9.0, 9.0)
    return values.astype(jnp.bfloat16)


def draw_w_qkv(key, part):
    values = jax.random.truncated_normal(jax.random.fold_in(key, 21), -4.0, 4.0, (3, D, D), jnp.float32) * D ** (-0.5)
    return values.astype(jnp.bfloat16)


def set_ends(values, stream_key, low, largest):
    spot = [jax.random.randint(jax.random.fold_in(stream_key, axis), (), 0, length) for axis, length in enumerate(values.shape)]
    main_axis = values.shape.index(max(values.shape))
    beside = spot[:main_axis] + [(spot[main_axis] + 1) % values.shape[main_axis]] + spot[main_axis + 1:]
    return values.at[tuple(spot)].set(low).at[tuple(beside)].set(largest)


def levels(rng, dims, cuts, smallest, largest):
    level, own = 1.0, jax.random.fold_in(rng, 6)
    for axis_at, shards_of in cuts:
        draws = jnp.exp(jax.random.uniform(jax.random.fold_in(own, axis_at), (shards_of,), jnp.float32, smallest / len(cuts), largest / len(cuts)))
        level = level * jnp.repeat(draws, dims[axis_at] // shards_of).reshape([-1 if axis == axis_at else 1 for axis in range(len(dims))])
    return level


def assign_block(stream_key, own, number, rows, count, top, bound, slope):
    ranking = jax.random.permutation(stream_key, count)
    heavy_load, usual = load_shares(count, rows * top, bound, slope, True), load_shares(count, rows * top, bound, slope, False)
    places = jnp.arange(count)

    def named(sizes, rotation):
        used = int((sizes > 0).sum())
        fixed = max(1, used // 4)
        shifted = fixed + (places - fixed + rotation * (used - fixed)) % max(1, count - fixed)
        return jnp.zeros((count,), jnp.int32).at[ranking[jnp.where(places < fixed, places, shifted)]].set(jnp.asarray(sizes, jnp.int32))

    sizes = jnp.where(number % 4 == 0, named(heavy_load, number // 4), named(usual, number - number // 4 - 1))
    mixed = jax.random.permutation(jax.random.fold_in(own, 3), count)
    giver, sink = mixed[0:count // 2 * 2:2], mixed[1:count // 2 * 2:2]
    slack = jnp.minimum(sizes[giver] - 1, bound - sizes[sink]) // 2
    slack = jnp.where((giver == ranking[0]) | (sink == ranking[0]) | (sizes[sink] == 0), 0, jnp.maximum(slack, 0))
    shifted = jax.random.randint(jax.random.fold_in(own, 4), (count // 2,), 0, 1 << 20) % (slack + 1)
    sizes = sizes.at[giver].add(-shifted).at[sink].add(shifted)
    labels = jnp.searchsorted(jnp.cumsum(sizes), jnp.arange(rows * top), side="right").astype(jnp.int32)
    table = labels.reshape(top, rows).T
    table = table[jax.random.permutation(jax.random.fold_in(own, 1), rows)]
    rotation = jax.random.randint(jax.random.fold_in(own, 2), (rows, 1), 0, top)
    return jnp.take_along_axis(table, (jnp.arange(top)[None, :] + rotation) % top, axis=1)


def load_shares(count, total, bound, lean, full):
    loads = [(1 << 20) // math.isqrt(rank ** lean) + 1 for rank in range(1, count + 1)]
    largest = bound if full else min(bound, max(-(-total // count), total * loads[0] // sum(loads)))
    least = 1 if total - largest >= count - 1 else 0
    given, rest = [largest] + [least] * (count - 1), total - largest - least * (count - 1)
    while rest > 0:
        free = [i for i in range(1, count) if given[i] < largest] or [i for i in range(1, count) if given[i] < bound]
        mass, budget = sum([loads[i] for i in free]), rest
        for i in free:
            addition = min(bound - given[i], max(1, budget * loads[i] // mass), rest)
            given[i] = given[i] + addition
            rest = rest - addition
    return np.array(given)


def noise(stream_key, dims, scale, reach, cuts=(), held_as=jnp.bfloat16):
    level = levels(stream_key, dims, cuts, -0.22, 0.18) if cuts else 1.0
    entries = jax.random.normal(stream_key, dims, jnp.float32) * scale * level
    return jnp.minimum(jnp.maximum(entries, -reach), reach).astype(held_as)


def setup_inputs(seed: int = 0) -> dict:
    keys = jax.random.split(jax.random.key(seed), 11)
    entities = draw_entities(jax.random.fold_in(keys[10], 71), 0)
    attn_gain = jnp.clip(1.0 + 0.15 * jax.random.normal(keys[1], (D,), jnp.float32), 0.25, 1.75)
    w_qkv = draw_w_qkv(jax.random.fold_in(keys[10], 71), 0)
    w_out = noise(keys[3], (D, D), D ** -0.5, 0.1875, ((0, 4),))
    mlp_gain = jnp.clip(1.0 + 0.15 * jax.random.normal(keys[4], (D,), jnp.float32), 0.25, 1.75)
    w_up = noise(keys[5], (D, FF), D ** -0.5, 0.1875, ((1, 4),))
    w_down = noise(keys[6], (FF, D), FF ** -0.5, 0.09375, ((0, 4),))
    far_owner_keys = jax.random.split(jax.random.fold_in(keys[7], 1), NBLK // NB_DEV)
    far_owner_turns = jax.random.permutation(jax.random.fold_in(keys[7], 3), NBLK // NB_DEV)
    far_owner = jax.vmap(lambda own, number: assign_block(jax.random.fold_in(keys[7], 2), own, number, NB_DEV, N_LOC, FAR, MOST, 2))(far_owner_keys, far_owner_turns).reshape((NBLK, FAR))
    far_local = set_ends(jax.random.randint(keys[8], (NBLK, FAR), 0, NB_DEV), jax.random.fold_in(keys[8], 1), 0, NB_DEV - 1).astype(jnp.int32)
    far_live = set_ends((jax.random.randint(keys[9], (NBLK, FAR), 0, 4) < 3).astype(jnp.int32), jax.random.fold_in(keys[9], 1), 0, 1)
    return {"entities": entities, "attn_gain": attn_gain, "w_qkv": w_qkv, "w_out": w_out, "mlp_gain": mlp_gain, "w_up": w_up, "w_down": w_down, "far_owner": far_owner, "far_local": far_local, "far_live": far_live}


def layer_norm(values, gain):
    center = values - lax.optimization_barrier(jnp.mean(values, axis=-1, keepdims=True))
    spread = lax.optimization_barrier(jnp.mean(center * center, axis=-1, keepdims=True))
    return center * lax.rsqrt(spread + 1e-05) * gain

def reference(entities, attn_gain, w_qkv, w_out, mlp_gain, w_up, w_down, far_owner, far_local, far_live):
    inputs = entities.astype(jnp.float32)
    normed = layer_norm(inputs, attn_gain).astype(jnp.bfloat16)
    queries = jnp.dot(normed, w_qkv[0], preferred_element_type=jnp.float32).astype(jnp.bfloat16)
    key_rows = jnp.dot(normed, w_qkv[1], preferred_element_type=jnp.float32).astype(jnp.bfloat16)
    value_rows = jnp.dot(normed, w_qkv[2], preferred_element_type=jnp.float32).astype(jnp.bfloat16)
    query_tiles = queries.reshape(NBLK, BLK, HEADS, HD)
    key_value = jnp.concatenate([key_rows, value_rows], axis=1).reshape(NBLK, BLK, 2 * D)
    far_ids = (far_owner * NB_DEV + far_local).astype(jnp.int32)
    scale = 1.0 / math.sqrt(HD)

    def one_block(index):
        near = jnp.stack([index - 1, index, index + 1]).astype(jnp.int32)
        listed = jnp.concatenate([near, far_ids[index]]).astype(jnp.int32)
        usable = jnp.concatenate([jnp.stack([index >= 1, index >= 0, index + 1 < NBLK]), far_live[index] == 1])
        picked = key_value[jnp.clip(listed, 0, NBLK - 1)].reshape((3 + FAR) * BLK, 2 * D)
        key_part = picked[:, :D].reshape((3 + FAR) * BLK, HEADS, HD).astype(jnp.float32)
        value_part = picked[:, D:].reshape((3 + FAR) * BLK, HEADS, HD).astype(jnp.float32)
        scores = jnp.einsum('qhd,khd->hqk', query_tiles[index].astype(jnp.float32), key_part) * scale
        key_valid = jnp.repeat(usable, BLK)
        scores = jnp.where(key_valid[None, None, :], scores, -1e+30)
        row_max = lax.optimization_barrier(jnp.max(scores, axis=-1, keepdims=True))
        weights = jnp.exp(scores - row_max)
        totals = lax.optimization_barrier(jnp.sum(weights, axis=-1))
        rounded = weights.astype(jnp.bfloat16).astype(jnp.float32)
        numerator = jnp.einsum('hqk,khd->qhd', rounded, value_part)
        attended = numerator / jnp.transpose(totals)[:, :, None]
        return attended.astype(jnp.bfloat16).reshape(BLK, D)
    attended = lax.map(one_block, jnp.arange(NBLK, dtype=jnp.int32)).reshape(ROWS, D)
    mixed = inputs + jnp.dot(attended, w_out, preferred_element_type=jnp.float32)
    inner = layer_norm(mixed, mlp_gain).astype(jnp.bfloat16)
    hidden = jax.nn.gelu(jnp.dot(inner, w_up, preferred_element_type=jnp.float32), approximate=False).astype(jnp.bfloat16)
    return (mixed + jnp.dot(hidden, w_down, preferred_element_type=jnp.float32)).astype(jnp.bfloat16)
```

```python
import functools

import jax
import jax.numpy as jnp
from jax import lax
from jax.experimental import pallas as pl
from jax.experimental.pallas import tpu as pltpu
from jax.sharding import PartitionSpec as P

MESH = pl.DeviceIdType.MESH
F32 = jnp.float32
BF16 = jnp.bfloat16
BLK = 128
HD = 64
NB = 8
SIDE = 4
CHUNKS = 4
ROWS = NB * BLK
GROUP = ROWS // SIDE
WIDTH = 1024
PART = WIDTH // SIDE
NEG = -1e30
MB = 2**20


def coords():
    loc = lax.axis_index("loc")
    return loc // 8, (loc // 2) % 4, loc % 2, lax.axis_index("head")


def device(y, x, core, z):
    return ((y % 4 * 4 + x % 4) * 2 + core, z % 4)


def shifted(axis, by):
    y, x, core, z = coords()
    if axis == "y":
        return device(y + by + 4, x, core, z)
    if axis == "x":
        return device(y, x + by + 4, core, z)
    if axis == "z":
        return device(y, x, core, z + by + 4)
    return device(y, x, 1 - core, z)


def loc_shifted(by):
    return ((lax.axis_index("loc") + by + 32) % 32, lax.axis_index("head"))


def greet(peers):
    barrier = pltpu.get_barrier_semaphore()
    for peer in peers:
        pl.semaphore_signal(barrier, inc=1, device_id=peer, device_id_type=MESH)
    pl.semaphore_wait(barrier, len(peers))


def remote(src, dst, send, recv, to):
    return pltpu.make_async_remote_copy(
        src_ref=src, dst_ref=dst, send_sem=send, recv_sem=recv, device_id=to, device_id_type=MESH
    )


def norm_rows(values, gain):
    center = values - jnp.mean(values, axis=-1, keepdims=True)
    spread = jnp.mean(center * center, axis=-1, keepdims=True)
    return center * lax.rsqrt(spread + 1e-05) * gain


def split_heads(query):
    zero = jnp.zeros((HD, BLK), query.dtype)
    top = jnp.concatenate([query[:HD], zero], axis=1)
    low = jnp.concatenate([zero, query[HD:]], axis=1)
    return jnp.concatenate([top, low], axis=0)


def gather_kernel(
    ent, gain, wqkv, xbuf, ybuf, near_o, near_st, ent_rows,
    zbuf, xown, yown, halo_low, halo_high,
    zs, zr, xs, xr, ys, yr, cs, cr, hs, hr, ls,
):
    y, x, core, z = coords()
    z_up, z_dn = shifted("z", 1), shifted("z", -1)
    x_up, x_dn = shifted("x", 1), shifted("x", -1)
    y_up, y_dn = shifted("y", 1), shifted("y", -1)
    sib = shifted("c", 0)
    nxt, prv = loc_shifted(1), loc_shifted(-1)
    greet([z_up, z_dn, x_up, x_dn, y_up, y_dn, sib, nxt, prv])
    rows = ROWS // CHUNKS
    blocks = NB // CHUNKS
    pending = []

    def go(copy):
        copy.start()
        pending.append(copy)
        return copy

    z_near = []
    for r in range(CHUNKS):
        at = pl.ds(r * rows, rows)
        z_near.append(
            (
                go(remote(ent.at[at], zbuf.at[z, at], zs.at[r, 0], zr.at[r, 0], z_up)),
                go(remote(ent.at[at], zbuf.at[z, at], zs.at[r, 1], zr.at[r, 1], z_dn)),
            )
        )
    zbuf[z] = ent[...]
    z_far = []

    def z_forward(r):
        a, b = z_near[r]
        low = pl.ds(r * rows, rows // 2)
        high = pl.ds(r * rows + rows // 2, rows // 2)
        a.wait_recv()
        s = (z + 3) % 4
        c = go(remote(zbuf.at[s, low], zbuf.at[s, low], zs.at[r, 2], zr.at[r, 2], z_up))
        b.wait_recv()
        s = (z + 1) % 4
        d = go(remote(zbuf.at[s, high], zbuf.at[s, high], zs.at[r, 3], zr.at[r, 3], z_dn))
        z_far.append((c, d))

    plane = {}
    core_copies = []
    local_copies = []

    def to_sibling(buf, place, blks, sem, src=None):
        view = buf.at[core, place, blks, pl.ds(0, 2)]
        core_copies.append(go(remote(view if src is None else src, view, cs.at[sem], cr.at[sem], sib)))

    def project(r):
        for copy in z_far[r]:
            copy.wait_recv()
        at = pl.ds(r * rows, rows)
        full = jnp.concatenate([zbuf[s, at, :] for s in range(SIDE)], axis=1).astype(F32)
        normed = norm_rows(full, gain[...]).astype(BF16)
        queries = jnp.dot(normed, wqkv[0], preferred_element_type=F32)
        keys = jnp.dot(normed, wqkv[1], preferred_element_type=F32).astype(BF16)
        values = jnp.dot(normed, wqkv[2], preferred_element_type=F32)
        q_t = (queries.T.astype(BF16).astype(F32) * 0.125).astype(BF16)
        v_t = values.T.astype(BF16)
        for i in range(blocks):
            b = r * blocks + i
            cut = slice(i * BLK, (i + 1) * BLK)
            xown[b, 0] = keys[cut, :BLK]
            yown[b, 0] = keys[cut, BLK:]
            xown[b, 1] = v_t[:BLK, cut]
            yown[b, 1] = v_t[BLK:, cut]
            yown[b, 2] = q_t[:BLK, cut]
            xown[b, 2] = q_t[BLK:, cut]
        blks = pl.ds(r * blocks, blocks)
        for name, own, buf, place, send, recv, up, dn, k in (
            ("x", xown, xbuf, x, xs, xr, x_up, x_dn, 0),
            ("y", yown, ybuf, y, ys, yr, y_up, y_dn, 1),
        ):
            src, dst = own.at[blks], buf.at[core, place, blks]
            plane[name, r] = (
                go(remote(src, dst, send.at[r, 0], recv.at[r, 0], up)),
                go(remote(src, dst, send.at[r, 1], recv.at[r, 1], dn)),
            )
            local = pltpu.make_async_copy(src, dst, ls.at[r * 2 + k])
            local.start()
            local_copies.append(local)
            to_sibling(buf, place, blks, r * 10 + k * 5, own.at[blks, pl.ds(0, 2)])

    def plane_forward(r):
        blks = pl.ds(r * blocks, blocks)
        low = pl.ds(r * blocks, blocks // 2)
        high = pl.ds(r * blocks + blocks // 2, blocks // 2)
        for name, buf, place, send, recv, up, dn, k in (
            ("x", xbuf, x, xs, xr, x_up, x_dn, 0),
            ("y", ybuf, y, ys, yr, y_up, y_dn, 1),
        ):
            a, b = plane[name, r]
            a.wait_recv()
            s = (place + 3) % 4
            view = buf.at[core, s, low]
            c = go(remote(view, view, send.at[r, 2], recv.at[r, 2], up))
            to_sibling(buf, s, blks, r * 10 + k * 5 + 1)
            b.wait_recv()
            s = (place + 1) % 4
            view = buf.at[core, s, high]
            d = go(remote(view, view, send.at[r, 3], recv.at[r, 3], dn))
            to_sibling(buf, s, blks, r * 10 + k * 5 + 2)
            plane[name, r] = (c, d)

    def plane_finish(r):
        low = pl.ds(r * blocks, blocks // 2)
        high = pl.ds(r * blocks + blocks // 2, blocks // 2)
        for name, buf, place, k in (("x", xbuf, x, 0), ("y", ybuf, y, 1)):
            c, d = plane[name, r]
            s = (place + 2) % 4
            c.wait_recv()
            to_sibling(buf, s, low, r * 10 + k * 5 + 3)
            d.wait_recv()
            to_sibling(buf, s, high, r * 10 + k * 5 + 4)

    loc = lax.axis_index("loc")

    def near(b):
        for p, (own, other) in enumerate(((xown, yown), (yown, xown))):
            query = split_heads(other[b, 2])
            parts = []
            for step in (-1, 0, 1):
                if b + step < 0:
                    key, val, ok = halo_low[p, 0], halo_low[p, 1], loc > 0
                elif b + step >= NB:
                    key, val, ok = halo_high[p, 0], halo_high[p, 1], loc < 31
                else:
                    key, val, ok = own[b + step, 0], own[b + step, 1], None
                score = jnp.dot(key, query, preferred_element_type=F32)
                if ok is not None:
                    score = jnp.where(ok, score, NEG)
                parts.append((score, val))
            top = functools.reduce(
                jnp.maximum, [jnp.max(score, axis=0, keepdims=True) for score, _ in parts]
            )
            total = jnp.zeros((1, 2 * BLK), F32)
            out = jnp.zeros((BLK, 2 * BLK), F32)
            for score, val in parts:
                weight = jnp.exp(score - top)
                total = total + jnp.sum(weight, axis=0, keepdims=True)
                out = out + jnp.dot(val, weight.astype(BF16), preferred_element_type=F32)
            near_o[b, p] = jnp.concatenate(
                [out[:HD, :BLK] / total[:, :BLK], out[HD:, BLK:] / total[:, BLK:]], axis=0
            )
            near_st[b, p, 0:1] = top[:, :BLK]
            near_st[b, p, 1:2] = top[:, BLK:]
            near_st[b, p, 2:3] = total[:, :BLK]
            near_st[b, p, 3:4] = total[:, BLK:]
            near_st[b, p, 4:8] = jnp.zeros((4, BLK), F32)

    z_forward(0)
    z_forward(1)
    project(0)
    halos = []
    for p, own in enumerate((xown, yown)):
        halos.append(go(remote(own.at[0, pl.ds(0, 2)], halo_high.at[p], hs.at[p], hr.at[p], prv)))
    z_forward(2)
    project(1)
    z_forward(3)
    project(2)
    plane_forward(0)
    project(3)
    for p, own in enumerate((xown, yown)):
        halos.append(
            go(remote(own.at[NB - 1, pl.ds(0, 2)], halo_low.at[p], hs.at[2 + p], hr.at[2 + p], nxt))
        )
    ent_rows[...] = jnp.concatenate(
        [zbuf[s, pl.ds(pl.multiple_of(z * GROUP, GROUP), GROUP), :] for s in range(SIDE)], axis=1
    )
    near(1)
    plane_forward(1)
    near(2)
    near(3)
    plane_forward(2)
    plane_finish(0)
    near(4)
    near(5)
    plane_forward(3)
    plane_finish(1)
    near(6)
    for copy in halos:
        copy.wait_recv()
    near(7)
    plane_finish(2)
    near(0)
    plane_finish(3)
    for copy in core_copies:
        copy.wait_recv()
    for copy in local_copies:
        copy.wait()
    for copy in pending:
        copy.wait_send()


def gather_call(ent, gain, wqkv):
    vmem = pl.BlockSpec(memory_space=pltpu.VMEM)
    hbm = pl.BlockSpec(memory_space=pl.ANY)
    dma = pltpu.SemaphoreType.DMA
    plane_shape = (2, SIDE, NB, 3, BLK, BLK)
    return pl.pallas_call(
        gather_kernel,
        out_shape=(
            jax.ShapeDtypeStruct(plane_shape, BF16),
            jax.ShapeDtypeStruct(plane_shape, BF16),
            jax.ShapeDtypeStruct((NB, 2, BLK, BLK), F32),
            jax.ShapeDtypeStruct((NB, 2, 8, BLK), F32),
            jax.ShapeDtypeStruct((GROUP, WIDTH), BF16),
        ),
        in_specs=[vmem] * 3,
        out_specs=(hbm, hbm, vmem, vmem, vmem),
        scratch_shapes=[
            pltpu.VMEM((SIDE, ROWS, PART), BF16),
            pltpu.VMEM((NB, 3, BLK, BLK), BF16),
            pltpu.VMEM((NB, 3, BLK, BLK), BF16),
            pltpu.VMEM((2, 2, BLK, BLK), BF16),
            pltpu.VMEM((2, 2, BLK, BLK), BF16),
            dma((CHUNKS, 4)), dma((CHUNKS, 4)),
            dma((CHUNKS, 4)), dma((CHUNKS, 4)),
            dma((CHUNKS, 4)), dma((CHUNKS, 4)),
            dma((CHUNKS * 10,)), dma((CHUNKS * 10,)),
            dma((4,)), dma((4,)),
            dma((CHUNKS * 2,)),
        ],
        compiler_params=pltpu.CompilerParams(
            collective_id=0, has_side_effects=True, vmem_limit_bytes=40 * MB
        ),
        name="gather_project",
    )(ent, gain, wqkv)


def far_kernel(tab, xbuf, ybuf, oa, sa, ob, sb, acc, state, hits):
    y, x, core, z = coords()
    live_q = SIDE * NB

    for pair in range(2):
        def find(i, count, pair=pair):
            s, b = i // NB, i % NB
            loc = (s * 4 + x) * 2 + core if pair == 0 else (y * 4 + s) * 2 + core
            base = (loc * NB + b) * 12
            for j in range(4):
                owner, local, live = tab[base + j], tab[base + 4 + j], tab[base + 8 + j]
                oy, ox, oc = owner // 8, (owner // 2) % 4, owner % 2
                if pair == 0:
                    mine, place = oy == y, ox
                else:
                    mine, place = ox == x, oy
                hits[count] = i * 1024 + (oc * 4 + place) * NB + local
                count = count + jnp.where(mine & (live == 1), 1, 0)
            return count

        count = lax.fori_loop(0, live_q, find, 0)
        for extra in range(4):
            hits[count + extra] = live_q * 1024
        keys_ref, query_ref = (xbuf, ybuf) if pair == 0 else (ybuf, xbuf)
        o_ref, s_ref = (oa, sa) if pair == 0 else (ob, sb)

        def clear(i, carry):
            acc[i] = jnp.zeros((BLK, BLK), F32)
            state[i, 0:2] = jnp.full((2, BLK), NEG, F32)
            state[i, 2:8] = jnp.zeros((6, BLK), F32)
            return carry

        lax.fori_loop(0, live_q + 1, clear, 0)

        def four(step, carry):
            work = []
            for u in range(4):
                code = hits[step * 4 + u]
                q, k = code // 1024, code % 1024
                q_at = jnp.minimum(q, live_q - 1)
                query = split_heads(query_ref[core, q_at // NB, q_at % NB, 2])
                kc, kp, kb = k // 32, (k // 8) % 4, k % 8
                key = keys_ref[kc, kp, kb, 0]
                val = keys_ref[kc, kp, kb, 1]
                score = jnp.dot(key, query, preferred_element_type=F32)
                top = jnp.max(score, axis=0, keepdims=True)
                weight = jnp.exp(score - top)
                total = jnp.sum(weight, axis=0, keepdims=True)
                out = jnp.dot(val, weight.astype(BF16), preferred_element_type=F32)
                work.append((q, top, total, out))
            for q, top, total, out in work:
                for h in range(2):
                    cut = slice(h * BLK, (h + 1) * BLK)
                    feat = pl.ds(h * HD, HD)
                    old_top = state[q, h : h + 1]
                    new_top = jnp.maximum(old_top, top[:, cut])
                    keep = jnp.exp(old_top - new_top)
                    add = jnp.exp(top[:, cut] - new_top)
                    acc[q, feat] = acc[q, feat] * keep + out[h * HD : (h + 1) * HD, cut] * add
                    state[q, h : h + 1] = new_top
                    state[q, 2 + h : 3 + h] = state[q, 2 + h : 3 + h] * keep + total[:, cut] * add
            return carry

        lax.fori_loop(0, (count + 3) // 4, four, 0)

        def finish(i, carry):
            s, b = i // NB, i % NB
            st = state[i]
            s_ref[s, b] = st
            for h in range(2):
                total = st[2 + h : 3 + h]
                scale = 1.0 / jnp.where(total > 0, total, 1.0)
                feat = pl.ds(h * HD, HD)
                o_ref[s, b, feat] = (acc[i, feat] * scale).astype(BF16)
            return carry

        lax.fori_loop(0, live_q, finish, 0)


def far_call(tab, xbuf, ybuf):
    vmem = pl.BlockSpec(memory_space=pltpu.VMEM)
    o_shape = jax.ShapeDtypeStruct((SIDE, NB, BLK, BLK), BF16)
    s_shape = jax.ShapeDtypeStruct((SIDE, NB, 8, BLK), F32)
    return pl.pallas_call(
        far_kernel,
        out_shape=(o_shape, s_shape, o_shape, s_shape),
        in_specs=[pl.BlockSpec(memory_space=pltpu.SMEM), vmem, vmem],
        out_specs=(vmem,) * 4,
        scratch_shapes=[
            pltpu.VMEM((SIDE * NB + 1, BLK, BLK), F32),
            pltpu.VMEM((SIDE * NB + 1, 8, BLK), F32),
            pltpu.SMEM((SIDE * NB * 4 + 8,), jnp.int32),
        ],
        compiler_params=pltpu.CompilerParams(vmem_limit_bytes=40 * MB),
        name="far_partials",
    )(tab, xbuf, ybuf)


def merge_kernel(
    oa, sa, ob, sb, near_o, near_st, ent_rows, w_out, gain, mixed, inner,
    ra, rsa, rb, rsb, relay, relay_st, att, part, got_half, got,
    os, orr, fs, fr, zs, zr,
):
    y, x, core, z = coords()
    z_up, z_dn = shifted("z", 1), shifted("z", -1)
    peers = [shifted("y", 1), shifted("y", -1), shifted("x", 1), shifted("x", -1), z_up, z_dn]
    greet(peers)
    pending = []

    def go(copy):
        copy.start()
        pending.append(copy)
        return copy

    half = NB // 2
    lanes = []
    for k, (place, up, dn, o, st, ro, rst) in enumerate(
        (
            (y, peers[0], peers[1], oa, sa, ra, rsa),
            (x, peers[2], peers[3], ob, sb, rb, rsb),
        )
    ):
        far_to, up_to, dn_to = (place + 2) % 4, (place + 1) % 4, (place + 3) % 4
        low, high = pl.ds(0, half), pl.ds(half, half)
        first = []
        for t, (src, hop, dst) in enumerate(((o, relay, ro), (st, relay_st, rst))):
            first.append(
                (
                    go(remote(src.at[far_to, low], hop.at[k, 0], os.at[k, t, 0], orr.at[k, t, 0], up)),
                    go(remote(src.at[far_to, high], hop.at[k, 1], os.at[k, t, 1], orr.at[k, t, 1], dn)),
                )
            )
        direct = []
        for t, (src, dst) in enumerate(((o, ro), (st, rst))):
            direct.append(
                (
                    go(remote(src.at[up_to], dst.at[place], os.at[k, t, 2], orr.at[k, t, 2], up)),
                    go(remote(src.at[dn_to], dst.at[place], os.at[k, t, 3], orr.at[k, t, 3], dn)),
                )
            )
        lanes.append((place, up, dn, ro, rst, first, direct))
    arrivals = []
    for k, (place, up, dn, ro, rst, first, direct) in enumerate(lanes):
        low, high = pl.ds(0, half), pl.ds(half, half)
        for t, (hop, dst) in enumerate(((relay, ro), (relay_st, rst))):
            a, b = first[t]
            a.wait_recv()
            arrivals.append(
                go(remote(hop.at[k, 0], dst.at[(place + 3) % 4, low], fs.at[k, t, 0], fr.at[k, t, 0], up))
            )
            b.wait_recv()
            arrivals.append(
                go(remote(hop.at[k, 1], dst.at[(place + 1) % 4, high], fs.at[k, t, 1], fr.at[k, t, 1], dn))
            )
        for pair in direct:
            arrivals.extend(pair)
    ra[y] = oa[y]
    rsa[y] = sa[y]
    rb[x] = ob[x]
    rsb[x] = sb[x]
    for copy in arrivals:
        copy.wait_recv()

    def merge(b, carry):
        for p, (ro, rst) in enumerate(((ra, rsa), (rb, rsb))):
            stats = [near_st[b, p]] + [rst[s, b] for s in range(SIDE)]
            outs = [near_o[b, p]] + [ro[s, b].astype(F32) for s in range(SIDE)]
            halves = []
            for h in range(2):
                top = functools.reduce(jnp.maximum, [st[h : h + 1] for st in stats])
                scale = [st[2 + h : 3 + h] * jnp.exp(st[h : h + 1] - top) for st in stats]
                inv = 1.0 / functools.reduce(jnp.add, scale)
                halves.append(
                    functools.reduce(
                        jnp.add,
                        [o[h * HD : (h + 1) * HD] * (w * inv) for o, w in zip(outs, scale)],
                    )
                )
            tile = jnp.concatenate(halves, axis=0).T.astype(BF16)
            att[pl.ds(pl.multiple_of(b * BLK, BLK), BLK), p * BLK : (p + 1) * BLK] = tile
        return carry

    lax.fori_loop(0, NB, merge, 0)

    def project(group):
        rows = att[pl.ds(pl.multiple_of(group * GROUP, GROUP), GROUP), :]
        return jnp.dot(rows, w_out[...], preferred_element_type=F32)

    h = GROUP // 2
    part[0] = project((z + 2) % 4).astype(BF16)
    f_up = go(remote(part.at[0, pl.ds(0, h)], got_half.at[0], zs.at[0], zr.at[0], z_up))
    f_dn = go(remote(part.at[0, pl.ds(h, h)], got_half.at[1], zs.at[1], zr.at[1], z_dn))
    to_up = project((z + 1) % 4)
    part[1, h:] = to_up[h:].astype(BF16)
    to_dn = project((z + 3) % 4)
    part[2, :h] = to_dn[:h].astype(BF16)
    f_up.wait_recv()
    part[1, :h] = (to_up[:h] + got_half[0].astype(F32)).astype(BF16)
    s_up = go(remote(part.at[1], got.at[0], zs.at[2], zr.at[2], z_up))
    f_dn.wait_recv()
    part[2, h:] = (to_dn[h:] + got_half[1].astype(F32)).astype(BF16)
    s_dn = go(remote(part.at[2], got.at[1], zs.at[3], zr.at[3], z_dn))
    mine = project(z) + ent_rows[...].astype(F32)
    s_up.wait_recv()
    s_dn.wait_recv()
    total = mine + got[0].astype(F32) + got[1].astype(F32)
    mixed[...] = total
    inner[...] = norm_rows(total, gain[...]).astype(BF16)
    for copy in pending:
        copy.wait_send()


def merge_call(oa, sa, ob, sb, near_o, near_st, ent_rows, w_out, gain):
    vmem = pl.BlockSpec(memory_space=pltpu.VMEM)
    dma = pltpu.SemaphoreType.DMA
    return pl.pallas_call(
        merge_kernel,
        out_shape=(
            jax.ShapeDtypeStruct((GROUP, WIDTH), F32),
            jax.ShapeDtypeStruct((GROUP, WIDTH), BF16),
        ),
        in_specs=[vmem] * 9,
        out_specs=(vmem, vmem),
        scratch_shapes=[
            pltpu.VMEM((SIDE, NB, BLK, BLK), BF16),
            pltpu.VMEM((SIDE, NB, 8, BLK), F32),
            pltpu.VMEM((SIDE, NB, BLK, BLK), BF16),
            pltpu.VMEM((SIDE, NB, 8, BLK), F32),
            pltpu.VMEM((2, 2, NB // 2, BLK, BLK), BF16),
            pltpu.VMEM((2, 2, NB // 2, 8, BLK), F32),
            pltpu.VMEM((ROWS, 2 * BLK), BF16),
            pltpu.VMEM((3, GROUP, WIDTH), BF16),
            pltpu.VMEM((2, GROUP // 2, WIDTH), BF16),
            pltpu.VMEM((2, GROUP, WIDTH), BF16),
            dma((2, 2, 4)), dma((2, 2, 4)),
            dma((2, 2, 2)), dma((2, 2, 2)),
            dma((4,)), dma((4,)),
        ],
        compiler_params=pltpu.CompilerParams(
            collective_id=1, has_side_effects=True, vmem_limit_bytes=40 * MB
        ),
        name="merge_project",
    )(oa, sa, ob, sb, near_o, near_st, ent_rows, w_out, gain)


def gelu(v):
    return 0.5 * v * (1.0 + lax.erf(v * 0.7071067811865476))


def mlp_kernel(inner, mixed, up, down, out, acc, res, landed, ss, rs):
    step = pl.program_id(0)
    last = pl.num_programs(0) - 1
    y, x, core, z = coords()

    @pl.when(step == 0)
    def _():
        greet([shifted("z", 1), shifted("z", 2), shifted("z", 3)])
        acc[...] = mixed[...]

    w_up = up[...].reshape(WIDTH, -1)
    w_down = down[...].reshape(-1, WIDTH)
    hidden = gelu(jnp.dot(inner[...], w_up, preferred_element_type=F32)).astype(BF16)
    acc[...] += jnp.dot(hidden, w_down, preferred_element_type=F32)

    @pl.when(step == last)
    def _():
        final = acc[...].astype(BF16)
        for s in range(SIDE):
            res[s] = final[:, s * PART : (s + 1) * PART]
        here = pl.ds(pl.multiple_of(z * GROUP, GROUP), GROUP)
        copies = []
        for by in (2, 1, 3):
            to = (z + by) % 4
            copies.append(
                remote(res.at[to], landed.at[z], ss.at[by], rs.at[by], shifted("z", by))
            )
            copies[-1].start()
        out[here, :] = res[z]
        for copy in copies:
            copy.wait()
        for by in range(1, SIDE):
            s = (z + by) % 4
            out[pl.ds(pl.multiple_of(s * GROUP, GROUP), GROUP), :] = landed[s]


def mlp_call(inner, mixed, weights, halves):
    vmem = pl.BlockSpec(memory_space=pltpu.VMEM)
    dma = pltpu.SemaphoreType.DMA
    unit = WIDTH // halves
    return pl.pallas_call(
        mlp_kernel,
        grid=(SIDE * halves,),
        out_shape=jax.ShapeDtypeStruct((ROWS, PART), BF16),
        in_specs=[
            vmem,
            vmem,
            pl.BlockSpec((1, 32, 1, 32, unit), lambda i: (i // halves, 0, 0, 0, i % halves)),
            pl.BlockSpec((1, 32 // halves, 1, 32, WIDTH), lambda i: (i // halves, i % halves, 1, 0, 0)),
        ],
        out_specs=vmem,
        scratch_shapes=[
            pltpu.VMEM((GROUP, WIDTH), F32),
            pltpu.VMEM((SIDE, GROUP, PART), BF16),
            pltpu.VMEM((SIDE, GROUP, PART), BF16),
            dma((4,)), dma((4,)),
        ],
        compiler_params=pltpu.CompilerParams(
            collective_id=2, has_side_effects=True, vmem_limit_bytes=40 * MB
        ),
        name="mlp_exchange",
    )(inner, mixed, weights, weights)


def on_device(
    entities, attn_gain, w_qkv, w_out, mlp_gain, w_up, w_down, far_owner, far_local, far_live
):
    loc = lax.axis_index("loc")
    piece = jnp.concatenate(
        [
            lax.dynamic_slice_in_dim(w_up, loc * 32, 32, 0),
            lax.dynamic_slice_in_dim(w_down, loc * 32, 32, 0),
        ],
        axis=0,
    )
    weights = lax.all_gather(piece, ("head", "loc"), axis=0, tiled=True)
    weights = weights.reshape(SIDE, 32, 2, 32, WIDTH)
    tab = jnp.concatenate([far_owner, far_local, far_live], axis=1)
    tab = lax.all_gather(tab, "loc", axis=0, tiled=True).reshape(-1)
    xbuf, ybuf, near_o, near_st, ent_rows = gather_call(
        entities, attn_gain.reshape(1, WIDTH), w_qkv
    )
    oa, sa, ob, sb = far_call(tab, xbuf, ybuf)
    mixed, inner = merge_call(
        oa, sa, ob, sb, near_o, near_st, ent_rows, w_out, mlp_gain.reshape(1, WIDTH)
    )
    return mlp_call(inner, mixed, weights, 2)


def solution(mesh):
    return jax.shard_map(
        on_device,
        mesh=mesh,
        in_specs=(
            P("loc", "head"),
            P(),
            P(None, None, "head"),
            P("head", None),
            P(),
            P(None, "head"),
            P("head", None),
            P("loc", None),
            P("loc", None),
            P("loc", None),
        ),
        out_specs=P("loc", "head"),
        check_vma=False,
    )
```

```python
import functools

import jax
import jax.numpy as jnp
from jax import lax
from jax.experimental import pallas as pl
from jax.experimental.pallas import tpu as pltpu
from jax.sharding import PartitionSpec as P

MESH = pl.DeviceIdType.MESH
F32 = jnp.float32
BF16 = jnp.bfloat16
BLK = 128
HD = 64
NB = 8
SIDE = 4
CHUNKS = 4
ROWS = NB * BLK
GROUP = ROWS // SIDE
WIDTH = 1024
PART = WIDTH // SIDE
NEG = -1e30
MB = 2**20
UNITS = 32


def coords():
    loc = lax.axis_index("loc")
    return loc // 8, (loc // 2) % 4, loc % 2, lax.axis_index("head")


def device(y, x, core, z):
    return ((y % 4 * 4 + x % 4) * 2 + core, z % 4)


def shifted(axis, by):
    y, x, core, z = coords()
    if axis == "y":
        return device(y + by + 4, x, core, z)
    if axis == "x":
        return device(y, x + by + 4, core, z)
    if axis == "z":
        return device(y, x, core, z + by + 4)
    return device(y, x, 1 - core, z)


def loc_shifted(by):
    return ((lax.axis_index("loc") + by + 32) % 32, lax.axis_index("head"))


def greet(peers):
    barrier = pltpu.get_barrier_semaphore()
    for peer in peers:
        pl.semaphore_signal(barrier, inc=1, device_id=peer, device_id_type=MESH)
    pl.semaphore_wait(barrier, len(peers))


def remote(src, dst, send, recv, to):
    return pltpu.make_async_remote_copy(
        src_ref=src, dst_ref=dst, send_sem=send, recv_sem=recv, device_id=to, device_id_type=MESH
    )


def norm_rows(values, gain):
    center = values - jnp.mean(values, axis=-1, keepdims=True)
    spread = jnp.mean(center * center, axis=-1, keepdims=True)
    return center * lax.rsqrt(spread + 1e-05) * gain


def split_heads(query):
    zero = jnp.zeros((HD, BLK), query.dtype)
    top = jnp.concatenate([query[:HD], zero], axis=1)
    low = jnp.concatenate([zero, query[HD:]], axis=1)
    return jnp.concatenate([top, low], axis=0)


def gather_kernel(
    ent, gain, wqkv, owner, local_at, live, up_hbm, down_hbm,
    xbuf, ybuf, near_o, near_st, ent_rows, key_a, key_b, wz, wline,
    zbuf, xown, yown, halo_low, halo_high, tab, tab_y, tab_x, up_cols, up_rows, piece,
    zs, zr, xs, xr, ys, yr, cs, cr, hs, hr, ls, ts, tr, ws, wr, wl,
):
    y, x, core, z = coords()
    loc = lax.axis_index("loc")
    load_up = pltpu.make_async_copy(
        up_hbm.at[:, pl.ds(pl.multiple_of(loc // 4 * BLK, BLK), BLK)], up_cols, wl.at[0]
    )
    load_down = pltpu.make_async_copy(
        down_hbm.at[pl.ds(pl.multiple_of(loc * UNITS, UNITS), UNITS)],
        piece.at[pl.ds(UNITS, UNITS)],
        wl.at[1],
    )
    load_up.start()
    load_down.start()
    tab[...] = jnp.zeros((NB, BLK), jnp.int32)
    tab[:, 0:4] = (owner[...] * NB + local_at[...]) * 2 + live[...]
    z_up, z_dn = shifted("z", 1), shifted("z", -1)
    x_up, x_dn = shifted("x", 1), shifted("x", -1)
    y_up, y_dn = shifted("y", 1), shifted("y", -1)
    sib = shifted("c", 0)
    nxt, prv = loc_shifted(1), loc_shifted(-1)
    w_place = x * (1 - core) + y * core
    w_up_to = device(y + core, x + 1 - core, core, z)
    w_dn_to = device(y + 3 * core, x + 3 * (1 - core), core, z)
    y_opp, x_opp = shifted("y", 2), shifted("x", 2)
    greet([z_up, z_dn, x_up, x_dn, y_up, y_dn, sib, nxt, prv, y_opp, x_opp])
    rows = ROWS // CHUNKS
    blocks = NB // CHUNKS
    pending = []

    def go(copy):
        copy.start()
        pending.append(copy)
        return copy

    z_near = []
    for r in range(CHUNKS):
        at = pl.ds(r * rows, rows)
        z_near.append(
            (
                go(remote(ent.at[at], zbuf.at[z, at], zs.at[r, 0], zr.at[r, 0], z_up)),
                go(remote(ent.at[at], zbuf.at[z, at], zs.at[r, 1], zr.at[r, 1], z_dn)),
            )
        )
    tab_copies = []
    for k, (dst, place, peers) in enumerate(
        ((tab_y, y, (y_up, y_dn, y_opp)), (tab_x, x, (x_up, x_dn, x_opp)))
    ):
        for n, peer in enumerate(peers):
            tab_copies.append(go(remote(tab, dst.at[place], ts.at[k, n], tr.at[k, n], peer)))
    zbuf[z] = ent[...]
    z_far = []

    def z_forward(r):
        a, b = z_near[r]
        low = pl.ds(r * rows, rows // 2)
        high = pl.ds(r * rows + rows // 2, rows // 2)
        a.wait_recv()
        s = (z + 3) % 4
        c = go(remote(zbuf.at[s, low], zbuf.at[s, low], zs.at[r, 2], zr.at[r, 2], z_up))
        b.wait_recv()
        s = (z + 1) % 4
        d = go(remote(zbuf.at[s, high], zbuf.at[s, high], zs.at[r, 3], zr.at[r, 3], z_dn))
        z_far.append((c, d))

    plane = {}
    core_copies = []
    local_copies = []

    def to_sibling(buf, place, blks, sem, src=None):
        view = buf.at[core, place, blks, pl.ds(0, 2)]
        core_copies.append(go(remote(view if src is None else src, view, cs.at[sem], cr.at[sem], sib)))

    def project(r):
        for copy in z_far[r]:
            copy.wait_recv()
        at = pl.ds(r * rows, rows)
        full = jnp.concatenate([zbuf[s, at, :] for s in range(SIDE)], axis=1).astype(F32)
        normed = norm_rows(full, gain[...]).astype(BF16)
        queries = jnp.dot(normed, wqkv[0], preferred_element_type=F32)
        keys = jnp.dot(normed, wqkv[1], preferred_element_type=F32).astype(BF16)
        values = jnp.dot(normed, wqkv[2], preferred_element_type=F32)
        q_t = (queries.T.astype(BF16).astype(F32) * 0.125).astype(BF16)
        v_t = values.T.astype(BF16)
        for i in range(blocks):
            b = r * blocks + i
            cut = slice(i * BLK, (i + 1) * BLK)
            xown[b, 0] = keys[cut, :BLK]
            yown[b, 0] = keys[cut, BLK:]
            xown[b, 1] = v_t[:BLK, cut]
            yown[b, 1] = v_t[BLK:, cut]
            yown[b, 2] = q_t[:BLK, cut]
            xown[b, 2] = q_t[BLK:, cut]
        blks = pl.ds(r * blocks, blocks)
        for name, own, buf, place, send, recv, up, dn, k in (
            ("x", xown, xbuf, x, xs, xr, x_up, x_dn, 0),
            ("y", yown, ybuf, y, ys, yr, y_up, y_dn, 1),
        ):
            src, dst = own.at[blks], buf.at[core, place, blks]
            plane[name, r] = (
                go(remote(src, dst, send.at[r, 0], recv.at[r, 0], up)),
                go(remote(src, dst, send.at[r, 1], recv.at[r, 1], dn)),
            )
            local = pltpu.make_async_copy(src, dst, ls.at[r * 2 + k])
            local.start()
            local_copies.append(local)
            to_sibling(buf, place, blks, r * 10 + k * 5, own.at[blks, pl.ds(0, 2)])

    def plane_forward(r):
        blks = pl.ds(r * blocks, blocks)
        low = pl.ds(r * blocks, blocks // 2)
        high = pl.ds(r * blocks + blocks // 2, blocks // 2)
        for name, buf, place, send, recv, up, dn, k in (
            ("x", xbuf, x, xs, xr, x_up, x_dn, 0),
            ("y", ybuf, y, ys, yr, y_up, y_dn, 1),
        ):
            a, b = plane[name, r]
            a.wait_recv()
            s = (place + 3) % 4
            view = buf.at[core, s, low]
            c = go(remote(view, view, send.at[r, 2], recv.at[r, 2], up))
            to_sibling(buf, s, blks, r * 10 + k * 5 + 1)
            b.wait_recv()
            s = (place + 1) % 4
            view = buf.at[core, s, high]
            d = go(remote(view, view, send.at[r, 3], recv.at[r, 3], dn))
            to_sibling(buf, s, blks, r * 10 + k * 5 + 2)
            plane[name, r] = (c, d)

    def plane_finish(r):
        low = pl.ds(r * blocks, blocks // 2)
        high = pl.ds(r * blocks + blocks // 2, blocks // 2)
        for name, buf, place, k in (("x", xbuf, x, 0), ("y", ybuf, y, 1)):
            c, d = plane[name, r]
            s = (place + 2) % 4
            c.wait_recv()
            to_sibling(buf, s, low, r * 10 + k * 5 + 3)
            d.wait_recv()
            to_sibling(buf, s, high, r * 10 + k * 5 + 4)

    def near(b):
        for p, (own, other) in enumerate(((xown, yown), (yown, xown))):
            query = split_heads(other[b, 2])
            parts = []
            for step in (-1, 0, 1):
                if b + step < 0:
                    key, val, ok = halo_low[p, 0], halo_low[p, 1], loc > 0
                elif b + step >= NB:
                    key, val, ok = halo_high[p, 0], halo_high[p, 1], loc < 31
                else:
                    key, val, ok = own[b + step, 0], own[b + step, 1], None
                score = jnp.dot(key, query, preferred_element_type=F32)
                if ok is not None:
                    score = jnp.where(ok, score, NEG)
                parts.append((score, val))
            top = functools.reduce(
                jnp.maximum, [jnp.max(score, axis=0, keepdims=True) for score, _ in parts]
            )
            total = jnp.zeros((1, 2 * BLK), F32)
            out = jnp.zeros((BLK, 2 * BLK), F32)
            for score, val in parts:
                weight = jnp.exp(score - top)
                total = total + jnp.sum(weight, axis=0, keepdims=True)
                out = out + jnp.dot(val, weight.astype(BF16), preferred_element_type=F32)
            near_o[b, p] = jnp.concatenate(
                [out[:HD, :BLK] / total[:, :BLK], out[HD:, BLK:] / total[:, BLK:]], axis=0
            )
            near_st[b, p, 0:1] = top[:, :BLK]
            near_st[b, p, 1:2] = top[:, BLK:]
            near_st[b, p, 2:3] = total[:, :BLK]
            near_st[b, p, 3:4] = total[:, BLK:]
            near_st[b, p, 4:8] = jnp.zeros((4, BLK), F32)

    load_up.wait()
    load_down.wait()
    up_rows[...] = up_cols[...].astype(F32).T
    piece[0:UNITS] = up_rows[pl.ds(pl.multiple_of(loc % 4 * UNITS, UNITS), UNITS)].astype(BF16)
    w_local = pltpu.make_async_copy(piece, wz.at[z], wl.at[2])
    w_local.start()
    wz_a = go(remote(piece, wz.at[z], ws.at[0], wr.at[0], z_up))
    wz_b = go(remote(piece, wz.at[z], ws.at[1], wr.at[1], z_dn))
    tab_y[y] = tab[...]
    tab_x[x] = tab[...]
    z_forward(0)
    z_forward(1)
    project(0)
    halos = []
    for p, own in enumerate((xown, yown)):
        halos.append(go(remote(own.at[0, pl.ds(0, 2)], halo_high.at[p], hs.at[p], hr.at[p], prv)))
    z_forward(2)
    project(1)
    z_forward(3)
    low, high = pl.ds(0, UNITS), pl.ds(UNITS, UNITS)
    wz_a.wait_recv()
    view = wz.at[(z + 3) % 4, low]
    wz_c = go(remote(view, view, ws.at[2], wr.at[2], z_up))
    wz_b.wait_recv()
    view = wz.at[(z + 1) % 4, high]
    wz_d = go(remote(view, view, ws.at[3], wr.at[3], z_dn))
    project(2)
    plane_forward(0)
    project(3)
    for p, own in enumerate((xown, yown)):
        halos.append(
            go(remote(own.at[NB - 1, pl.ds(0, 2)], halo_low.at[p], hs.at[2 + p], hr.at[2 + p], nxt))
        )
    ent_rows[...] = jnp.concatenate(
        [zbuf[s, pl.ds(pl.multiple_of(z * GROUP, GROUP), GROUP), :] for s in range(SIDE)], axis=1
    )
    near(1)
    plane_forward(1)
    near(2)
    near(3)
    plane_forward(2)
    plane_finish(0)
    near(4)
    near(5)
    plane_forward(3)
    plane_finish(1)
    wz_c.wait_recv()
    wz_d.wait_recv()
    w_local.wait()
    wl_a = go(remote(wz, wline.at[w_place], ws.at[4], wr.at[4], w_up_to))
    wl_b = go(remote(wz, wline.at[w_place], ws.at[5], wr.at[5], w_dn_to))
    w_local = pltpu.make_async_copy(wz, wline.at[w_place], wl.at[3])
    w_local.start()
    near(6)
    for copy in halos:
        copy.wait_recv()
    near(7)
    plane_finish(2)
    near(0)
    for copy in tab_copies:
        copy.wait_recv()
    code = tab_y[...]
    at_key = code // 16 % 2 * 32 + code // 32 % 4 * NB + code // 2 % NB
    key_a[...] = jnp.where((code % 2 == 1) & (code // 128 == y), at_key, -1)
    code = tab_x[...]
    at_key = code // 16 % 2 * 32 + code // 128 * NB + code // 2 % NB
    key_b[...] = jnp.where((code % 2 == 1) & (code // 32 % 4 == x), at_key, -1)
    plane_finish(3)
    wl_a.wait_recv()
    view = wline.at[(w_place + 3) % 4, pl.ds(0, 2)]
    wl_c = go(remote(view, view, ws.at[6], wr.at[6], w_up_to))
    wl_b.wait_recv()
    view = wline.at[(w_place + 1) % 4, pl.ds(2, 2)]
    wl_d = go(remote(view, view, ws.at[7], wr.at[7], w_dn_to))
    wl_c.wait_recv()
    wl_d.wait_recv()
    w_local.wait()
    for copy in core_copies:
        copy.wait_recv()
    for copy in local_copies:
        copy.wait()
    for copy in pending:
        copy.wait_send()


def gather_call(ent, gain, wqkv, owner, local_at, live, w_up, w_down):
    vmem = pl.BlockSpec(memory_space=pltpu.VMEM)
    hbm = pl.BlockSpec(memory_space=pl.ANY)
    dma = pltpu.SemaphoreType.DMA
    plane_shape = (2, SIDE, NB, 3, BLK, BLK)
    return pl.pallas_call(
        gather_kernel,
        out_shape=(
            jax.ShapeDtypeStruct(plane_shape, BF16),
            jax.ShapeDtypeStruct(plane_shape, BF16),
            jax.ShapeDtypeStruct((NB, 2, BLK, BLK), F32),
            jax.ShapeDtypeStruct((NB, 2, 8, BLK), F32),
            jax.ShapeDtypeStruct((GROUP, WIDTH), BF16),
            jax.ShapeDtypeStruct((SIDE, NB, BLK), jnp.int32),
            jax.ShapeDtypeStruct((SIDE, NB, BLK), jnp.int32),
            jax.ShapeDtypeStruct((SIDE, 2 * UNITS, WIDTH), BF16),
            jax.ShapeDtypeStruct((SIDE, SIDE, 2 * UNITS, WIDTH), BF16),
        ),
        in_specs=[vmem] * 6 + [hbm] * 2,
        out_specs=(hbm, hbm, vmem, vmem, vmem, vmem, vmem, hbm, hbm),
        scratch_shapes=[
            pltpu.VMEM((SIDE, ROWS, PART), BF16),
            pltpu.VMEM((NB, 3, BLK, BLK), BF16),
            pltpu.VMEM((NB, 3, BLK, BLK), BF16),
            pltpu.VMEM((2, 2, BLK, BLK), BF16),
            pltpu.VMEM((2, 2, BLK, BLK), BF16),
            pltpu.VMEM((NB, BLK), jnp.int32),
            pltpu.VMEM((SIDE, NB, BLK), jnp.int32),
            pltpu.VMEM((SIDE, NB, BLK), jnp.int32),
            pltpu.VMEM((WIDTH, BLK), BF16),
            pltpu.VMEM((BLK, WIDTH), F32),
            pltpu.VMEM((2 * UNITS, WIDTH), BF16),
            dma((CHUNKS, 4)), dma((CHUNKS, 4)),
            dma((CHUNKS, 4)), dma((CHUNKS, 4)),
            dma((CHUNKS, 4)), dma((CHUNKS, 4)),
            dma((CHUNKS * 10,)), dma((CHUNKS * 10,)),
            dma((4,)), dma((4,)),
            dma((CHUNKS * 2,)),
            dma((2, 3)), dma((2, 3)),
            dma((8,)), dma((8,)),
            dma((4,)),
        ],
        compiler_params=pltpu.CompilerParams(
            collective_id=0, has_side_effects=True, vmem_limit_bytes=40 * MB
        ),
        name="gather_project",
    )(ent, gain, wqkv, owner, local_at, live, w_up, w_down)


def far_kernel(key_a, key_b, x_hbm, y_hbm, oa, sa, ob, sb, xbuf, ybuf, acc, state, hits_a, hits_b, sems):
    core = lax.axis_index("loc") % 2
    live_q = SIDE * NB
    loads = [
        pltpu.make_async_copy(x_hbm, xbuf, sems.at[0]),
        pltpu.make_async_copy(y_hbm, ybuf, sems.at[1]),
    ]
    for load in loads:
        load.start()

    def find(i, counts):
        count_a, count_b = counts
        s, b = i // NB, i % NB
        for j in range(4):
            key = key_a[s, b, j]
            hits_a[count_a] = i * 1024 + key
            count_a = count_a + jnp.where(key >= 0, 1, 0)
            key = key_b[s, b, j]
            hits_b[count_b] = i * 1024 + key
            count_b = count_b + jnp.where(key >= 0, 1, 0)
        return count_a, count_b

    counts = lax.fori_loop(0, live_q, find, (0, 0))
    for hits, count in zip((hits_a, hits_b), counts):
        for extra in range(4):
            hits[count + extra] = live_q * 1024

    def clear(i, carry):
        acc[i] = jnp.zeros((BLK, BLK), F32)
        state[i, 0:2] = jnp.full((2, BLK), NEG, F32)
        state[i, 2:8] = jnp.zeros((6, BLK), F32)
        return carry

    lax.fori_loop(0, 2 * (live_q + 1), clear, 0)
    for load in loads:
        load.wait()

    for pair in range(2):
        hits, count = (hits_a, counts[0]) if pair == 0 else (hits_b, counts[1])
        keys_ref, query_ref = (xbuf, ybuf) if pair == 0 else (ybuf, xbuf)
        o_ref, s_ref = (oa, sa) if pair == 0 else (ob, sb)
        base = pair * (live_q + 1)

        def four(step, carry):
            work = []
            for u in range(4):
                code = hits[step * 4 + u]
                q, k = code // 1024, code % 1024
                q_at = jnp.minimum(q, live_q - 1)
                query = split_heads(query_ref[core, q_at // NB, q_at % NB, 2])
                kc, kp, kb = k // 32, (k // 8) % 4, k % 8
                key = keys_ref[kc, kp, kb, 0]
                val = keys_ref[kc, kp, kb, 1]
                score = jnp.dot(key, query, preferred_element_type=F32)
                top = jnp.max(score, axis=0, keepdims=True)
                weight = jnp.exp(score - top)
                total = jnp.sum(weight, axis=0, keepdims=True)
                out = jnp.dot(val, weight.astype(BF16), preferred_element_type=F32)
                work.append((q + base, top, total, out))
            for q, top, total, out in work:
                for h in range(2):
                    cut = slice(h * BLK, (h + 1) * BLK)
                    feat = pl.ds(h * HD, HD)
                    old_top = state[q, h : h + 1]
                    new_top = jnp.maximum(old_top, top[:, cut])
                    keep = jnp.exp(old_top - new_top)
                    add = jnp.exp(top[:, cut] - new_top)
                    acc[q, feat] = acc[q, feat] * keep + out[h * HD : (h + 1) * HD, cut] * add
                    state[q, h : h + 1] = new_top
                    state[q, 2 + h : 3 + h] = state[q, 2 + h : 3 + h] * keep + total[:, cut] * add
            return carry

        lax.fori_loop(0, (count + 3) // 4, four, 0)

        def finish(i, carry):
            s, b = i // NB, i % NB
            st = state[base + i]
            s_ref[s, b] = st
            for h in range(2):
                total = st[2 + h : 3 + h]
                scale = 1.0 / jnp.where(total > 0, total, 1.0)
                feat = pl.ds(h * HD, HD)
                o_ref[s, b, feat] = (acc[base + i, feat] * scale).astype(BF16)
            return carry

        lax.fori_loop(0, live_q, finish, 0)


def far_call(key_a, key_b, xbuf, ybuf):
    vmem = pl.BlockSpec(memory_space=pltpu.VMEM)
    smem = pl.BlockSpec(memory_space=pltpu.SMEM)
    hbm = pl.BlockSpec(memory_space=pl.ANY)
    o_shape = jax.ShapeDtypeStruct((SIDE, NB, BLK, BLK), BF16)
    s_shape = jax.ShapeDtypeStruct((SIDE, NB, 8, BLK), F32)
    return pl.pallas_call(
        far_kernel,
        out_shape=(o_shape, s_shape, o_shape, s_shape),
        in_specs=[smem, smem, hbm, hbm],
        out_specs=(vmem,) * 4,
        scratch_shapes=[
            pltpu.VMEM(xbuf.shape, BF16),
            pltpu.VMEM(ybuf.shape, BF16),
            pltpu.VMEM((2 * (SIDE * NB + 1), BLK, BLK), F32),
            pltpu.VMEM((2 * (SIDE * NB + 1), 8, BLK), F32),
            pltpu.SMEM((SIDE * NB * 4 + 8,), jnp.int32),
            pltpu.SMEM((SIDE * NB * 4 + 8,), jnp.int32),
            pltpu.SemaphoreType.DMA((2,)),
        ],
        compiler_params=pltpu.CompilerParams(vmem_limit_bytes=40 * MB),
        name="far_partials",
    )(key_a, key_b, xbuf, ybuf)


def merge_kernel(
    oa, sa, ob, sb, near_o, near_st, ent_rows, w_out, gain, wline, result,
    ra, rsa, rb, rsb, relay, relay_st, att, part, got_half, got,
    weights, inner, acc, send_sib, got_sib, res, landed,
    os, orr, fs, fr, zs, zr, ws, wr, wl, ss, sr, es, er,
):
    y, x, core, z = coords()
    z_up, z_dn = shifted("z", 1), shifted("z", -1)
    z_opp, sib = shifted("z", 2), shifted("c", 0)
    peers = [shifted("y", 1), shifted("y", -1), shifted("x", 1), shifted("x", -1), z_up, z_dn]
    w_place = y * (1 - core) + x * core
    w_up_to = device(y + 1 - core, x + core, core, z)
    w_dn_to = device(y + 3 * (1 - core), x + 3 * core, core, z)
    greet(peers + [z_opp, sib])
    w_local = pltpu.make_async_copy(wline, weights.at[w_place], wl)
    w_local.start()
    pending = []

    def go(copy):
        copy.start()
        pending.append(copy)
        return copy

    half = NB // 2
    lanes = []
    for k, (place, up, dn, o, st, ro, rst) in enumerate(
        (
            (y, peers[0], peers[1], oa, sa, ra, rsa),
            (x, peers[2], peers[3], ob, sb, rb, rsb),
        )
    ):
        far_to, up_to, dn_to = (place + 2) % 4, (place + 1) % 4, (place + 3) % 4
        low, high = pl.ds(0, half), pl.ds(half, half)
        first = []
        for t, (src, hop, dst) in enumerate(((o, relay, ro), (st, relay_st, rst))):
            first.append(
                (
                    go(remote(src.at[far_to, low], hop.at[k, 0], os.at[k, t, 0], orr.at[k, t, 0], up)),
                    go(remote(src.at[far_to, high], hop.at[k, 1], os.at[k, t, 1], orr.at[k, t, 1], dn)),
                )
            )
        direct = []
        for t, (src, dst) in enumerate(((o, ro), (st, rst))):
            direct.append(
                (
                    go(remote(src.at[up_to], dst.at[place], os.at[k, t, 2], orr.at[k, t, 2], up)),
                    go(remote(src.at[dn_to], dst.at[place], os.at[k, t, 3], orr.at[k, t, 3], dn)),
                )
            )
        lanes.append((place, up, dn, ro, rst, first, direct))
    arrivals = []
    for k, (place, up, dn, ro, rst, first, direct) in enumerate(lanes):
        low, high = pl.ds(0, half), pl.ds(half, half)
        for t, (hop, dst) in enumerate(((relay, ro), (relay_st, rst))):
            a, b = first[t]
            a.wait_recv()
            arrivals.append(
                go(remote(hop.at[k, 0], dst.at[(place + 3) % 4, low], fs.at[k, t, 0], fr.at[k, t, 0], up))
            )
            b.wait_recv()
            arrivals.append(
                go(remote(hop.at[k, 1], dst.at[(place + 1) % 4, high], fs.at[k, t, 1], fr.at[k, t, 1], dn))
            )
        for pair in direct:
            arrivals.extend(pair)
    w_up_copies, w_dn_copies = [None] * 4, [None] * 4
    for n in range(SIDE):
        u, d = n, (n + 2) % 4
        dst = weights.at[w_place]
        w_up_copies[u] = go(remote(wline.at[u], dst.at[u], ws.at[0, u], wr.at[0, u], w_up_to))
        w_dn_copies[d] = go(remote(wline.at[d], dst.at[d], ws.at[1, d], wr.at[1, d], w_dn_to))
    w_far = []

    def weights_forward(n):
        w_up_copies[n].wait_recv()
        view = weights.at[(w_place + 3) % 4, n]
        w_far.append(go(remote(view, view, ws.at[2, n], wr.at[2, n], w_up_to)))
        w_dn_copies[n + 2].wait_recv()
        view = weights.at[(w_place + 1) % 4, n + 2]
        w_far.append(go(remote(view, view, ws.at[2, n + 2], wr.at[2, n + 2], w_dn_to)))

    ra[y] = oa[y]
    rsa[y] = sa[y]
    rb[x] = ob[x]
    rsb[x] = sb[x]
    for copy in arrivals:
        copy.wait_recv()

    def merge(b, carry):
        for p, (ro, rst) in enumerate(((ra, rsa), (rb, rsb))):
            stats = [near_st[b, p]] + [rst[s, b] for s in range(SIDE)]
            outs = [near_o[b, p]] + [ro[s, b].astype(F32) for s in range(SIDE)]
            halves = []
            for h in range(2):
                top = functools.reduce(jnp.maximum, [st[h : h + 1] for st in stats])
                scale = [st[2 + h : 3 + h] * jnp.exp(st[h : h + 1] - top) for st in stats]
                inv = 1.0 / functools.reduce(jnp.add, scale)
                halves.append(
                    functools.reduce(
                        jnp.add,
                        [o[h * HD : (h + 1) * HD] * (w * inv) for o, w in zip(outs, scale)],
                    )
                )
            tile = jnp.concatenate(halves, axis=0).T.astype(BF16)
            att[pl.ds(pl.multiple_of(b * BLK, BLK), BLK), p * BLK : (p + 1) * BLK] = tile
        return carry

    lax.fori_loop(0, NB, merge, 0)

    def project(group):
        rows = att[pl.ds(pl.multiple_of(group * GROUP, GROUP), GROUP), :]
        return jnp.dot(rows, w_out[...], preferred_element_type=F32)

    h = GROUP // 2
    part[0] = project((z + 2) % 4).astype(BF16)
    f_up = go(remote(part.at[0, pl.ds(0, h)], got_half.at[0], zs.at[0], zr.at[0], z_up))
    f_dn = go(remote(part.at[0, pl.ds(h, h)], got_half.at[1], zs.at[1], zr.at[1], z_dn))
    to_up = project((z + 1) % 4)
    part[1, h:] = to_up[h:].astype(BF16)
    to_dn = project((z + 3) % 4)
    part[2, :h] = to_dn[:h].astype(BF16)
    f_up.wait_recv()
    part[1, :h] = (to_up[:h] + got_half[0].astype(F32)).astype(BF16)
    s_up = go(remote(part.at[1], got.at[0], zs.at[2], zr.at[2], z_up))
    f_dn.wait_recv()
    part[2, h:] = (to_dn[h:] + got_half[1].astype(F32)).astype(BF16)
    s_dn = go(remote(part.at[2], got.at[1], zs.at[3], zr.at[3], z_dn))
    mine = project(z) + ent_rows[...].astype(F32)
    weights_forward(0)
    s_up.wait_recv()
    s_dn.wait_recv()
    mixed = mine + got[0].astype(F32) + got[1].astype(F32)
    inner[core] = norm_rows(mixed, gain[...]).astype(BF16)
    to_sib = go(remote(inner.at[core], inner.at[core], ss.at[0], sr.at[0], sib))
    acc[core] = mixed
    acc[1 - core] = jnp.zeros((GROUP, WIDTH), F32)
    weights_forward(1)
    w_local.wait()

    def mlp(slot, who):
        w_up = weights[slot, :, :, 0:UNITS].reshape(SIDE * SIDE * UNITS, WIDTH)
        w_down = weights[slot, :, :, UNITS:].reshape(SIDE * SIDE * UNITS, WIDTH)
        hidden = lax.dot_general(
            inner[who], w_up, (((1,), (1,)), ((), ())), preferred_element_type=F32
        )
        acc[who] += jnp.dot(gelu(hidden).astype(BF16), w_down, preferred_element_type=F32)

    def mlp_both(slot):
        def body(t, carry):
            mlp(slot, (core + 1 + t) % 2)
            return carry

        lax.fori_loop(0, 2, body, 0)

    to_sib.wait_recv()
    mlp_both(w_place)
    w_up_copies[2].wait_recv()
    w_up_copies[3].wait_recv()
    mlp_both((w_place + 3) % 4)
    w_dn_copies[0].wait_recv()
    w_dn_copies[1].wait_recv()
    mlp_both((w_place + 1) % 4)
    for copy in w_far:
        copy.wait_recv()
    mlp((w_place + 2) % 4, 1 - core)
    send_sib[...] = acc[1 - core].astype(BF16)
    back = go(remote(send_sib, got_sib, ss.at[1], sr.at[1], sib))
    mlp((w_place + 2) % 4, core)
    back.wait_recv()
    final = (acc[core] + got_sib[...].astype(F32)).astype(BF16)
    for s in range(SIDE):
        res[s] = final[:, s * PART : (s + 1) * PART]
    copies = []
    for n, to in ((2, z_opp), (1, z_up), (3, z_dn)):
        copies.append(go(remote(res.at[(z + n) % 4], landed.at[z], es.at[n], er.at[n], to)))
    result[pl.ds(pl.multiple_of(z * GROUP, GROUP), GROUP), :] = res[z]
    for copy in copies:
        copy.wait_recv()
    for n in range(1, SIDE):
        s = (z + n) % 4
        result[pl.ds(pl.multiple_of(s * GROUP, GROUP), GROUP), :] = landed[s]
    for copy in pending:
        copy.wait_send()


def gelu(v):
    return 0.5 * v * (1.0 + lax.erf(v * 0.7071067811865476))


def merge_call(oa, sa, ob, sb, near_o, near_st, ent_rows, w_out, gain, wline):
    vmem = pl.BlockSpec(memory_space=pltpu.VMEM)
    dma = pltpu.SemaphoreType.DMA
    return pl.pallas_call(
        merge_kernel,
        out_shape=jax.ShapeDtypeStruct((ROWS, PART), BF16),
        in_specs=[vmem] * 9 + [pl.BlockSpec(memory_space=pl.ANY)],
        out_specs=vmem,
        scratch_shapes=[
            pltpu.VMEM((SIDE, NB, BLK, BLK), BF16),
            pltpu.VMEM((SIDE, NB, 8, BLK), F32),
            pltpu.VMEM((SIDE, NB, BLK, BLK), BF16),
            pltpu.VMEM((SIDE, NB, 8, BLK), F32),
            pltpu.VMEM((2, 2, NB // 2, BLK, BLK), BF16),
            pltpu.VMEM((2, 2, NB // 2, 8, BLK), F32),
            pltpu.VMEM((ROWS, 2 * BLK), BF16),
            pltpu.VMEM((3, GROUP, WIDTH), BF16),
            pltpu.VMEM((2, GROUP // 2, WIDTH), BF16),
            pltpu.VMEM((2, GROUP, WIDTH), BF16),
            pltpu.VMEM((SIDE, SIDE, SIDE, 2 * UNITS, WIDTH), BF16),
            pltpu.VMEM((2, GROUP, WIDTH), BF16),
            pltpu.VMEM((2, GROUP, WIDTH), F32),
            pltpu.VMEM((GROUP, WIDTH), BF16),
            pltpu.VMEM((GROUP, WIDTH), BF16),
            pltpu.VMEM((SIDE, GROUP, PART), BF16),
            pltpu.VMEM((SIDE, GROUP, PART), BF16),
            dma((2, 2, 4)), dma((2, 2, 4)),
            dma((2, 2, 2)), dma((2, 2, 2)),
            dma((4,)), dma((4,)),
            dma((3, 4)), dma((3, 4)), dma,
            dma((2,)), dma((2,)),
            dma((4,)), dma((4,)),
        ],
        compiler_params=pltpu.CompilerParams(
            collective_id=1, has_side_effects=True, vmem_limit_bytes=40 * MB
        ),
        name="merge_project",
    )(oa, sa, ob, sb, near_o, near_st, ent_rows, w_out, gain, wline)


def on_device(
    entities, attn_gain, w_qkv, w_out, mlp_gain, w_up, w_down, far_owner, far_local, far_live
):
    xbuf, ybuf, near_o, near_st, ent_rows, key_a, key_b, _, wline = gather_call(
        entities,
        attn_gain.reshape(1, WIDTH),
        w_qkv,
        far_owner,
        far_local,
        far_live,
        w_up,
        w_down,
    )
    oa, sa, ob, sb = far_call(key_a, key_b, xbuf, ybuf)
    return merge_call(
        oa, sa, ob, sb, near_o, near_st, ent_rows, w_out, mlp_gain.reshape(1, WIDTH), wline
    )


def solution(mesh):
    return jax.shard_map(
        on_device,
        mesh=mesh,
        in_specs=(
            P("loc", "head"),
            P(),
            P(None, None, "head"),
            P("head", None),
            P(),
            P(None, "head"),
            P("head", None),
            P("loc", None),
            P("loc", None),
            P("loc", None),
        ),
        out_specs=P("loc", "head"),
        check_vma=False,
    )
```

```python
import functools

import jax
import jax.numpy as jnp
from jax import lax
from jax.experimental import pallas as pl
from jax.experimental.pallas import tpu as pltpu
from jax.sharding import PartitionSpec as P

MESH = pl.DeviceIdType.MESH
F32 = jnp.float32
BF16 = jnp.bfloat16
BLK = 128
HD = 64
NB = 8
SIDE = 4
CHUNKS = 4
ROWS = NB * BLK
GROUP = ROWS // SIDE
WIDTH = 1024
PART = WIDTH // SIDE
NEG = -1e30
MB = 2**20
UNITS = 32


def coords():
    loc = lax.axis_index("loc")
    return loc // 8, (loc // 2) % 4, loc % 2, lax.axis_index("head")


def device(y, x, core, z):
    return ((y % 4 * 4 + x % 4) * 2 + core, z % 4)


def shifted(axis, by):
    y, x, core, z = coords()
    if axis == "y":
        return device(y + by + 4, x, core, z)
    if axis == "x":
        return device(y, x + by + 4, core, z)
    if axis == "z":
        return device(y, x, core, z + by + 4)
    return device(y, x, 1 - core, z)


def loc_shifted(by):
    return ((lax.axis_index("loc") + by + 32) % 32, lax.axis_index("head"))


def greet(peers):
    barrier = pltpu.get_barrier_semaphore()
    for peer in peers:
        pl.semaphore_signal(barrier, inc=1, device_id=peer, device_id_type=MESH)


def greeted(peers):
    pl.semaphore_wait(pltpu.get_barrier_semaphore(), len(peers))


def remote(src, dst, send, recv, to):
    return pltpu.make_async_remote_copy(
        src_ref=src, dst_ref=dst, send_sem=send, recv_sem=recv, device_id=to, device_id_type=MESH
    )


def norm_rows(values, gain):
    center = values - jnp.mean(values, axis=-1, keepdims=True)
    spread = jnp.mean(center * center, axis=-1, keepdims=True)
    return center * lax.rsqrt(spread + 1e-05) * gain


def split_heads(query):
    zero = jnp.zeros((HD, BLK), query.dtype)
    top = jnp.concatenate([query[:HD], zero], axis=1)
    low = jnp.concatenate([zero, query[HD:]], axis=1)
    return jnp.concatenate([top, low], axis=0)


ORDER = (
    ("zs", 0), ("zs", 1), ("ts", 0), ("pp", 0), ("zf", 0), ("zs", 2), ("zf", 1), ("zs", 3),
    ("pr", 0), ("hf", 0), ("zf", 2), ("pr", 1), ("zf", 3), ("ws", 0), ("pf", 0), ("pr", 2),
    ("pf", 1), ("pr", 3), ("hl", 0), ("pf", 2), ("wf", 0), ("pf", 3), ("ls", 0), ("ro", 0),
    ("pe", 0), ("n", 1), ("n", 2), ("n", 3), ("n", 4), ("n", 5), ("pe", 1), ("n", 6), ("hw", 0),
    ("n", 7), ("n", 0), ("ko", 0), ("pe", 2), ("lf", 0), ("pe", 3), ("le", 0),
)


def gather_kernel(
    ent_hbm, gain, wqkv_hbm, owner, local_at, live, up_hbm, down_hbm,
    xbuf, ybuf, near_o, near_st, ent_rows, key_a, key_b, wz, wline,
    ent, wqkv, zbuf, xown, yown, halo_low, halo_high, tab, tab_y, tab_x, up_cols, up_rows, piece,
    zs, zr, xs, xr, ys, yr, cs, cr, hs, hr, ls, ts, tr, ws, wr, wl,
):
    y, x, core, z = coords()
    loc = lax.axis_index("loc")
    z_up, z_dn = shifted("z", 1), shifted("z", -1)
    x_up, x_dn = shifted("x", 1), shifted("x", -1)
    y_up, y_dn = shifted("y", 1), shifted("y", -1)
    sib = shifted("c", 0)
    nxt, prv = loc_shifted(1), loc_shifted(-1)
    w_place = x * (1 - core) + y * core
    w_up_to = device(y + core, x + 1 - core, core, z)
    w_dn_to = device(y + 3 * core, x + 3 * (1 - core), core, z)
    y_opp, x_opp = shifted("y", 2), shifted("x", 2)
    peers = [z_up, z_dn, x_up, x_dn, y_up, y_dn, sib, nxt, prv, y_opp, x_opp]
    greet(peers)
    load_up = pltpu.make_async_copy(
        up_hbm.at[:, pl.ds(pl.multiple_of(loc // 4 * BLK, BLK), BLK)], up_cols, wl.at[0]
    )
    load_down = pltpu.make_async_copy(
        down_hbm.at[pl.ds(pl.multiple_of(loc * UNITS, UNITS), UNITS)],
        piece.at[pl.ds(UNITS, UNITS)],
        wl.at[1],
    )
    load_ent = pltpu.make_async_copy(ent_hbm, ent, wl.at[4])
    load_qkv = pltpu.make_async_copy(wqkv_hbm, wqkv, wl.at[5])
    load_ent.start()
    load_up.start()
    load_down.start()
    load_qkv.start()
    tab[...] = jnp.zeros((NB, BLK), jnp.int32)
    tab[:, 0:4] = (owner[...] * NB + local_at[...]) * 2 + live[...]
    tab_y[y] = tab[...]
    tab_x[x] = tab[...]
    load_ent.wait()
    greeted(peers)
    rows = ROWS // CHUNKS
    blocks = NB // CHUNKS
    pending = []

    def go(copy):
        copy.start()
        pending.append(copy)
        return copy

    z_near = []

    def z_start(r):
        at = pl.ds(r * rows, rows)
        z_near.append(
            (
                go(remote(ent.at[at], zbuf.at[z, at], zs.at[r, 0], zr.at[r, 0], z_up)),
                go(remote(ent.at[at], zbuf.at[z, at], zs.at[r, 1], zr.at[r, 1], z_dn)),
            )
        )

    tab_copies = []

    def tab_start(_):
        for k, (dst, place, to) in enumerate(
            ((tab_y, y, (y_up, y_dn, y_opp)), (tab_x, x, (x_up, x_dn, x_opp)))
        ):
            for n, peer in enumerate(to):
                tab_copies.append(go(remote(tab, dst.at[place], ts.at[k, n], tr.at[k, n], peer)))

    lines = {}
    place_copies = []

    def weights_start(_):
        load_up.wait()
        load_down.wait()
        up_rows[...] = up_cols[...].astype(F32).T
        piece[0:UNITS] = up_rows[pl.ds(pl.multiple_of(loc % 4 * UNITS, UNITS), UNITS)].astype(BF16)
        lines["z"] = (
            go(remote(piece, wz.at[z], ws.at[0], wr.at[0], z_up)),
            go(remote(piece, wz.at[z], ws.at[1], wr.at[1], z_dn)),
        )
        local = pltpu.make_async_copy(piece, wz.at[z], wl.at[2])
        local.start()
        place_copies.append(local)

    def line_pass(name, buf, place, sem, up, dn, half):
        a, b = lines[name]
        a.wait_recv()
        view = buf.at[(place + 3) % 4, pl.ds(0, half)]
        c = go(remote(view, view, ws.at[sem], wr.at[sem], up))
        b.wait_recv()
        view = buf.at[(place + 1) % 4, pl.ds(half, half)]
        d = go(remote(view, view, ws.at[sem + 1], wr.at[sem + 1], dn))
        lines[name] = (c, d)

    def weights_forward(_):
        line_pass("z", wz, z, 2, z_up, z_dn, UNITS)

    def line_start(_):
        for copy in lines["z"]:
            copy.wait_recv()
        place_copies.pop().wait()
        lines["line"] = (
            go(remote(wz, wline.at[w_place], ws.at[4], wr.at[4], w_up_to)),
            go(remote(wz, wline.at[w_place], ws.at[5], wr.at[5], w_dn_to)),
        )
        local = pltpu.make_async_copy(wz, wline.at[w_place], wl.at[3])
        local.start()
        place_copies.append(local)

    def line_forward(_):
        line_pass("line", wline, w_place, 6, w_up_to, w_dn_to, SIDE // 2)

    def line_finish(_):
        for copy in lines["line"]:
            copy.wait_recv()
        place_copies.pop().wait()

    def prepare(_):
        zbuf[z] = ent[...]
        load_qkv.wait()

    z_far = []

    def z_forward(r):
        a, b = z_near[r]
        low = pl.ds(r * rows, rows // 2)
        high = pl.ds(r * rows + rows // 2, rows // 2)
        a.wait_recv()
        s = (z + 3) % 4
        c = go(remote(zbuf.at[s, low], zbuf.at[s, low], zs.at[r, 2], zr.at[r, 2], z_up))
        b.wait_recv()
        s = (z + 1) % 4
        d = go(remote(zbuf.at[s, high], zbuf.at[s, high], zs.at[r, 3], zr.at[r, 3], z_dn))
        z_far.append((c, d))

    plane = {}
    core_copies = []
    local_copies = []

    def to_sibling(buf, place, blks, sem, src=None):
        view = buf.at[core, place, blks, pl.ds(0, 2)]
        core_copies.append(go(remote(view if src is None else src, view, cs.at[sem], cr.at[sem], sib)))

    def project(r):
        for copy in z_far[r]:
            copy.wait_recv()
        at = pl.ds(r * rows, rows)
        full = jnp.concatenate([zbuf[s, at, :] for s in range(SIDE)], axis=1).astype(F32)
        normed = norm_rows(full, gain[...]).astype(BF16)
        queries = jnp.dot(normed, wqkv[0], preferred_element_type=F32)
        keys = jnp.dot(normed, wqkv[1], preferred_element_type=F32).astype(BF16)
        values = jnp.dot(normed, wqkv[2], preferred_element_type=F32)
        q_t = (queries.T.astype(BF16).astype(F32) * 0.125).astype(BF16)
        v_t = values.T.astype(BF16)
        for i in range(blocks):
            b = r * blocks + i
            cut = slice(i * BLK, (i + 1) * BLK)
            xown[b, 0] = keys[cut, :BLK]
            yown[b, 0] = keys[cut, BLK:]
            xown[b, 1] = v_t[:BLK, cut]
            yown[b, 1] = v_t[BLK:, cut]
            yown[b, 2] = q_t[:BLK, cut]
            xown[b, 2] = q_t[BLK:, cut]
        blks = pl.ds(r * blocks, blocks)
        for name, own, buf, place, send, recv, up, dn, k in (
            ("x", xown, xbuf, x, xs, xr, x_up, x_dn, 0),
            ("y", yown, ybuf, y, ys, yr, y_up, y_dn, 1),
        ):
            src, dst = own.at[blks], buf.at[core, place, blks]
            plane[name, r] = (
                go(remote(src, dst, send.at[r, 0], recv.at[r, 0], up)),
                go(remote(src, dst, send.at[r, 1], recv.at[r, 1], dn)),
            )
            local = pltpu.make_async_copy(src, dst, ls.at[r * 2 + k])
            local.start()
            local_copies.append(local)
            to_sibling(buf, place, blks, r * 10 + k * 5, own.at[blks, pl.ds(0, 2)])

    def plane_forward(r):
        blks = pl.ds(r * blocks, blocks)
        low = pl.ds(r * blocks, blocks // 2)
        high = pl.ds(r * blocks + blocks // 2, blocks // 2)
        for name, buf, place, send, recv, up, dn, k in (
            ("x", xbuf, x, xs, xr, x_up, x_dn, 0),
            ("y", ybuf, y, ys, yr, y_up, y_dn, 1),
        ):
            a, b = plane[name, r]
            a.wait_recv()
            s = (place + 3) % 4
            view = buf.at[core, s, low]
            c = go(remote(view, view, send.at[r, 2], recv.at[r, 2], up))
            to_sibling(buf, s, blks, r * 10 + k * 5 + 1)
            b.wait_recv()
            s = (place + 1) % 4
            view = buf.at[core, s, high]
            d = go(remote(view, view, send.at[r, 3], recv.at[r, 3], dn))
            to_sibling(buf, s, blks, r * 10 + k * 5 + 2)
            plane[name, r] = (c, d)

    def plane_finish(r):
        low = pl.ds(r * blocks, blocks // 2)
        high = pl.ds(r * blocks + blocks // 2, blocks // 2)
        for name, buf, place, k in (("x", xbuf, x, 0), ("y", ybuf, y, 1)):
            c, d = plane[name, r]
            s = (place + 2) % 4
            c.wait_recv()
            to_sibling(buf, s, low, r * 10 + k * 5 + 3)
            d.wait_recv()
            to_sibling(buf, s, high, r * 10 + k * 5 + 4)

    def near(b):
        for p, (own, other) in enumerate(((xown, yown), (yown, xown))):
            query = split_heads(other[b, 2])
            parts = []
            for step in (-1, 0, 1):
                if b + step < 0:
                    key, val, ok = halo_low[p, 0], halo_low[p, 1], loc > 0
                elif b + step >= NB:
                    key, val, ok = halo_high[p, 0], halo_high[p, 1], loc < 31
                else:
                    key, val, ok = own[b + step, 0], own[b + step, 1], None
                score = jnp.dot(key, query, preferred_element_type=F32)
                if ok is not None:
                    score = jnp.where(ok, score, NEG)
                parts.append((score, val))
            top = functools.reduce(
                jnp.maximum, [jnp.max(score, axis=0, keepdims=True) for score, _ in parts]
            )
            total = jnp.zeros((1, 2 * BLK), F32)
            out = jnp.zeros((BLK, 2 * BLK), F32)
            for score, val in parts:
                weight = jnp.exp(score - top)
                total = total + jnp.sum(weight, axis=0, keepdims=True)
                out = out + jnp.dot(val, weight.astype(BF16), preferred_element_type=F32)
            near_o[b, p] = jnp.concatenate(
                [out[:HD, :BLK] / total[:, :BLK], out[HD:, BLK:] / total[:, BLK:]], axis=0
            )
            near_st[b, p, 0:1] = top[:, :BLK]
            near_st[b, p, 1:2] = top[:, BLK:]
            near_st[b, p, 2:3] = total[:, :BLK]
            near_st[b, p, 3:4] = total[:, BLK:]
            near_st[b, p, 4:8] = jnp.zeros((4, BLK), F32)

    halos = []

    def halo_first(_):
        for p, own in enumerate((xown, yown)):
            halos.append(go(remote(own.at[0, pl.ds(0, 2)], halo_high.at[p], hs.at[p], hr.at[p], prv)))

    def halo_last(_):
        for p, own in enumerate((xown, yown)):
            src = own.at[NB - 1, pl.ds(0, 2)]
            halos.append(go(remote(src, halo_low.at[p], hs.at[2 + p], hr.at[2 + p], nxt)))

    def halo_wait(_):
        for copy in halos:
            copy.wait_recv()

    def rows_out(_):
        mine = pl.ds(pl.multiple_of(z * GROUP, GROUP), GROUP)
        ent_rows[...] = jnp.concatenate([zbuf[s, mine, :] for s in range(SIDE)], axis=1)

    def keys_out(_):
        for copy in tab_copies:
            copy.wait_recv()
        code = tab_y[...]
        at_key = code // 16 % 2 * 32 + code // 32 % 4 * NB + code // 2 % NB
        key_a[...] = jnp.where((code % 2 == 1) & (code // 128 == y), at_key, -1)
        code = tab_x[...]
        at_key = code // 16 % 2 * 32 + code // 128 * NB + code // 2 % NB
        key_b[...] = jnp.where((code % 2 == 1) & (code // 32 % 4 == x), at_key, -1)

    steps = {
        "zs": z_start, "zf": z_forward, "pr": project, "pf": plane_forward, "pe": plane_finish,
        "n": near, "ts": tab_start, "ws": weights_start, "wf": weights_forward, "ls": line_start,
        "lf": line_forward, "le": line_finish, "hf": halo_first, "hl": halo_last, "hw": halo_wait,
        "ro": rows_out, "ko": keys_out, "pp": prepare,
    }
    for name, place in ORDER:
        steps[name](place)
    for copy in core_copies:
        copy.wait_recv()
    for copy in local_copies:
        copy.wait()
    for copy in pending:
        copy.wait_send()


def gather_call(ent, gain, wqkv, owner, local_at, live, w_up, w_down):
    vmem = pl.BlockSpec(memory_space=pltpu.VMEM)
    hbm = pl.BlockSpec(memory_space=pl.ANY)
    pinned = pl.BlockSpec(memory_space=pltpu.HBM)
    dma = pltpu.SemaphoreType.DMA
    plane_shape = (2, SIDE, NB, 3, BLK, BLK)
    return pl.pallas_call(
        gather_kernel,
        out_shape=(
            jax.ShapeDtypeStruct(plane_shape, BF16),
            jax.ShapeDtypeStruct(plane_shape, BF16),
            jax.ShapeDtypeStruct((NB, 2, BLK, BLK), F32),
            jax.ShapeDtypeStruct((NB, 2, 8, BLK), F32),
            jax.ShapeDtypeStruct((GROUP, WIDTH), BF16),
            jax.ShapeDtypeStruct((SIDE, NB, BLK), jnp.int32),
            jax.ShapeDtypeStruct((SIDE, NB, BLK), jnp.int32),
            jax.ShapeDtypeStruct((SIDE, 2 * UNITS, WIDTH), BF16),
            jax.ShapeDtypeStruct((SIDE, SIDE, 2 * UNITS, WIDTH), BF16),
        ),
        in_specs=[pinned, vmem, pinned] + [vmem] * 3 + [pinned] * 2,
        out_specs=(hbm, hbm) + (vmem,) * 5 + (hbm, hbm),
        scratch_shapes=[
            pltpu.VMEM((ROWS, PART), BF16),
            pltpu.VMEM((3, WIDTH, PART), BF16),
            pltpu.VMEM((SIDE, ROWS, PART), BF16),
            pltpu.VMEM((NB, 3, BLK, BLK), BF16),
            pltpu.VMEM((NB, 3, BLK, BLK), BF16),
            pltpu.VMEM((2, 2, BLK, BLK), BF16),
            pltpu.VMEM((2, 2, BLK, BLK), BF16),
            pltpu.VMEM((NB, BLK), jnp.int32),
            pltpu.VMEM((SIDE, NB, BLK), jnp.int32),
            pltpu.VMEM((SIDE, NB, BLK), jnp.int32),
            pltpu.VMEM((WIDTH, BLK), BF16),
            pltpu.VMEM((BLK, WIDTH), F32),
            pltpu.VMEM((2 * UNITS, WIDTH), BF16),
            dma((CHUNKS, 4)), dma((CHUNKS, 4)),
            dma((CHUNKS, 4)), dma((CHUNKS, 4)),
            dma((CHUNKS, 4)), dma((CHUNKS, 4)),
            dma((CHUNKS * 10,)), dma((CHUNKS * 10,)),
            dma((4,)), dma((4,)),
            dma((CHUNKS * 2,)),
            dma((2, 3)), dma((2, 3)),
            dma((8,)), dma((8,)),
            dma((6,)),
        ],
        compiler_params=pltpu.CompilerParams(
            collective_id=0, has_side_effects=True, vmem_limit_bytes=60 * MB
        ),
        name="gather_project",
    )(ent, gain, wqkv, owner, local_at, live, w_up, w_down)


def far_kernel(key_a, key_b, x_hbm, y_hbm, oa, sa, ob, sb, xbuf, ybuf, acc, state, hits_a, hits_b, sems):
    core = lax.axis_index("loc") % 2
    live_q = SIDE * NB
    loads = [
        pltpu.make_async_copy(x_hbm, xbuf, sems.at[0]),
        pltpu.make_async_copy(y_hbm, ybuf, sems.at[1]),
    ]
    for load in loads:
        load.start()

    def find(i, counts):
        count_a, count_b = counts
        s, b = i // NB, i % NB
        for j in range(4):
            key = key_a[s, b, j]
            hits_a[count_a] = i * 1024 + key
            count_a = count_a + jnp.where(key >= 0, 1, 0)
            key = key_b[s, b, j]
            hits_b[count_b] = i * 1024 + key
            count_b = count_b + jnp.where(key >= 0, 1, 0)
        return count_a, count_b

    counts = lax.fori_loop(0, live_q, find, (0, 0))
    for hits, count in zip((hits_a, hits_b), counts):
        for extra in range(4):
            hits[count + extra] = live_q * 1024

    def clear(i, carry):
        acc[i] = jnp.zeros((BLK, BLK), F32)
        state[i, 0:2] = jnp.full((2, BLK), NEG, F32)
        state[i, 2:8] = jnp.zeros((6, BLK), F32)
        return carry

    lax.fori_loop(0, 2 * (live_q + 1), clear, 0)
    for load in loads:
        load.wait()

    for pair in range(2):
        hits, count = (hits_a, counts[0]) if pair == 0 else (hits_b, counts[1])
        keys_ref, query_ref = (xbuf, ybuf) if pair == 0 else (ybuf, xbuf)
        o_ref, s_ref = (oa, sa) if pair == 0 else (ob, sb)
        base = pair * (live_q + 1)

        def four(step, carry):
            work = []
            for u in range(4):
                code = hits[step * 4 + u]
                q, k = code // 1024, code % 1024
                q_at = jnp.minimum(q, live_q - 1)
                query = split_heads(query_ref[core, q_at // NB, q_at % NB, 2])
                kc, kp, kb = k // 32, (k // 8) % 4, k % 8
                key = keys_ref[kc, kp, kb, 0]
                val = keys_ref[kc, kp, kb, 1]
                score = jnp.dot(key, query, preferred_element_type=F32)
                top = jnp.max(score, axis=0, keepdims=True)
                weight = jnp.exp(score - top)
                total = jnp.sum(weight, axis=0, keepdims=True)
                out = jnp.dot(val, weight.astype(BF16), preferred_element_type=F32)
                work.append((q + base, top, total, out))
            for q, top, total, out in work:
                for h in range(2):
                    cut = slice(h * BLK, (h + 1) * BLK)
                    feat = pl.ds(h * HD, HD)
                    old_top = state[q, h : h + 1]
                    new_top = jnp.maximum(old_top, top[:, cut])
                    keep = jnp.exp(old_top - new_top)
                    add = jnp.exp(top[:, cut] - new_top)
                    acc[q, feat] = acc[q, feat] * keep + out[h * HD : (h + 1) * HD, cut] * add
                    state[q, h : h + 1] = new_top
                    state[q, 2 + h : 3 + h] = state[q, 2 + h : 3 + h] * keep + total[:, cut] * add
            return carry

        lax.fori_loop(0, (count + 3) // 4, four, 0)

        def finish(i, carry):
            s, b = i // NB, i % NB
            st = state[base + i]
            s_ref[s, b] = st
            for h in range(2):
                total = st[2 + h : 3 + h]
                scale = 1.0 / jnp.where(total > 0, total, 1.0)
                feat = pl.ds(h * HD, HD)
                o_ref[s, b, feat] = (acc[base + i, feat] * scale).astype(BF16)
            return carry

        lax.fori_loop(0, live_q, finish, 0)


def far_call(key_a, key_b, xbuf, ybuf):
    vmem = pl.BlockSpec(memory_space=pltpu.VMEM)
    smem = pl.BlockSpec(memory_space=pltpu.SMEM)
    hbm = pl.BlockSpec(memory_space=pltpu.HBM)
    o_shape = jax.ShapeDtypeStruct((SIDE, NB, BLK, BLK), BF16)
    s_shape = jax.ShapeDtypeStruct((SIDE, NB, 8, BLK), F32)
    return pl.pallas_call(
        far_kernel,
        out_shape=(o_shape, s_shape, o_shape, s_shape),
        in_specs=[smem, smem, hbm, hbm],
        out_specs=(vmem,) * 4,
        scratch_shapes=[
            pltpu.VMEM(xbuf.shape, BF16),
            pltpu.VMEM(ybuf.shape, BF16),
            pltpu.VMEM((2 * (SIDE * NB + 1), BLK, BLK), F32),
            pltpu.VMEM((2 * (SIDE * NB + 1), 8, BLK), F32),
            pltpu.SMEM((SIDE * NB * 4 + 8,), jnp.int32),
            pltpu.SMEM((SIDE * NB * 4 + 8,), jnp.int32),
            pltpu.SemaphoreType.DMA((2,)),
        ],
        compiler_params=pltpu.CompilerParams(vmem_limit_bytes=58 * MB),
        name="far_partials",
    )(key_a, key_b, xbuf, ybuf)


def merge_kernel(
    oa, sa, ob, sb, near_o, near_st, ent_rows, w_out, gain, wline, result,
    ra, rsa, rb, rsb, relay, relay_st, att, part, got_half, got,
    weights, inner, acc, send_sib, got_sib, res, landed,
    os, orr, fs, fr, zs, zr, ws, wr, wl, ss, sr, es, er,
):
    y, x, core, z = coords()
    z_up, z_dn = shifted("z", 1), shifted("z", -1)
    z_opp, sib = shifted("z", 2), shifted("c", 0)
    peers = [shifted("y", 1), shifted("y", -1), shifted("x", 1), shifted("x", -1), z_up, z_dn]
    w_place = y * (1 - core) + x * core
    w_up_to = device(y + 1 - core, x + core, core, z)
    w_dn_to = device(y + 3 * (1 - core), x + 3 * core, core, z)
    peers = peers + [z_opp, sib]
    greet(peers)
    greeted(peers)
    w_local = pltpu.make_async_copy(wline, weights.at[w_place], wl)
    w_local.start()
    pending = []

    def go(copy):
        copy.start()
        pending.append(copy)
        return copy

    half = NB // 2
    lanes = []
    for k, (place, up, dn, o, st, ro, rst) in enumerate(
        (
            (y, peers[0], peers[1], oa, sa, ra, rsa),
            (x, peers[2], peers[3], ob, sb, rb, rsb),
        )
    ):
        far_to, up_to, dn_to = (place + 2) % 4, (place + 1) % 4, (place + 3) % 4
        low, high = pl.ds(0, half), pl.ds(half, half)
        first = []
        for t, (src, hop, dst) in enumerate(((o, relay, ro), (st, relay_st, rst))):
            first.append(
                (
                    go(remote(src.at[far_to, low], hop.at[k, 0], os.at[k, t, 0], orr.at[k, t, 0], up)),
                    go(remote(src.at[far_to, high], hop.at[k, 1], os.at[k, t, 1], orr.at[k, t, 1], dn)),
                )
            )
        direct = []
        for t, (src, dst) in enumerate(((o, ro), (st, rst))):
            direct.append(
                (
                    go(remote(src.at[up_to], dst.at[place], os.at[k, t, 2], orr.at[k, t, 2], up)),
                    go(remote(src.at[dn_to], dst.at[place], os.at[k, t, 3], orr.at[k, t, 3], dn)),
                )
            )
        lanes.append((place, up, dn, ro, rst, first, direct))
    arrivals = []
    for k, (place, up, dn, ro, rst, first, direct) in enumerate(lanes):
        low, high = pl.ds(0, half), pl.ds(half, half)
        for t, (hop, dst) in enumerate(((relay, ro), (relay_st, rst))):
            a, b = first[t]
            a.wait_recv()
            arrivals.append(
                go(remote(hop.at[k, 0], dst.at[(place + 3) % 4, low], fs.at[k, t, 0], fr.at[k, t, 0], up))
            )
            b.wait_recv()
            arrivals.append(
                go(remote(hop.at[k, 1], dst.at[(place + 1) % 4, high], fs.at[k, t, 1], fr.at[k, t, 1], dn))
            )
        for pair in direct:
            arrivals.extend(pair)
    w_up_copies, w_dn_copies = [None] * 4, [None] * 4
    for n in range(SIDE):
        u, d = n, (n + 2) % 4
        dst = weights.at[w_place]
        w_up_copies[u] = go(remote(wline.at[u], dst.at[u], ws.at[0, u], wr.at[0, u], w_up_to))
        w_dn_copies[d] = go(remote(wline.at[d], dst.at[d], ws.at[1, d], wr.at[1, d], w_dn_to))
    w_far = []

    def weights_forward(n):
        w_up_copies[n].wait_recv()
        view = weights.at[(w_place + 3) % 4, n]
        w_far.append(go(remote(view, view, ws.at[2, n], wr.at[2, n], w_up_to)))
        w_dn_copies[n + 2].wait_recv()
        view = weights.at[(w_place + 1) % 4, n + 2]
        w_far.append(go(remote(view, view, ws.at[2, n + 2], wr.at[2, n + 2], w_dn_to)))

    ra[y] = oa[y]
    rsa[y] = sa[y]
    rb[x] = ob[x]
    rsb[x] = sb[x]
    for copy in arrivals:
        copy.wait_recv()

    def merge(b, carry):
        for p, (ro, rst) in enumerate(((ra, rsa), (rb, rsb))):
            stats = [near_st[b, p]] + [rst[s, b] for s in range(SIDE)]
            outs = [near_o[b, p]] + [ro[s, b].astype(F32) for s in range(SIDE)]
            halves = []
            for h in range(2):
                top = functools.reduce(jnp.maximum, [st[h : h + 1] for st in stats])
                scale = [st[2 + h : 3 + h] * jnp.exp(st[h : h + 1] - top) for st in stats]
                inv = 1.0 / functools.reduce(jnp.add, scale)
                halves.append(
                    functools.reduce(
                        jnp.add,
                        [o[h * HD : (h + 1) * HD] * (w * inv) for o, w in zip(outs, scale)],
                    )
                )
            tile = jnp.concatenate(halves, axis=0).T.astype(BF16)
            att[pl.ds(pl.multiple_of(b * BLK, BLK), BLK), p * BLK : (p + 1) * BLK] = tile
        return carry

    lax.fori_loop(0, NB, merge, 0)

    def project(group):
        rows = att[pl.ds(pl.multiple_of(group * GROUP, GROUP), GROUP), :]
        return jnp.dot(rows, w_out[...], preferred_element_type=F32)

    h = GROUP // 2
    part[0] = project((z + 2) % 4).astype(BF16)
    f_up = go(remote(part.at[0, pl.ds(0, h)], got_half.at[0], zs.at[0], zr.at[0], z_up))
    f_dn = go(remote(part.at[0, pl.ds(h, h)], got_half.at[1], zs.at[1], zr.at[1], z_dn))
    to_up = project((z + 1) % 4)
    part[1, h:] = to_up[h:].astype(BF16)
    to_dn = project((z + 3) % 4)
    part[2, :h] = to_dn[:h].astype(BF16)
    f_up.wait_recv()
    part[1, :h] = (to_up[:h] + got_half[0].astype(F32)).astype(BF16)
    s_up = go(remote(part.at[1], got.at[0], zs.at[2], zr.at[2], z_up))
    f_dn.wait_recv()
    part[2, h:] = (to_dn[h:] + got_half[1].astype(F32)).astype(BF16)
    s_dn = go(remote(part.at[2], got.at[1], zs.at[3], zr.at[3], z_dn))
    mine = project(z) + ent_rows[...].astype(F32)
    weights_forward(0)
    s_up.wait_recv()
    s_dn.wait_recv()
    mixed = mine + got[0].astype(F32) + got[1].astype(F32)
    inner[core] = norm_rows(mixed, gain[...]).astype(BF16)
    to_sib = go(remote(inner.at[core], inner.at[core], ss.at[0], sr.at[0], sib))
    acc[core] = mixed
    acc[1 - core] = jnp.zeros((GROUP, WIDTH), F32)
    weights_forward(1)
    w_local.wait()

    def mlp(slot, who):
        w_up = weights[slot, :, :, 0:UNITS].reshape(SIDE * SIDE * UNITS, WIDTH)
        w_down = weights[slot, :, :, UNITS:].reshape(SIDE * SIDE * UNITS, WIDTH)
        hidden = lax.dot_general(
            inner[who], w_up, (((1,), (1,)), ((), ())), preferred_element_type=F32
        )
        acc[who] += jnp.dot(gelu(hidden).astype(BF16), w_down, preferred_element_type=F32)

    def mlp_both(slot):
        def body(t, carry):
            mlp(slot, (core + 1 + t) % 2)
            return carry

        lax.fori_loop(0, 2, body, 0)

    to_sib.wait_recv()
    mlp_both(w_place)
    w_up_copies[2].wait_recv()
    w_up_copies[3].wait_recv()
    mlp_both((w_place + 3) % 4)
    w_dn_copies[0].wait_recv()
    w_dn_copies[1].wait_recv()
    mlp_both((w_place + 1) % 4)
    for copy in w_far:
        copy.wait_recv()
    mlp((w_place + 2) % 4, 1 - core)
    send_sib[...] = acc[1 - core].astype(BF16)
    back = go(remote(send_sib, got_sib, ss.at[1], sr.at[1], sib))
    mlp((w_place + 2) % 4, core)
    back.wait_recv()
    final = (acc[core] + got_sib[...].astype(F32)).astype(BF16)
    for s in range(SIDE):
        res[s] = final[:, s * PART : (s + 1) * PART]
    copies = []
    for n, to in ((2, z_opp), (1, z_up), (3, z_dn)):
        copies.append(go(remote(res.at[(z + n) % 4], landed.at[z], es.at[n], er.at[n], to)))
    result[pl.ds(pl.multiple_of(z * GROUP, GROUP), GROUP), :] = res[z]
    for copy in copies:
        copy.wait_recv()
    for n in range(1, SIDE):
        s = (z + n) % 4
        result[pl.ds(pl.multiple_of(s * GROUP, GROUP), GROUP), :] = landed[s]
    for copy in pending:
        copy.wait_send()


def gelu(v):
    return 0.5 * v * (1.0 + lax.erf(v * 0.7071067811865476))


def merge_call(oa, sa, ob, sb, near_o, near_st, ent_rows, w_out, gain, wline):
    vmem = pl.BlockSpec(memory_space=pltpu.VMEM)
    dma = pltpu.SemaphoreType.DMA
    return pl.pallas_call(
        merge_kernel,
        out_shape=jax.ShapeDtypeStruct((ROWS, PART), BF16),
        in_specs=[vmem] * 9 + [pl.BlockSpec(memory_space=pl.ANY)],
        out_specs=vmem,
        scratch_shapes=[
            pltpu.VMEM((SIDE, NB, BLK, BLK), BF16),
            pltpu.VMEM((SIDE, NB, 8, BLK), F32),
            pltpu.VMEM((SIDE, NB, BLK, BLK), BF16),
            pltpu.VMEM((SIDE, NB, 8, BLK), F32),
            pltpu.VMEM((2, 2, NB // 2, BLK, BLK), BF16),
            pltpu.VMEM((2, 2, NB // 2, 8, BLK), F32),
            pltpu.VMEM((ROWS, 2 * BLK), BF16),
            pltpu.VMEM((3, GROUP, WIDTH), BF16),
            pltpu.VMEM((2, GROUP // 2, WIDTH), BF16),
            pltpu.VMEM((2, GROUP, WIDTH), BF16),
            pltpu.VMEM((SIDE, SIDE, SIDE, 2 * UNITS, WIDTH), BF16),
            pltpu.VMEM((2, GROUP, WIDTH), BF16),
            pltpu.VMEM((2, GROUP, WIDTH), F32),
            pltpu.VMEM((GROUP, WIDTH), BF16),
            pltpu.VMEM((GROUP, WIDTH), BF16),
            pltpu.VMEM((SIDE, GROUP, PART), BF16),
            pltpu.VMEM((SIDE, GROUP, PART), BF16),
            dma((2, 2, 4)), dma((2, 2, 4)),
            dma((2, 2, 2)), dma((2, 2, 2)),
            dma((4,)), dma((4,)),
            dma((3, 4)), dma((3, 4)), dma,
            dma((2,)), dma((2,)),
            dma((4,)), dma((4,)),
        ],
        compiler_params=pltpu.CompilerParams(
            collective_id=1, has_side_effects=True, vmem_limit_bytes=40 * MB
        ),
        name="merge_project",
    )(oa, sa, ob, sb, near_o, near_st, ent_rows, w_out, gain, wline)


def on_device(
    entities, attn_gain, w_qkv, w_out, mlp_gain, w_up, w_down, far_owner, far_local, far_live
):
    xbuf, ybuf, near_o, near_st, ent_rows, key_a, key_b, _, wline = gather_call(
        entities,
        attn_gain.reshape(1, WIDTH),
        w_qkv,
        far_owner,
        far_local,
        far_live,
        w_up,
        w_down,
    )
    oa, sa, ob, sb = far_call(key_a, key_b, xbuf, ybuf)
    return merge_call(
        oa, sa, ob, sb, near_o, near_st, ent_rows, w_out, mlp_gain.reshape(1, WIDTH), wline
    )


def solution(mesh):
    return jax.shard_map(
        on_device,
        mesh=mesh,
        in_specs=(
            P("loc", "head"),
            P(),
            P(None, None, "head"),
            P("head", None),
            P(),
            P(None, "head"),
            P("head", None),
            P("loc", None),
            P("loc", None),
            P("loc", None),
        ),
        out_specs=P("loc", "head"),
        check_vma=False,
    )
```

```python
import functools

import jax
import jax.numpy as jnp
from jax import lax
from jax.experimental import pallas as pl
from jax.experimental.pallas import tpu as pltpu
from jax.sharding import PartitionSpec as P

MESH = pl.DeviceIdType.MESH
F32 = jnp.float32
BF16 = jnp.bfloat16
BLK = 128
HD = 64
NB = 8
SIDE = 4
CHUNKS = 4
ROWS = NB * BLK
GROUP = ROWS // SIDE
WIDTH = 1024
PART = WIDTH // SIDE
NEG = -1e30
MB = 2**20
TALL = BLK + 16
UNITS = 32


def coords():
    loc = lax.axis_index("loc")
    return loc // 8, (loc // 2) % 4, loc % 2, lax.axis_index("head")


def device(y, x, core, z):
    return ((y % 4 * 4 + x % 4) * 2 + core, z % 4)


def shifted(axis, by):
    y, x, core, z = coords()
    if axis == "y":
        return device(y + by + 4, x, core, z)
    if axis == "x":
        return device(y, x + by + 4, core, z)
    if axis == "z":
        return device(y, x, core, z + by + 4)
    return device(y, x, 1 - core, z)


def loc_shifted(by):
    return ((lax.axis_index("loc") + by + 32) % 32, lax.axis_index("head"))


def greet(peers):
    barrier = pltpu.get_barrier_semaphore()
    for peer in peers:
        pl.semaphore_signal(barrier, inc=1, device_id=peer, device_id_type=MESH)


def greeted(peers):
    pl.semaphore_wait(pltpu.get_barrier_semaphore(), len(peers))


def remote(src, dst, send, recv, to):
    return pltpu.make_async_remote_copy(
        src_ref=src, dst_ref=dst, send_sem=send, recv_sem=recv, device_id=to, device_id_type=MESH
    )


def norm_rows(values, gain):
    center = values - jnp.mean(values, axis=-1, keepdims=True)
    spread = jnp.mean(center * center, axis=-1, keepdims=True)
    return center * lax.rsqrt(spread + 1e-05) * gain


def split_heads(query):
    zero = jnp.zeros((HD, BLK), query.dtype)
    top = jnp.concatenate([query[:HD], zero], axis=1)
    low = jnp.concatenate([zero, query[HD:]], axis=1)
    return jnp.concatenate([top, low], axis=0)


ORDER = (
    ("zs", 0), ("zs", 1), ("ts", 0), ("pp", 0), ("zf", 0), ("zs", 2), ("zf", 1), ("zs", 3),
    ("pr", 0), ("hf", 0), ("zf", 2), ("pr", 1), ("zf", 3), ("ws", 0), ("pf", 0), ("pr", 2),
    ("pf", 1), ("pr", 3), ("hl", 0), ("pf", 2), ("wf", 0), ("pf", 3), ("ro", 0),
    ("pe", 0), ("n", 1), ("n", 2), ("n", 3), ("n", 4), ("n", 5), ("pe", 1), ("n", 6), ("hw", 0),
    ("n", 7), ("n", 0), ("ko", 0), ("pe", 2), ("pe", 3), ("we", 0),
)


def gather_kernel(
    ent_hbm, gain, wqkv_hbm, tab, up_hbm, down_hbm,
    xbuf, ybuf, near_o, near_st, ent_rows, key_a, key_b, wz,
    ent, wqkv, zbuf, xown, yown, halo_low, halo_high, tab_y, tab_x, up_cols, up_rows, piece,
    zs, zr, xs, xr, ys, yr, cs, cr, hs, hr, ls, ts, tr, ws, wr, wl,
):
    y, x, core, z = coords()
    loc = lax.axis_index("loc")
    z_up, z_dn = shifted("z", 1), shifted("z", -1)
    x_up, x_dn = shifted("x", 1), shifted("x", -1)
    y_up, y_dn = shifted("y", 1), shifted("y", -1)
    sib = shifted("c", 0)
    nxt, prv = loc_shifted(1), loc_shifted(-1)
    y_opp, x_opp = shifted("y", 2), shifted("x", 2)
    peers = [z_up, z_dn, x_up, x_dn, y_up, y_dn, sib, nxt, prv, y_opp, x_opp]
    greet(peers)
    load_up = pltpu.make_async_copy(
        up_hbm.at[:, pl.ds(pl.multiple_of(loc // 4 * BLK, BLK), BLK)], up_cols, wl.at[0]
    )
    load_down = pltpu.make_async_copy(
        down_hbm.at[pl.ds(pl.multiple_of(loc * UNITS, UNITS), UNITS)],
        piece.at[pl.ds(UNITS, UNITS)],
        wl.at[1],
    )
    load_ent = pltpu.make_async_copy(ent_hbm, ent, wl.at[4])
    load_qkv = pltpu.make_async_copy(wqkv_hbm, wqkv, wl.at[5])
    load_ent.start()
    load_up.start()
    load_down.start()
    load_qkv.start()
    tab_y[y] = tab[...]
    tab_x[x] = tab[...]
    load_ent.wait()
    greeted(peers)
    rows = ROWS // CHUNKS
    blocks = NB // CHUNKS
    pending = []

    def go(copy):
        copy.start()
        pending.append(copy)
        return copy

    z_near = []

    def z_start(r):
        at = pl.ds(r * rows, rows)
        z_near.append(
            (
                go(remote(ent.at[at], zbuf.at[z, at], zs.at[r, 0], zr.at[r, 0], z_up)),
                go(remote(ent.at[at], zbuf.at[z, at], zs.at[r, 1], zr.at[r, 1], z_dn)),
            )
        )

    tab_copies = []

    def tab_start(_):
        for k, (dst, place, to) in enumerate(
            ((tab_y, y, (y_up, y_dn, y_opp)), (tab_x, x, (x_up, x_dn, x_opp)))
        ):
            for n, peer in enumerate(to):
                tab_copies.append(go(remote(tab, dst.at[place], ts.at[k, n], tr.at[k, n], peer)))

    lines = {}
    place_copies = []

    def weights_start(_):
        load_up.wait()
        load_down.wait()
        up_rows[...] = up_cols[...].astype(F32).T
        piece[0:UNITS] = up_rows[pl.ds(pl.multiple_of(loc % 4 * UNITS, UNITS), UNITS)].astype(BF16)
        lines["z"] = (
            go(remote(piece, wz.at[z], ws.at[0], wr.at[0], z_up)),
            go(remote(piece, wz.at[z], ws.at[1], wr.at[1], z_dn)),
        )
        local = pltpu.make_async_copy(piece, wz.at[z], wl.at[2])
        local.start()
        place_copies.append(local)

    def line_pass(name, buf, place, sem, up, dn, half):
        a, b = lines[name]
        a.wait_recv()
        view = buf.at[(place + 3) % 4, pl.ds(0, half)]
        c = go(remote(view, view, ws.at[sem], wr.at[sem], up))
        b.wait_recv()
        view = buf.at[(place + 1) % 4, pl.ds(half, half)]
        d = go(remote(view, view, ws.at[sem + 1], wr.at[sem + 1], dn))
        lines[name] = (c, d)

    def weights_forward(_):
        line_pass("z", wz, z, 2, z_up, z_dn, UNITS)

    def weights_finish(_):
        for copy in lines["z"]:
            copy.wait_recv()
        place_copies.pop().wait()

    def prepare(_):
        zbuf[z] = ent[...]
        load_qkv.wait()

    z_far = []

    def z_forward(r):
        a, b = z_near[r]
        low = pl.ds(r * rows, rows // 2)
        high = pl.ds(r * rows + rows // 2, rows // 2)
        a.wait_recv()
        s = (z + 3) % 4
        c = go(remote(zbuf.at[s, low], zbuf.at[s, low], zs.at[r, 2], zr.at[r, 2], z_up))
        b.wait_recv()
        s = (z + 1) % 4
        d = go(remote(zbuf.at[s, high], zbuf.at[s, high], zs.at[r, 3], zr.at[r, 3], z_dn))
        z_far.append((c, d))

    plane = {}
    core_copies = []
    local_copies = []

    def to_sibling(buf, place, blks, sem, src=None):
        view = buf.at[core, place, blks, pl.ds(0, 2)]
        core_copies.append(go(remote(view if src is None else src, view, cs.at[sem], cr.at[sem], sib)))

    def project(r):
        for copy in z_far[r]:
            copy.wait_recv()
        at = pl.ds(r * rows, rows)
        full = jnp.concatenate([zbuf[s, at, :] for s in range(SIDE)], axis=1).astype(F32)
        normed = norm_rows(full, gain[...]).astype(BF16)
        queries = jnp.dot(normed, wqkv[0], preferred_element_type=F32)
        keys = jnp.dot(normed, wqkv[1], preferred_element_type=F32).astype(BF16)
        values = jnp.dot(normed, wqkv[2], preferred_element_type=F32)
        q_t = (queries.T.astype(BF16).astype(F32) * 0.125).astype(BF16)
        v_t = values.T.astype(BF16)
        for i in range(blocks):
            b = r * blocks + i
            cut = slice(i * BLK, (i + 1) * BLK)
            xown[b, 0] = keys[cut, :BLK]
            yown[b, 0] = keys[cut, BLK:]
            xown[b, 1] = v_t[:BLK, cut]
            yown[b, 1] = v_t[BLK:, cut]
            yown[b, 2] = q_t[:BLK, cut]
            xown[b, 2] = q_t[BLK:, cut]
        blks = pl.ds(r * blocks, blocks)
        for name, own, buf, place, send, recv, up, dn, k in (
            ("x", xown, xbuf, x, xs, xr, x_up, x_dn, 0),
            ("y", yown, ybuf, y, ys, yr, y_up, y_dn, 1),
        ):
            src, dst = own.at[blks], buf.at[core, place, blks]
            plane[name, r] = (
                go(remote(src, dst, send.at[r, 0], recv.at[r, 0], up)),
                go(remote(src, dst, send.at[r, 1], recv.at[r, 1], dn)),
            )
            local = pltpu.make_async_copy(src, dst, ls.at[r * 2 + k])
            local.start()
            local_copies.append(local)
            to_sibling(buf, place, blks, r * 10 + k * 5, own.at[blks, pl.ds(0, 2)])

    def plane_forward(r):
        blks = pl.ds(r * blocks, blocks)
        low = pl.ds(r * blocks, blocks // 2)
        high = pl.ds(r * blocks + blocks // 2, blocks // 2)
        for name, buf, place, send, recv, up, dn, k in (
            ("x", xbuf, x, xs, xr, x_up, x_dn, 0),
            ("y", ybuf, y, ys, yr, y_up, y_dn, 1),
        ):
            a, b = plane[name, r]
            a.wait_recv()
            s = (place + 3) % 4
            view = buf.at[core, s, low]
            c = go(remote(view, view, send.at[r, 2], recv.at[r, 2], up))
            to_sibling(buf, s, blks, r * 10 + k * 5 + 1)
            b.wait_recv()
            s = (place + 1) % 4
            view = buf.at[core, s, high]
            d = go(remote(view, view, send.at[r, 3], recv.at[r, 3], dn))
            to_sibling(buf, s, blks, r * 10 + k * 5 + 2)
            plane[name, r] = (c, d)

    def plane_finish(r):
        low = pl.ds(r * blocks, blocks // 2)
        high = pl.ds(r * blocks + blocks // 2, blocks // 2)
        for name, buf, place, k in (("x", xbuf, x, 0), ("y", ybuf, y, 1)):
            c, d = plane[name, r]
            s = (place + 2) % 4
            c.wait_recv()
            to_sibling(buf, s, low, r * 10 + k * 5 + 3)
            d.wait_recv()
            to_sibling(buf, s, high, r * 10 + k * 5 + 4)

    def near(b):
        for p, (own, other) in enumerate(((xown, yown), (yown, xown))):
            query = split_heads(other[b, 2])
            parts = []
            for step in (-1, 0, 1):
                if b + step < 0:
                    key, val, ok = halo_low[p, 0], halo_low[p, 1], loc > 0
                elif b + step >= NB:
                    key, val, ok = halo_high[p, 0], halo_high[p, 1], loc < 31
                else:
                    key, val, ok = own[b + step, 0], own[b + step, 1], None
                score = jnp.dot(key, query, preferred_element_type=F32)
                if ok is not None:
                    score = jnp.where(ok, score, NEG)
                parts.append((score, val))
            top = functools.reduce(
                jnp.maximum, [jnp.max(score, axis=0, keepdims=True) for score, _ in parts]
            )
            total = jnp.zeros((1, 2 * BLK), F32)
            out = jnp.zeros((BLK, 2 * BLK), F32)
            for score, val in parts:
                weight = jnp.exp(score - top)
                total = total + jnp.sum(weight, axis=0, keepdims=True)
                out = out + jnp.dot(val, weight.astype(BF16), preferred_element_type=F32)
            near_o[b, p] = jnp.concatenate(
                [out[:HD, :BLK] / total[:, :BLK], out[HD:, BLK:] / total[:, BLK:]], axis=0
            )
            near_st[b, p, 0:1] = top[:, :BLK]
            near_st[b, p, 1:2] = top[:, BLK:]
            near_st[b, p, 2:3] = total[:, :BLK]
            near_st[b, p, 3:4] = total[:, BLK:]
            near_st[b, p, 4:8] = jnp.zeros((4, BLK), F32)

    halos = []

    def halo_first(_):
        for p, own in enumerate((xown, yown)):
            halos.append(go(remote(own.at[0, pl.ds(0, 2)], halo_high.at[p], hs.at[p], hr.at[p], prv)))

    def halo_last(_):
        for p, own in enumerate((xown, yown)):
            src = own.at[NB - 1, pl.ds(0, 2)]
            halos.append(go(remote(src, halo_low.at[p], hs.at[2 + p], hr.at[2 + p], nxt)))

    def halo_wait(_):
        for copy in halos:
            copy.wait_recv()

    def rows_out(_):
        mine = pl.ds(pl.multiple_of(z * GROUP, GROUP), GROUP)
        ent_rows[...] = jnp.concatenate([zbuf[s, mine, :] for s in range(SIDE)], axis=1)

    def keys_out(_):
        for copy in tab_copies:
            copy.wait_recv()
        code = jnp.concatenate([tab_y[s][:, :NB] for s in range(SIDE)], axis=1)
        at_key = code // 16 % 2 * 32 + code // 32 % 4 * NB + code // 2 % NB
        key_a[...] = jnp.where((code % 2 == 1) & (code // 128 == y), at_key, -1)
        code = jnp.concatenate([tab_x[s][:, :NB] for s in range(SIDE)], axis=1)
        at_key = code // 16 % 2 * 32 + code // 128 * NB + code // 2 % NB
        key_b[...] = jnp.where((code % 2 == 1) & (code // 32 % 4 == x), at_key, -1)

    steps = {
        "zs": z_start, "zf": z_forward, "pr": project, "pf": plane_forward, "pe": plane_finish,
        "n": near, "ts": tab_start, "ws": weights_start, "wf": weights_forward, "we": weights_finish,
        "hf": halo_first, "hl": halo_last, "hw": halo_wait,
        "ro": rows_out, "ko": keys_out, "pp": prepare,
    }
    for name, place in ORDER:
        steps[name](place)
    for copy in core_copies:
        copy.wait_recv()
    for copy in local_copies:
        copy.wait()
    for copy in pending:
        copy.wait_send()


def gather_call(ent, gain, wqkv, tab, w_up, w_down):
    vmem = pl.BlockSpec(memory_space=pltpu.VMEM)
    hbm = pl.BlockSpec(memory_space=pl.ANY)
    pinned = pl.BlockSpec(memory_space=pltpu.HBM)
    dma = pltpu.SemaphoreType.DMA
    plane_shape = (2, SIDE, NB, 3, BLK, BLK)
    return pl.pallas_call(
        gather_kernel,
        out_shape=(
            jax.ShapeDtypeStruct(plane_shape, BF16),
            jax.ShapeDtypeStruct(plane_shape, BF16),
            jax.ShapeDtypeStruct((NB, 2, BLK, BLK), F32),
            jax.ShapeDtypeStruct((NB, 2, 8, BLK), F32),
            jax.ShapeDtypeStruct((GROUP, WIDTH), BF16),
            jax.ShapeDtypeStruct((8, SIDE * NB), jnp.int32),
            jax.ShapeDtypeStruct((8, SIDE * NB), jnp.int32),
            jax.ShapeDtypeStruct((SIDE, 2 * UNITS, WIDTH), BF16),
        ),
        in_specs=[pinned, vmem, pinned, vmem, pinned, pinned],
        out_specs=(hbm, hbm) + (vmem,) * 5 + (hbm,),
        scratch_shapes=[
            pltpu.VMEM((ROWS, PART), BF16),
            pltpu.VMEM((3, WIDTH, PART), BF16),
            pltpu.VMEM((SIDE, ROWS, PART), BF16),
            pltpu.VMEM((NB, 3, BLK, BLK), BF16),
            pltpu.VMEM((NB, 3, BLK, BLK), BF16),
            pltpu.VMEM((2, 2, BLK, BLK), BF16),
            pltpu.VMEM((2, 2, BLK, BLK), BF16),
            pltpu.VMEM((SIDE, NB, BLK), jnp.int32),
            pltpu.VMEM((SIDE, NB, BLK), jnp.int32),
            pltpu.VMEM((WIDTH, BLK), BF16),
            pltpu.VMEM((BLK, WIDTH), F32),
            pltpu.VMEM((2 * UNITS, WIDTH), BF16),
            dma((CHUNKS, 4)), dma((CHUNKS, 4)),
            dma((CHUNKS, 4)), dma((CHUNKS, 4)),
            dma((CHUNKS, 4)), dma((CHUNKS, 4)),
            dma((CHUNKS * 10,)), dma((CHUNKS * 10,)),
            dma((4,)), dma((4,)),
            dma((CHUNKS * 2,)),
            dma((2, 3)), dma((2, 3)),
            dma((8,)), dma((8,)),
            dma((6,)),
        ],
        compiler_params=pltpu.CompilerParams(
            collective_id=0, has_side_effects=True, vmem_limit_bytes=60 * MB
        ),
        name="gather_project",
    )(ent, gain, wqkv, tab, w_up, w_down)


def far_kernel(
    key_a, key_b, x_hbm, y_hbm, oa, ob, query, pairs, acc, state, hits_a, hits_b, qs, ks
):
    core = lax.axis_index("loc") % 2
    live_q = SIDE * NB
    mine = pl.ds(core * live_q, live_q)
    loads = []
    for pair, (keys_hbm, query_hbm) in enumerate(((x_hbm, y_hbm), (y_hbm, x_hbm))):
        loads.append(
            (
                pltpu.make_async_copy(query_hbm.at[mine, 2], query.at[pair], qs.at[pair]),
                pltpu.make_async_copy(keys_hbm.at[:, pl.ds(0, 2)], pairs.at[pair], ks.at[pair]),
            )
        )
    for pair in loads:
        for load in pair:
            load.start()

    def find(s, counts):
        counts = list(counts)
        for b in range(NB):
            for j in range(4):
                for pair, (keys, hits) in enumerate(((key_a, hits_a), (key_b, hits_b))):
                    key = keys[j, s * NB + b]
                    hits[counts[pair]] = (s * NB + b) * 1024 + key
                    counts[pair] = counts[pair] + jnp.where(key >= 0, 1, 0)
        return tuple(counts)

    counts = lax.fori_loop(0, SIDE, find, (0, 0))
    for hits, count in zip((hits_a, hits_b), counts):
        for extra in range(4):
            hits[count + extra] = live_q * 1024

    def clear(i, carry):
        acc[i] = jnp.zeros((BLK, BLK), F32)
        state[i, 0:2] = jnp.full((2, BLK), NEG, F32)
        state[i, 2:8] = jnp.zeros((6, BLK), F32)
        return carry

    lax.fori_loop(0, 2 * (live_q + 1), clear, 0)

    for pair in range(2):
        hits, count = (hits_a, counts[0]) if pair == 0 else (hits_b, counts[1])
        o_ref = oa if pair == 0 else ob
        base = pair * (live_q + 1)
        for load in loads[pair]:
            load.wait()

        def four(step, carry):
            work = []
            for u in range(4):
                code = hits[step * 4 + u]
                q, k = lax.shift_right_logical(code, 10), code & 1023
                asked = split_heads(query[pair, jnp.minimum(q, live_q - 1)])
                key = pairs[pair, k, 0]
                val = pairs[pair, k, 1]
                score = jnp.dot(key, asked, preferred_element_type=F32)
                top = jnp.max(score, axis=0, keepdims=True)
                weight = jnp.exp(score - top)
                total = jnp.sum(weight, axis=0, keepdims=True)
                out = jnp.dot(val, weight.astype(BF16), preferred_element_type=F32)
                work.append((q + base, top, total, out))
            for q, top, total, out in work:
                for h in range(2):
                    cut = slice(h * BLK, (h + 1) * BLK)
                    feat = pl.ds(h * HD, HD)
                    old_top = state[q, h : h + 1]
                    new_top = jnp.maximum(old_top, top[:, cut])
                    keep = jnp.exp(old_top - new_top)
                    add = jnp.exp(top[:, cut] - new_top)
                    acc[q, feat] = acc[q, feat] * keep + out[h * HD : (h + 1) * HD, cut] * add
                    state[q, h : h + 1] = new_top
                    state[q, 2 + h : 3 + h] = state[q, 2 + h : 3 + h] * keep + total[:, cut] * add
            return carry

        lax.fori_loop(0, lax.shift_right_logical(count + 3, 2), four, 0)

        def finish(i, carry):
            st = state[base + i]
            left, terms = st[0:4], []
            for _ in range(3):
                terms.append(left.astype(BF16).astype(F32))
                left = left - terms[-1]
            terms.append(jnp.zeros((4, BLK), F32))
            o_ref[i, BLK:] = jnp.concatenate(terms, axis=0).astype(BF16)
            for h in range(2):
                total = st[2 + h : 3 + h]
                scale = 1.0 / jnp.where(total > 0, total, 1.0)
                feat = pl.ds(h * HD, HD)
                o_ref[i, feat] = (acc[base + i, feat] * scale).astype(BF16)
            return carry

        lax.fori_loop(0, live_q, finish, 0)


def far_call(key_a, key_b, xbuf, ybuf):
    vmem = pl.BlockSpec(memory_space=pltpu.VMEM)
    smem = pl.BlockSpec(memory_space=pltpu.SMEM)
    hbm = pl.BlockSpec(memory_space=pltpu.HBM)
    dma = pltpu.SemaphoreType.DMA
    live_q = SIDE * NB
    o_shape = jax.ShapeDtypeStruct((live_q, TALL, BLK), BF16)
    flat = (2 * live_q, 3, BLK, BLK)
    oa, ob = pl.pallas_call(
        far_kernel,
        out_shape=(o_shape, o_shape),
        in_specs=[smem, smem, hbm, hbm],
        out_specs=(vmem, vmem),
        scratch_shapes=[
            pltpu.VMEM((2, live_q, BLK, BLK), BF16),
            pltpu.VMEM((2, 2 * live_q, 2, BLK, BLK), BF16),
            pltpu.VMEM((2 * (live_q + 1), BLK, BLK), F32),
            pltpu.VMEM((2 * (live_q + 1), 8, BLK), F32),
            pltpu.SMEM((live_q * 4 + 8,), jnp.int32),
            pltpu.SMEM((live_q * 4 + 8,), jnp.int32),
            dma((2,)),
            dma((2,)),
        ],
        compiler_params=pltpu.CompilerParams(vmem_limit_bytes=58 * MB),
        cost_estimate=pl.CostEstimate(
            flops=8 * 10**9, bytes_accessed=30 * MB, transcendentals=3 * 10**6
        ),
        name="far_partials",
    )(key_a, key_b, xbuf.reshape(flat), ybuf.reshape(flat))
    shape = (SIDE, NB, TALL, BLK)
    return oa.reshape(shape), ob.reshape(shape)


def merge_kernel(
    oa, ob, near_o_hbm, near_st_hbm, ent_rows_hbm, w_out_hbm, gain, line_0, line_1, line_2, line_3, result,
    ra, rb, relay, att, part, got_half, got,
    weights, inner, acc, send_sib, got_sib, res, landed, near_o, near_st, ent_rows, w_out,
    os, orr, fs, fr, zs, zr, ws, wr, wl, ss, sr, es, er, ls,
):
    y, x, core, z = coords()
    z_up, z_dn = shifted("z", 1), shifted("z", -1)
    z_opp, sib = shifted("z", 2), shifted("c", 0)
    peers = [shifted("y", 1), shifted("y", -1), shifted("x", 1), shifted("x", -1), z_up, z_dn]
    w_place = y * (1 - core) + x * core
    w_up_to = device(y + 1 - core, x + core, core, z)
    w_dn_to = device(y + 3 * (1 - core), x + 3 * core, core, z)
    peers = peers + [z_opp, sib]
    greet(peers)
    loads = [
        pltpu.make_async_copy(src, dst, ls.at[n])
        for n, (src, dst) in enumerate(
            (
                (oa.at[y], ra.at[y]),
                (ob.at[x], rb.at[x]),
                (near_o_hbm, near_o),
                (near_st_hbm, near_st),
                (w_out_hbm, w_out),
                (ent_rows_hbm, ent_rows),
            )
        )
    ]
    for load in loads:
        load.start()
    line = (line_0, line_1, line_2, line_3)
    w_local = [
        pltpu.make_async_copy(line[n], weights.at[w_place, n], wl.at[n]) for n in range(SIDE)
    ]
    for copy in w_local:
        copy.start()
    greeted(peers)
    pending = []

    def go(copy):
        copy.start()
        pending.append(copy)
        return copy

    groups = [(z + by) % 4 for by in (2, 1, 3, 0)]
    per = NB // SIDE
    lanes = ((y, peers[0], peers[1], oa, ra), (x, peers[2], peers[3], ob, rb))
    relays, arrivals = {}, {}
    for n, g in enumerate(groups):
        arrivals[n] = []
        for k, (place, up, dn, o, ro) in enumerate(lanes):
            send, recv = os.at[k, n], orr.at[k, n]
            far_to, up_to, dn_to = (place + 2) % 4, (place + 1) % 4, (place + 3) % 4
            relays[k, n] = (
                go(remote(o.at[far_to, g * per], relay.at[k, n, 0], send.at[0], recv.at[0], up)),
                go(remote(o.at[far_to, g * per + 1], relay.at[k, n, 1], send.at[1], recv.at[1], dn)),
            )
            both = pl.ds(g * per, per)
            arrivals[n] += [
                go(remote(o.at[up_to, both], ro.at[place, both], send.at[2], recv.at[2], up)),
                go(remote(o.at[dn_to, both], ro.at[place, both], send.at[3], recv.at[3], dn)),
            ]

    def pass_on(n):
        g = groups[n]
        for k, (place, up, dn, o, ro) in enumerate(lanes):
            a, b = relays[k, n]
            a.wait_recv()
            dst = ro.at[(place + 3) % 4, g * per]
            arrivals[n].append(go(remote(relay.at[k, n, 0], dst, fs.at[k, n, 0], fr.at[k, n, 0], up)))
            b.wait_recv()
            dst = ro.at[(place + 1) % 4, g * per + 1]
            arrivals[n].append(go(remote(relay.at[k, n, 1], dst, fs.at[k, n, 1], fr.at[k, n, 1], dn)))

    pass_on(0)
    pass_on(1)
    w_up_copies, w_dn_copies = [None] * 4, [None] * 4

    def weights_start():
        for n in range(SIDE):
            u, d = n, (n + 2) % 4
            dst = weights.at[w_place]
            w_up_copies[u] = go(remote(line[u], dst.at[u], ws.at[0, u], wr.at[0, u], w_up_to))
            w_dn_copies[d] = go(remote(line[d], dst.at[d], ws.at[1, d], wr.at[1, d], w_dn_to))

    pass_on(2)
    pass_on(3)
    weights_start()
    w_far = []

    def weights_forward(n):
        w_up_copies[n].wait_recv()
        view = weights.at[(w_place + 3) % 4, n]
        w_far.append(go(remote(view, view, ws.at[2, n], wr.at[2, n], w_up_to)))
        w_dn_copies[n + 2].wait_recv()
        view = weights.at[(w_place + 1) % 4, n + 2]
        w_far.append(go(remote(view, view, ws.at[2, n + 2], wr.at[2, n + 2], w_dn_to)))

    for load in loads:
        load.wait()

    def merge(b, carry):
        for p, ro in enumerate((ra, rb)):
            stats, outs = [near_st[b, p]], [near_o[b, p]]
            for s in range(SIDE):
                tail = ro[s, b, BLK:].astype(F32)
                stats.append(tail[0:4] + tail[4:8] + tail[8:12])
                outs.append(ro[s, b, :BLK].astype(F32))
            halves = []
            for h in range(2):
                top = functools.reduce(jnp.maximum, [st[h : h + 1] for st in stats])
                scale = [st[2 + h : 3 + h] * jnp.exp(st[h : h + 1] - top) for st in stats]
                inv = 1.0 / functools.reduce(jnp.add, scale)
                halves.append(
                    functools.reduce(
                        jnp.add,
                        [o[h * HD : (h + 1) * HD] * (w * inv) for o, w in zip(outs, scale)],
                    )
                )
            tile = jnp.concatenate(halves, axis=0).T.astype(BF16)
            att[pl.ds(pl.multiple_of(b * BLK, BLK), BLK), p * BLK : (p + 1) * BLK] = tile
        return carry

    def project(n):
        for copy in arrivals[n]:
            copy.wait_recv()
        lax.fori_loop(groups[n] * per, groups[n] * per + per, merge, 0)
        rows = att[pl.ds(pl.multiple_of(groups[n] * GROUP, GROUP), GROUP), :]
        return jnp.dot(rows, w_out[...], preferred_element_type=F32)

    h = GROUP // 2
    part[0] = project(0).astype(BF16)
    f_up = go(remote(part.at[0, pl.ds(0, h)], got_half.at[0], zs.at[0], zr.at[0], z_up))
    f_dn = go(remote(part.at[0, pl.ds(h, h)], got_half.at[1], zs.at[1], zr.at[1], z_dn))
    to_up = project(1)
    part[1, h:] = to_up[h:].astype(BF16)
    f_up.wait_recv()
    part[1, :h] = (to_up[:h] + got_half[0].astype(F32)).astype(BF16)
    s_up = go(remote(part.at[1], got.at[0], zs.at[2], zr.at[2], z_up))
    weights_forward(0)
    to_dn = project(2)
    part[2, :h] = to_dn[:h].astype(BF16)
    f_dn.wait_recv()
    part[2, h:] = (to_dn[h:] + got_half[1].astype(F32)).astype(BF16)
    s_dn = go(remote(part.at[2], got.at[1], zs.at[3], zr.at[3], z_dn))
    mine = project(3) + ent_rows[...].astype(F32)
    weights_forward(1)
    s_up.wait_recv()
    s_dn.wait_recv()
    mixed = mine + got[0].astype(F32) + got[1].astype(F32)
    inner[core] = norm_rows(mixed, gain[...]).astype(BF16)
    to_sib = go(remote(inner.at[core], inner.at[core], ss.at[0], sr.at[0], sib))
    acc[core] = mixed
    acc[1 - core] = jnp.zeros((GROUP, WIDTH), F32)
    for copy in w_local:
        copy.wait()

    def mlp(slot, who):
        w_up = weights[slot, :, :, 0:UNITS].reshape(SIDE * SIDE * UNITS, WIDTH)
        w_down = weights[slot, :, :, UNITS:].reshape(SIDE * SIDE * UNITS, WIDTH)
        hidden = lax.dot_general(
            inner[who], w_up, (((1,), (1,)), ((), ())), preferred_element_type=F32
        )
        acc[who] += jnp.dot(gelu(hidden).astype(BF16), w_down, preferred_element_type=F32)

    def mlp_both(slot):
        def body(t, carry):
            mlp(slot, (core + 1 + t) % 2)
            return carry

        lax.fori_loop(0, 2, body, 0)

    to_sib.wait_recv()
    mlp_both(w_place)
    w_up_copies[2].wait_recv()
    w_up_copies[3].wait_recv()
    mlp_both((w_place + 3) % 4)
    w_dn_copies[0].wait_recv()
    w_dn_copies[1].wait_recv()
    mlp_both((w_place + 1) % 4)
    for copy in w_far:
        copy.wait_recv()
    mlp((w_place + 2) % 4, 1 - core)
    send_sib[...] = acc[1 - core].astype(BF16)
    back = go(remote(send_sib, got_sib, ss.at[1], sr.at[1], sib))
    mlp((w_place + 2) % 4, core)
    back.wait_recv()
    final = (acc[core] + got_sib[...].astype(F32)).astype(BF16)
    for s in range(SIDE):
        res[s] = final[:, s * PART : (s + 1) * PART]
    copies = []
    for n, to in ((2, z_opp), (1, z_up), (3, z_dn)):
        copies.append(go(remote(res.at[(z + n) % 4], landed.at[z], es.at[n], er.at[n], to)))
    result[pl.ds(pl.multiple_of(z * GROUP, GROUP), GROUP), :] = res[z]
    for copy in copies:
        copy.wait_recv()
    for n in range(1, SIDE):
        s = (z + n) % 4
        result[pl.ds(pl.multiple_of(s * GROUP, GROUP), GROUP), :] = landed[s]
    for copy in pending:
        copy.wait_send()


def gelu(v):
    return 0.5 * v * (1.0 + lax.erf(v * 0.7071067811865476))


def merge_call(oa, ob, near_o, near_st, ent_rows, w_out, gain, lines):
    vmem = pl.BlockSpec(memory_space=pltpu.VMEM)
    hbm = pl.BlockSpec(memory_space=pltpu.HBM)
    dma = pltpu.SemaphoreType.DMA
    return pl.pallas_call(
        merge_kernel,
        out_shape=jax.ShapeDtypeStruct((ROWS, PART), BF16),
        in_specs=[hbm] * 6 + [vmem] + [hbm] * 4,
        out_specs=vmem,
        scratch_shapes=[
            pltpu.VMEM((SIDE, NB, TALL, BLK), BF16),
            pltpu.VMEM((SIDE, NB, TALL, BLK), BF16),
            pltpu.VMEM((2, SIDE, 2, TALL, BLK), BF16),
            pltpu.VMEM((ROWS, 2 * BLK), BF16),
            pltpu.VMEM((3, GROUP, WIDTH), BF16),
            pltpu.VMEM((2, GROUP // 2, WIDTH), BF16),
            pltpu.VMEM((2, GROUP, WIDTH), BF16),
            pltpu.VMEM((SIDE, SIDE, SIDE, 2 * UNITS, WIDTH), BF16),
            pltpu.VMEM((2, GROUP, WIDTH), BF16),
            pltpu.VMEM((2, GROUP, WIDTH), F32),
            pltpu.VMEM((GROUP, WIDTH), BF16),
            pltpu.VMEM((GROUP, WIDTH), BF16),
            pltpu.VMEM((SIDE, GROUP, PART), BF16),
            pltpu.VMEM((SIDE, GROUP, PART), BF16),
            pltpu.VMEM((NB, 2, BLK, BLK), F32),
            pltpu.VMEM((NB, 2, 8, BLK), F32),
            pltpu.VMEM((GROUP, WIDTH), BF16),
            pltpu.VMEM((PART, WIDTH), BF16),
            dma((2, 4, 4)), dma((2, 4, 4)),
            dma((2, 4, 2)), dma((2, 4, 2)),
            dma((4,)), dma((4,)),
            dma((3, 4)), dma((3, 4)), dma((4,)),
            dma((2,)), dma((2,)),
            dma((4,)), dma((4,)),
            dma((8,)),
        ],
        compiler_params=pltpu.CompilerParams(
            collective_id=1, has_side_effects=True, vmem_limit_bytes=60 * MB
        ),
        name="merge_project",
    )(oa, ob, near_o, near_st, ent_rows, w_out, gain, *lines)


def on_device(
    entities, attn_gain, w_qkv, w_out, mlp_gain, w_up, w_down, far_owner, far_local, far_live
):
    xbuf, ybuf, near_o, near_st, ent_rows, key_a, key_b, piece = gather_call(
        entities,
        attn_gain.reshape(1, WIDTH),
        w_qkv,
        jnp.pad(((far_owner * NB + far_local) * 2 + far_live).T, ((0, 4), (0, BLK - NB))),
        w_up,
        w_down,
    )
    def along(by):
        pairs = []
        for i in range(lax.axis_size("loc")):
            y, x, core = i // 8, i // 2 % 4, i % 2
            y, x = (y, (x + by) % 4) if core == 0 else ((y + by) % 4, x)
            pairs.append((i, (y * 4 + x) * 2 + core))
        return lax.ppermute(piece, "loc", pairs)

    lines = [piece] + [along(by) for by in (2, 1, 3)]
    oa, ob = far_call(key_a, key_b, xbuf, ybuf)
    return merge_call(
        oa, ob, near_o, near_st, ent_rows, w_out, mlp_gain.reshape(1, WIDTH), lines
    )


def solution(mesh):
    return jax.shard_map(
        on_device,
        mesh=mesh,
        in_specs=(
            P("loc", "head"),
            P(),
            P(None, None, "head"),
            P("head", None),
            P(),
            P(None, "head"),
            P("head", None),
            P("loc", None),
            P("loc", None),
            P("loc", None),
        ),
        out_specs=P("loc", "head"),
        check_vma=False,
    )
```

```python
import functools

import jax
import jax.numpy as jnp
from jax import lax
from jax.experimental import pallas as pl
from jax.experimental.pallas import tpu as pltpu
from jax.sharding import PartitionSpec as P

MESH = pl.DeviceIdType.MESH
F32 = jnp.float32
BF16 = jnp.bfloat16
BLK = 128
HD = 64
NB = 8
SIDE = 4
CHUNKS = 4
ROWS = NB * BLK
GROUP = ROWS // SIDE
WIDTH = 1024
PART = WIDTH // SIDE
NEG = -1e30
MB = 2**20
TALL = BLK + 16
UNITS = 32


def coords():
    loc = lax.axis_index("loc")
    return loc // 8, (loc // 2) % 4, loc % 2, lax.axis_index("head")


def device(y, x, core, z):
    return ((y % 4 * 4 + x % 4) * 2 + core, z % 4)


def shifted(axis, by):
    y, x, core, z = coords()
    if axis == "y":
        return device(y + by + 4, x, core, z)
    if axis == "x":
        return device(y, x + by + 4, core, z)
    if axis == "z":
        return device(y, x, core, z + by + 4)
    return device(y, x, 1 - core, z)


def loc_shifted(by):
    return ((lax.axis_index("loc") + by + 32) % 32, lax.axis_index("head"))


def greet(peers):
    barrier = pltpu.get_barrier_semaphore()
    for peer in peers:
        pl.semaphore_signal(barrier, inc=1, device_id=peer, device_id_type=MESH)


def greeted(peers):
    pl.semaphore_wait(pltpu.get_barrier_semaphore(), len(peers))


def remote(src, dst, send, recv, to):
    return pltpu.make_async_remote_copy(
        src_ref=src, dst_ref=dst, send_sem=send, recv_sem=recv, device_id=to, device_id_type=MESH
    )


def norm_rows(values, gain):
    center = values - jnp.mean(values, axis=-1, keepdims=True)
    spread = jnp.mean(center * center, axis=-1, keepdims=True)
    return center * lax.rsqrt(spread + 1e-05) * gain


def split_heads(query):
    zero = jnp.zeros((HD, BLK), query.dtype)
    top = jnp.concatenate([query[:HD], zero], axis=1)
    low = jnp.concatenate([zero, query[HD:]], axis=1)
    return jnp.concatenate([top, low], axis=0)


ORDER = (
    ("zs", 0), ("zs", 1), ("ts", 0), ("pp", 0), ("zf", 0), ("zs", 2), ("zf", 1), ("zs", 3),
    ("pr", 0), ("hf", 0), ("zf", 2), ("pr", 1), ("zf", 3), ("ws", 0), ("pf", 0), ("pr", 2),
    ("pf", 1), ("pr", 3), ("hl", 0), ("pf", 2), ("wf", 0), ("pf", 3), ("ro", 0),
    ("pe", 0), ("n", 1), ("n", 2), ("n", 3), ("n", 4), ("n", 5), ("pe", 1), ("n", 6), ("hw", 0),
    ("n", 7), ("n", 0), ("ko", 0), ("pe", 2), ("pe", 3), ("we", 0),
)


def gather_kernel(
    ent_hbm, gain, wqkv_hbm, tab, up_hbm, down_hbm,
    xbuf, ybuf, near_o, near_st, ent_rows, key_a, key_b, wz,
    ent, wqkv, zbuf, xown, yown, halo_low, halo_high, tab_y, tab_x, up_cols, up_rows, piece,
    zs, zr, xs, xr, ys, yr, cs, cr, hs, hr, ls, ts, tr, ws, wr, wl,
):
    y, x, core, z = coords()
    loc = lax.axis_index("loc")
    z_up, z_dn = shifted("z", 1), shifted("z", -1)
    x_up, x_dn = shifted("x", 1), shifted("x", -1)
    y_up, y_dn = shifted("y", 1), shifted("y", -1)
    sib = shifted("c", 0)
    nxt, prv = loc_shifted(1), loc_shifted(-1)
    y_opp, x_opp = shifted("y", 2), shifted("x", 2)
    peers = [z_up, z_dn, x_up, x_dn, y_up, y_dn, sib, nxt, prv, y_opp, x_opp]
    greet(peers)
    load_up = pltpu.make_async_copy(
        up_hbm.at[:, pl.ds(pl.multiple_of(loc // 4 * BLK, BLK), BLK)], up_cols, wl.at[0]
    )
    load_down = pltpu.make_async_copy(
        down_hbm.at[pl.ds(pl.multiple_of(loc * UNITS, UNITS), UNITS)],
        piece.at[pl.ds(UNITS, UNITS)],
        wl.at[1],
    )
    load_ent = pltpu.make_async_copy(ent_hbm, ent, wl.at[4])
    load_qkv = pltpu.make_async_copy(wqkv_hbm, wqkv, wl.at[5])
    load_ent.start()
    load_up.start()
    load_down.start()
    load_qkv.start()
    tab_y[y] = tab[...]
    tab_x[x] = tab[...]
    load_ent.wait()
    greeted(peers)
    rows = ROWS // CHUNKS
    blocks = NB // CHUNKS
    pending = []

    def go(copy):
        copy.start()
        pending.append(copy)
        return copy

    z_near = []

    def z_start(r):
        at = pl.ds(r * rows, rows)
        z_near.append(
            (
                go(remote(ent.at[at], zbuf.at[z, at], zs.at[r, 0], zr.at[r, 0], z_up)),
                go(remote(ent.at[at], zbuf.at[z, at], zs.at[r, 1], zr.at[r, 1], z_dn)),
            )
        )

    tab_copies = []

    def tab_start(_):
        for k, (dst, place, to) in enumerate(
            ((tab_y, y, (y_up, y_dn, y_opp)), (tab_x, x, (x_up, x_dn, x_opp)))
        ):
            for n, peer in enumerate(to):
                tab_copies.append(go(remote(tab, dst.at[place], ts.at[k, n], tr.at[k, n], peer)))

    lines = {}
    place_copies = []

    def weights_start(_):
        load_up.wait()
        load_down.wait()
        up_rows[...] = up_cols[...].astype(F32).T
        piece[0:UNITS] = up_rows[pl.ds(pl.multiple_of(loc % 4 * UNITS, UNITS), UNITS)].astype(BF16)
        lines["z"] = (
            go(remote(piece, wz.at[z], ws.at[0], wr.at[0], z_up)),
            go(remote(piece, wz.at[z], ws.at[1], wr.at[1], z_dn)),
        )
        local = pltpu.make_async_copy(piece, wz.at[z], wl.at[2])
        local.start()
        place_copies.append(local)

    def line_pass(name, buf, place, sem, up, dn, half):
        a, b = lines[name]
        a.wait_recv()
        view = buf.at[(place + 3) % 4, pl.ds(0, half)]
        c = go(remote(view, view, ws.at[sem], wr.at[sem], up))
        b.wait_recv()
        view = buf.at[(place + 1) % 4, pl.ds(half, half)]
        d = go(remote(view, view, ws.at[sem + 1], wr.at[sem + 1], dn))
        lines[name] = (c, d)

    def weights_forward(_):
        line_pass("z", wz, z, 2, z_up, z_dn, UNITS)

    def weights_finish(_):
        for copy in lines["z"]:
            copy.wait_recv()
        place_copies.pop().wait()

    def prepare(_):
        zbuf[z] = ent[...]
        load_qkv.wait()

    z_far = []

    def z_forward(r):
        a, b = z_near[r]
        low = pl.ds(r * rows, rows // 2)
        high = pl.ds(r * rows + rows // 2, rows // 2)
        a.wait_recv()
        s = (z + 3) % 4
        c = go(remote(zbuf.at[s, low], zbuf.at[s, low], zs.at[r, 2], zr.at[r, 2], z_up))
        b.wait_recv()
        s = (z + 1) % 4
        d = go(remote(zbuf.at[s, high], zbuf.at[s, high], zs.at[r, 3], zr.at[r, 3], z_dn))
        z_far.append((c, d))

    plane = {}
    core_copies = []
    local_copies = []

    def to_sibling(buf, place, blks, sem, src=None):
        view = buf.at[core, place, blks, pl.ds(0, 2)]
        core_copies.append(go(remote(view if src is None else src, view, cs.at[sem], cr.at[sem], sib)))

    def project(r):
        for copy in z_far[r]:
            copy.wait_recv()
        at = pl.ds(r * rows, rows)
        full = jnp.concatenate([zbuf[s, at, :] for s in range(SIDE)], axis=1).astype(F32)
        normed = norm_rows(full, gain[...]).astype(BF16)
        queries = jnp.dot(normed, wqkv[0], preferred_element_type=F32)
        keys = jnp.dot(normed, wqkv[1], preferred_element_type=F32).astype(BF16)
        values = jnp.dot(normed, wqkv[2], preferred_element_type=F32)
        q_t = (queries.T.astype(BF16).astype(F32) * 0.125).astype(BF16)
        v_t = values.T.astype(BF16)
        for i in range(blocks):
            b = r * blocks + i
            cut = slice(i * BLK, (i + 1) * BLK)
            xown[b, 0] = keys[cut, :BLK]
            yown[b, 0] = keys[cut, BLK:]
            xown[b, 1] = v_t[:BLK, cut]
            yown[b, 1] = v_t[BLK:, cut]
            yown[b, 2] = q_t[:BLK, cut]
            xown[b, 2] = q_t[BLK:, cut]
        blks = pl.ds(r * blocks, blocks)
        for name, own, buf, place, send, recv, up, dn, k in (
            ("x", xown, xbuf, x, xs, xr, x_up, x_dn, 0),
            ("y", yown, ybuf, y, ys, yr, y_up, y_dn, 1),
        ):
            src, dst = own.at[blks], buf.at[core, place, blks]
            plane[name, r] = (
                go(remote(src, dst, send.at[r, 0], recv.at[r, 0], up)),
                go(remote(src, dst, send.at[r, 1], recv.at[r, 1], dn)),
            )
            local = pltpu.make_async_copy(src, dst, ls.at[r * 2 + k])
            local.start()
            local_copies.append(local)
            to_sibling(buf, place, blks, r * 10 + k * 5, own.at[blks, pl.ds(0, 2)])

    def plane_forward(r):
        blks = pl.ds(r * blocks, blocks)
        low = pl.ds(r * blocks, blocks // 2)
        high = pl.ds(r * blocks + blocks // 2, blocks // 2)
        for name, buf, place, send, recv, up, dn, k in (
            ("x", xbuf, x, xs, xr, x_up, x_dn, 0),
            ("y", ybuf, y, ys, yr, y_up, y_dn, 1),
        ):
            a, b = plane[name, r]
            a.wait_recv()
            s = (place + 3) % 4
            view = buf.at[core, s, low]
            c = go(remote(view, view, send.at[r, 2], recv.at[r, 2], up))
            to_sibling(buf, s, blks, r * 10 + k * 5 + 1)
            b.wait_recv()
            s = (place + 1) % 4
            view = buf.at[core, s, high]
            d = go(remote(view, view, send.at[r, 3], recv.at[r, 3], dn))
            to_sibling(buf, s, blks, r * 10 + k * 5 + 2)
            plane[name, r] = (c, d)

    def plane_finish(r):
        low = pl.ds(r * blocks, blocks // 2)
        high = pl.ds(r * blocks + blocks // 2, blocks // 2)
        for name, buf, place, k in (("x", xbuf, x, 0), ("y", ybuf, y, 1)):
            c, d = plane[name, r]
            s = (place + 2) % 4
            c.wait_recv()
            to_sibling(buf, s, low, r * 10 + k * 5 + 3)
            d.wait_recv()
            to_sibling(buf, s, high, r * 10 + k * 5 + 4)

    def near(b):
        for p, (own, other) in enumerate(((xown, yown), (yown, xown))):
            query = split_heads(other[b, 2])
            parts = []
            for step in (-1, 0, 1):
                if b + step < 0:
                    key, val, ok = halo_low[p, 0], halo_low[p, 1], loc > 0
                elif b + step >= NB:
                    key, val, ok = halo_high[p, 0], halo_high[p, 1], loc < 31
                else:
                    key, val, ok = own[b + step, 0], own[b + step, 1], None
                score = jnp.dot(key, query, preferred_element_type=F32)
                if ok is not None:
                    score = jnp.where(ok, score, NEG)
                parts.append((score, val))
            top = functools.reduce(
                jnp.maximum, [jnp.max(score, axis=0, keepdims=True) for score, _ in parts]
            )
            total = jnp.zeros((1, 2 * BLK), F32)
            out = jnp.zeros((BLK, 2 * BLK), F32)
            for score, val in parts:
                weight = jnp.exp(score - top)
                total = total + jnp.sum(weight, axis=0, keepdims=True)
                out = out + jnp.dot(val, weight.astype(BF16), preferred_element_type=F32)
            near_o[b, p] = jnp.concatenate(
                [out[:HD, :BLK] / total[:, :BLK], out[HD:, BLK:] / total[:, BLK:]], axis=0
            )
            near_st[b, p, 0:1] = top[:, :BLK]
            near_st[b, p, 1:2] = top[:, BLK:]
            near_st[b, p, 2:3] = total[:, :BLK]
            near_st[b, p, 3:4] = total[:, BLK:]
            near_st[b, p, 4:8] = jnp.zeros((4, BLK), F32)

    halos = []

    def halo_first(_):
        for p, own in enumerate((xown, yown)):
            halos.append(go(remote(own.at[0, pl.ds(0, 2)], halo_high.at[p], hs.at[p], hr.at[p], prv)))

    def halo_last(_):
        for p, own in enumerate((xown, yown)):
            src = own.at[NB - 1, pl.ds(0, 2)]
            halos.append(go(remote(src, halo_low.at[p], hs.at[2 + p], hr.at[2 + p], nxt)))

    def halo_wait(_):
        for copy in halos:
            copy.wait_recv()

    def rows_out(_):
        mine = pl.ds(pl.multiple_of(z * GROUP, GROUP), GROUP)
        ent_rows[...] = jnp.concatenate([zbuf[s, mine, :] for s in range(SIDE)], axis=1)

    def keys_out(_):
        for copy in tab_copies:
            copy.wait_recv()
        code = jnp.concatenate([tab_y[s][:, :NB] for s in range(SIDE)], axis=1)
        at_key = code // 16 % 2 * 32 + code // 32 % 4 * NB + code // 2 % NB
        key_a[...] = jnp.where((code % 2 == 1) & (code // 128 == y), at_key, -1)
        code = jnp.concatenate([tab_x[s][:, :NB] for s in range(SIDE)], axis=1)
        at_key = code // 16 % 2 * 32 + code // 128 * NB + code // 2 % NB
        key_b[...] = jnp.where((code % 2 == 1) & (code // 32 % 4 == x), at_key, -1)

    steps = {
        "zs": z_start, "zf": z_forward, "pr": project, "pf": plane_forward, "pe": plane_finish,
        "n": near, "ts": tab_start, "ws": weights_start, "wf": weights_forward, "we": weights_finish,
        "hf": halo_first, "hl": halo_last, "hw": halo_wait,
        "ro": rows_out, "ko": keys_out, "pp": prepare,
    }
    for name, place in ORDER:
        steps[name](place)
    for copy in core_copies:
        copy.wait_recv()
    for copy in local_copies:
        copy.wait()
    for copy in pending:
        copy.wait_send()


def gather_call(ent, gain, wqkv, tab, w_up, w_down):
    vmem = pl.BlockSpec(memory_space=pltpu.VMEM)
    hbm = pl.BlockSpec(memory_space=pl.ANY)
    pinned = pl.BlockSpec(memory_space=pltpu.HBM)
    dma = pltpu.SemaphoreType.DMA
    plane_shape = (2, SIDE, NB, 3, BLK, BLK)
    return pl.pallas_call(
        gather_kernel,
        out_shape=(
            jax.ShapeDtypeStruct(plane_shape, BF16),
            jax.ShapeDtypeStruct(plane_shape, BF16),
            jax.ShapeDtypeStruct((NB, 2, BLK, BLK), F32),
            jax.ShapeDtypeStruct((NB, 2, 8, BLK), F32),
            jax.ShapeDtypeStruct((GROUP, WIDTH), BF16),
            jax.ShapeDtypeStruct((8, SIDE * NB), jnp.int32),
            jax.ShapeDtypeStruct((8, SIDE * NB), jnp.int32),
            jax.ShapeDtypeStruct((SIDE, 2 * UNITS, WIDTH), BF16),
        ),
        in_specs=[pinned, vmem, pinned, vmem, pinned, pinned],
        out_specs=(hbm, hbm) + (vmem,) * 5 + (hbm,),
        scratch_shapes=[
            pltpu.VMEM((ROWS, PART), BF16),
            pltpu.VMEM((3, WIDTH, PART), BF16),
            pltpu.VMEM((SIDE, ROWS, PART), BF16),
            pltpu.VMEM((NB, 3, BLK, BLK), BF16),
            pltpu.VMEM((NB, 3, BLK, BLK), BF16),
            pltpu.VMEM((2, 2, BLK, BLK), BF16),
            pltpu.VMEM((2, 2, BLK, BLK), BF16),
            pltpu.VMEM((SIDE, NB, BLK), jnp.int32),
            pltpu.VMEM((SIDE, NB, BLK), jnp.int32),
            pltpu.VMEM((WIDTH, BLK), BF16),
            pltpu.VMEM((BLK, WIDTH), F32),
            pltpu.VMEM((2 * UNITS, WIDTH), BF16),
            dma((CHUNKS, 4)), dma((CHUNKS, 4)),
            dma((CHUNKS, 4)), dma((CHUNKS, 4)),
            dma((CHUNKS, 4)), dma((CHUNKS, 4)),
            dma((CHUNKS * 10,)), dma((CHUNKS * 10,)),
            dma((4,)), dma((4,)),
            dma((CHUNKS * 2,)),
            dma((2, 3)), dma((2, 3)),
            dma((8,)), dma((8,)),
            dma((6,)),
        ],
        compiler_params=pltpu.CompilerParams(
            collective_id=0, has_side_effects=True, vmem_limit_bytes=60 * MB
        ),
        name="gather_project",
    )(ent, gain, wqkv, tab, w_up, w_down)


def far_kernel(
    key_a, key_b, x_hbm, y_hbm, oa, ob, query, pairs, acc, state, hits_a, hits_b, qs, ks
):
    core = lax.axis_index("loc") % 2
    live_q = SIDE * NB
    mine = pl.ds(core * live_q, live_q)
    loads = []
    for pair, (keys_hbm, query_hbm) in enumerate(((x_hbm, y_hbm), (y_hbm, x_hbm))):
        loads.append(
            (
                pltpu.make_async_copy(query_hbm.at[mine, 2], query.at[pair], qs.at[pair]),
                pltpu.make_async_copy(keys_hbm.at[:, pl.ds(0, 2)], pairs.at[pair], ks.at[pair]),
            )
        )
    for pair in loads:
        for load in pair:
            load.start()

    def find(s, counts):
        counts = list(counts)
        for b in range(NB):
            for j in range(4):
                for pair, (keys, hits) in enumerate(((key_a, hits_a), (key_b, hits_b))):
                    key = keys[j, s * NB + b]
                    hits[counts[pair]] = (s * NB + b) * 1024 + key
                    counts[pair] = counts[pair] + jnp.where(key >= 0, 1, 0)
        return tuple(counts)

    counts = lax.fori_loop(0, SIDE, find, (0, 0))
    for hits, count in zip((hits_a, hits_b), counts):
        for extra in range(8):
            hits[count + extra] = live_q * 1024

    def clear(i, carry):
        acc[i] = jnp.zeros((BLK, BLK), F32)
        state[i, 0:2] = jnp.full((2, BLK), NEG, F32)
        state[i, 2:8] = jnp.zeros((6, BLK), F32)
        return carry

    lax.fori_loop(0, 2 * (live_q + 1), clear, 0)

    for pair in range(2):
        hits, count = (hits_a, counts[0]) if pair == 0 else (hits_b, counts[1])
        o_ref = oa if pair == 0 else ob
        base = pair * (live_q + 1)
        for load in loads[pair]:
            load.wait()

        def eight(step, carry):
            work = []
            for u in range(8):
                code = hits[step * 8 + u]
                q, k = lax.shift_right_logical(code, 10), code & 1023
                asked = split_heads(query[pair, jnp.minimum(q, live_q - 1)])
                key = pairs[pair, k, 0]
                val = pairs[pair, k, 1]
                score = jnp.dot(key, asked, preferred_element_type=F32)
                top = jnp.max(score, axis=0, keepdims=True)
                weight = jnp.exp(score - top)
                total = jnp.sum(weight, axis=0, keepdims=True)
                out = jnp.dot(val, weight.astype(BF16), preferred_element_type=F32)
                work.append((q + base, top, total, out))
            for q, top, total, out in work:
                for h in range(2):
                    cut = slice(h * BLK, (h + 1) * BLK)
                    feat = pl.ds(h * HD, HD)
                    old_top = state[q, h : h + 1]
                    new_top = jnp.maximum(old_top, top[:, cut])
                    keep = jnp.exp(old_top - new_top)
                    add = jnp.exp(top[:, cut] - new_top)
                    acc[q, feat] = acc[q, feat] * keep + out[h * HD : (h + 1) * HD, cut] * add
                    state[q, h : h + 1] = new_top
                    state[q, 2 + h : 3 + h] = state[q, 2 + h : 3 + h] * keep + total[:, cut] * add
            return carry

        lax.fori_loop(0, lax.shift_right_logical(count + 7, 3), eight, 0)

        def finish(i, carry):
            st = state[base + i]
            left, terms = st[0:4], []
            for _ in range(3):
                terms.append(left.astype(BF16).astype(F32))
                left = left - terms[-1]
            terms.append(jnp.zeros((4, BLK), F32))
            o_ref[i, BLK:] = jnp.concatenate(terms, axis=0).astype(BF16)
            for h in range(2):
                total = st[2 + h : 3 + h]
                scale = 1.0 / jnp.where(total > 0, total, 1.0)
                feat = pl.ds(h * HD, HD)
                o_ref[i, feat] = (acc[base + i, feat] * scale).astype(BF16)
            return carry

        lax.fori_loop(0, live_q, finish, 0)


def far_call(key_a, key_b, xbuf, ybuf):
    vmem = pl.BlockSpec(memory_space=pltpu.VMEM)
    smem = pl.BlockSpec(memory_space=pltpu.SMEM)
    hbm = pl.BlockSpec(memory_space=pltpu.HBM)
    dma = pltpu.SemaphoreType.DMA
    live_q = SIDE * NB
    o_shape = jax.ShapeDtypeStruct((live_q, TALL, BLK), BF16)
    flat = (2 * live_q, 3, BLK, BLK)
    oa, ob = pl.pallas_call(
        far_kernel,
        out_shape=(o_shape, o_shape),
        in_specs=[smem, smem, hbm, hbm],
        out_specs=(vmem, vmem),
        scratch_shapes=[
            pltpu.VMEM((2, live_q, BLK, BLK), BF16),
            pltpu.VMEM((2, 2 * live_q, 2, BLK, BLK), BF16),
            pltpu.VMEM((2 * (live_q + 1), BLK, BLK), F32),
            pltpu.VMEM((2 * (live_q + 1), 8, BLK), F32),
            pltpu.SMEM((live_q * 4 + 8,), jnp.int32),
            pltpu.SMEM((live_q * 4 + 8,), jnp.int32),
            dma((2,)),
            dma((2,)),
        ],
        compiler_params=pltpu.CompilerParams(vmem_limit_bytes=58 * MB),
        cost_estimate=pl.CostEstimate(
            flops=8 * 10**9, bytes_accessed=30 * MB, transcendentals=3 * 10**6
        ),
        name="far_partials",
    )(key_a, key_b, xbuf.reshape(flat), ybuf.reshape(flat))
    shape = (SIDE, NB, TALL, BLK)
    return oa.reshape(shape), ob.reshape(shape)


def merge_kernel(
    oa, ob, near_o_hbm, near_st_hbm, ent_rows_hbm, w_out_hbm, gain, line_0, line_1, line_2, line_3, result,
    ra, rb, relay, att, part, got_half, got,
    weights, inner, acc, send_sib, got_sib, res, landed, near_o, near_st, ent_rows, w_out,
    os, orr, fs, fr, zs, zr, ws, wr, wl, ss, sr, es, er, ls,
):
    y, x, core, z = coords()
    z_up, z_dn = shifted("z", 1), shifted("z", -1)
    z_opp, sib = shifted("z", 2), shifted("c", 0)
    peers = [shifted("y", 1), shifted("y", -1), shifted("x", 1), shifted("x", -1), z_up, z_dn]
    w_place = y * (1 - core) + x * core
    w_up_to = device(y + 1 - core, x + core, core, z)
    w_dn_to = device(y + 3 * (1 - core), x + 3 * core, core, z)
    peers = peers + [z_opp, sib]
    greet(peers)
    loads = [
        pltpu.make_async_copy(src, dst, ls.at[n])
        for n, (src, dst) in enumerate(
            (
                (oa.at[y], ra.at[y]),
                (ob.at[x], rb.at[x]),
                (near_o_hbm, near_o),
                (near_st_hbm, near_st),
                (w_out_hbm, w_out),
                (ent_rows_hbm, ent_rows),
            )
        )
    ]
    for load in loads:
        load.start()
    line = (line_0, line_1, line_2, line_3)
    w_local = [
        pltpu.make_async_copy(line[n], weights.at[w_place, n], wl.at[n]) for n in range(SIDE)
    ]
    for copy in w_local:
        copy.start()
    greeted(peers)
    pending = []

    def go(copy):
        copy.start()
        pending.append(copy)
        return copy

    groups = [(z + by) % 4 for by in (2, 1, 3, 0)]
    per = NB // SIDE
    lanes = ((y, peers[0], peers[1], oa, ra), (x, peers[2], peers[3], ob, rb))
    relays, arrivals = {}, {}
    for n, g in enumerate(groups):
        arrivals[n] = []
        for k, (place, up, dn, o, ro) in enumerate(lanes):
            send, recv = os.at[k, n], orr.at[k, n]
            far_to, up_to, dn_to = (place + 2) % 4, (place + 1) % 4, (place + 3) % 4
            relays[k, n] = (
                go(remote(o.at[far_to, g * per], relay.at[k, n, 0], send.at[0], recv.at[0], up)),
                go(remote(o.at[far_to, g * per + 1], relay.at[k, n, 1], send.at[1], recv.at[1], dn)),
            )
            both = pl.ds(g * per, per)
            arrivals[n] += [
                go(remote(o.at[up_to, both], ro.at[place, both], send.at[2], recv.at[2], up)),
                go(remote(o.at[dn_to, both], ro.at[place, both], send.at[3], recv.at[3], dn)),
            ]

    def pass_on(n):
        g = groups[n]
        for k, (place, up, dn, o, ro) in enumerate(lanes):
            a, b = relays[k, n]
            a.wait_recv()
            dst = ro.at[(place + 3) % 4, g * per]
            arrivals[n].append(go(remote(relay.at[k, n, 0], dst, fs.at[k, n, 0], fr.at[k, n, 0], up)))
            b.wait_recv()
            dst = ro.at[(place + 1) % 4, g * per + 1]
            arrivals[n].append(go(remote(relay.at[k, n, 1], dst, fs.at[k, n, 1], fr.at[k, n, 1], dn)))

    pass_on(0)
    pass_on(1)
    w_up_copies, w_dn_copies = [None] * 4, [None] * 4

    def weights_start():
        for n in range(SIDE):
            u, d = n, (n + 2) % 4
            dst = weights.at[w_place]
            w_up_copies[u] = go(remote(line[u], dst.at[u], ws.at[0, u], wr.at[0, u], w_up_to))
            w_dn_copies[d] = go(remote(line[d], dst.at[d], ws.at[1, d], wr.at[1, d], w_dn_to))

    pass_on(2)
    pass_on(3)
    weights_start()
    w_far = []

    def weights_forward(n):
        w_up_copies[n].wait_recv()
        view = weights.at[(w_place + 3) % 4, n]
        w_far.append(go(remote(view, view, ws.at[2, n], wr.at[2, n], w_up_to)))
        w_dn_copies[n + 2].wait_recv()
        view = weights.at[(w_place + 1) % 4, n + 2]
        w_far.append(go(remote(view, view, ws.at[2, n + 2], wr.at[2, n + 2], w_dn_to)))

    for load in loads:
        load.wait()

    def merge(b, carry):
        for p, ro in enumerate((ra, rb)):
            stats, outs = [near_st[b, p]], [near_o[b, p]]
            for s in range(SIDE):
                tail = ro[s, b, BLK:].astype(F32)
                stats.append(tail[0:4] + tail[4:8] + tail[8:12])
                outs.append(ro[s, b, :BLK].astype(F32))
            halves = []
            for h in range(2):
                top = functools.reduce(jnp.maximum, [st[h : h + 1] for st in stats])
                scale = [st[2 + h : 3 + h] * jnp.exp(st[h : h + 1] - top) for st in stats]
                inv = 1.0 / functools.reduce(jnp.add, scale)
                halves.append(
                    functools.reduce(
                        jnp.add,
                        [o[h * HD : (h + 1) * HD] * (w * inv) for o, w in zip(outs, scale)],
                    )
                )
            tile = jnp.concatenate(halves, axis=0).T.astype(BF16)
            att[pl.ds(pl.multiple_of(b * BLK, BLK), BLK), p * BLK : (p + 1) * BLK] = tile
        return carry

    def project(n):
        for copy in arrivals[n]:
            copy.wait_recv()
        lax.fori_loop(groups[n] * per, groups[n] * per + per, merge, 0)
        rows = att[pl.ds(pl.multiple_of(groups[n] * GROUP, GROUP), GROUP), :]
        return jnp.dot(rows, w_out[...], preferred_element_type=F32)

    h = GROUP // 2
    part[0] = project(0).astype(BF16)
    f_up = go(remote(part.at[0, pl.ds(0, h)], got_half.at[0], zs.at[0], zr.at[0], z_up))
    f_dn = go(remote(part.at[0, pl.ds(h, h)], got_half.at[1], zs.at[1], zr.at[1], z_dn))
    to_up = project(1)
    part[1, h:] = to_up[h:].astype(BF16)
    f_up.wait_recv()
    part[1, :h] = (to_up[:h] + got_half[0].astype(F32)).astype(BF16)
    s_up = go(remote(part.at[1], got.at[0], zs.at[2], zr.at[2], z_up))
    weights_forward(0)
    to_dn = project(2)
    part[2, :h] = to_dn[:h].astype(BF16)
    f_dn.wait_recv()
    part[2, h:] = (to_dn[h:] + got_half[1].astype(F32)).astype(BF16)
    s_dn = go(remote(part.at[2], got.at[1], zs.at[3], zr.at[3], z_dn))
    mine = project(3) + ent_rows[...].astype(F32)
    weights_forward(1)
    s_up.wait_recv()
    s_dn.wait_recv()
    mixed = mine + got[0].astype(F32) + got[1].astype(F32)
    inner[core] = norm_rows(mixed, gain[...]).astype(BF16)
    to_sib = go(remote(inner.at[core], inner.at[core], ss.at[0], sr.at[0], sib))
    acc[core] = mixed
    acc[1 - core] = jnp.zeros((GROUP, WIDTH), F32)
    for copy in w_local:
        copy.wait()

    def mlp(slot, who):
        w_up = weights[slot, :, :, 0:UNITS].reshape(SIDE * SIDE * UNITS, WIDTH)
        w_down = weights[slot, :, :, UNITS:].reshape(SIDE * SIDE * UNITS, WIDTH)
        hidden = lax.dot_general(
            inner[who], w_up, (((1,), (1,)), ((), ())), preferred_element_type=F32
        )
        acc[who] += jnp.dot(gelu(hidden).astype(BF16), w_down, preferred_element_type=F32)

    def mlp_both(slot):
        def body(t, carry):
            mlp(slot, (core + 1 + t) % 2)
            return carry

        lax.fori_loop(0, 2, body, 0)

    to_sib.wait_recv()
    mlp_both(w_place)
    w_up_copies[2].wait_recv()
    w_up_copies[3].wait_recv()
    mlp_both((w_place + 3) % 4)
    w_dn_copies[0].wait_recv()
    w_dn_copies[1].wait_recv()
    mlp_both((w_place + 1) % 4)
    for copy in w_far:
        copy.wait_recv()
    mlp((w_place + 2) % 4, 1 - core)
    send_sib[...] = acc[1 - core].astype(BF16)
    back = go(remote(send_sib, got_sib, ss.at[1], sr.at[1], sib))
    mlp((w_place + 2) % 4, core)
    back.wait_recv()
    final = (acc[core] + got_sib[...].astype(F32)).astype(BF16)
    for s in range(SIDE):
        res[s] = final[:, s * PART : (s + 1) * PART]
    copies = []
    for n, to in ((2, z_opp), (1, z_up), (3, z_dn)):
        copies.append(go(remote(res.at[(z + n) % 4], landed.at[z], es.at[n], er.at[n], to)))
    result[pl.ds(pl.multiple_of(z * GROUP, GROUP), GROUP), :] = res[z]
    for copy in copies:
        copy.wait_recv()
    for n in range(1, SIDE):
        s = (z + n) % 4
        result[pl.ds(pl.multiple_of(s * GROUP, GROUP), GROUP), :] = landed[s]
    for copy in pending:
        copy.wait_send()


def gelu(v):
    return 0.5 * v * (1.0 + lax.erf(v * 0.7071067811865476))


def merge_call(oa, ob, near_o, near_st, ent_rows, w_out, gain, lines):
    vmem = pl.BlockSpec(memory_space=pltpu.VMEM)
    hbm = pl.BlockSpec(memory_space=pltpu.HBM)
    dma = pltpu.SemaphoreType.DMA
    return pl.pallas_call(
        merge_kernel,
        out_shape=jax.ShapeDtypeStruct((ROWS, PART), BF16),
        in_specs=[hbm] * 6 + [vmem] + [pl.BlockSpec(memory_space=pl.ANY)] * 4,
        out_specs=vmem,
        scratch_shapes=[
            pltpu.VMEM((SIDE, NB, TALL, BLK), BF16),
            pltpu.VMEM((SIDE, NB, TALL, BLK), BF16),
            pltpu.VMEM((2, SIDE, 2, TALL, BLK), BF16),
            pltpu.VMEM((ROWS, 2 * BLK), BF16),
            pltpu.VMEM((3, GROUP, WIDTH), BF16),
            pltpu.VMEM((2, GROUP // 2, WIDTH), BF16),
            pltpu.VMEM((2, GROUP, WIDTH), BF16),
            pltpu.VMEM((SIDE, SIDE, SIDE, 2 * UNITS, WIDTH), BF16),
            pltpu.VMEM((2, GROUP, WIDTH), BF16),
            pltpu.VMEM((2, GROUP, WIDTH), F32),
            pltpu.VMEM((GROUP, WIDTH), BF16),
            pltpu.VMEM((GROUP, WIDTH), BF16),
            pltpu.VMEM((SIDE, GROUP, PART), BF16),
            pltpu.VMEM((SIDE, GROUP, PART), BF16),
            pltpu.VMEM((NB, 2, BLK, BLK), F32),
            pltpu.VMEM((NB, 2, 8, BLK), F32),
            pltpu.VMEM((GROUP, WIDTH), BF16),
            pltpu.VMEM((PART, WIDTH), BF16),
            dma((2, 4, 4)), dma((2, 4, 4)),
            dma((2, 4, 2)), dma((2, 4, 2)),
            dma((4,)), dma((4,)),
            dma((3, 4)), dma((3, 4)), dma((4,)),
            dma((2,)), dma((2,)),
            dma((4,)), dma((4,)),
            dma((8,)),
        ],
        compiler_params=pltpu.CompilerParams(
            collective_id=1, has_side_effects=True, vmem_limit_bytes=50 * MB
        ),
        name="merge_project",
    )(oa, ob, near_o, near_st, ent_rows, w_out, gain, *lines)


def on_device(
    entities, attn_gain, w_qkv, w_out, mlp_gain, w_up, w_down, far_owner, far_local, far_live
):
    xbuf, ybuf, near_o, near_st, ent_rows, key_a, key_b, piece = gather_call(
        entities,
        attn_gain.reshape(1, WIDTH),
        w_qkv,
        jnp.pad(((far_owner * NB + far_local) * 2 + far_live).T, ((0, 4), (0, BLK - NB))),
        w_up,
        w_down,
    )
    def along(by):
        pairs = []
        for i in range(lax.axis_size("loc")):
            y, x, core = i // 8, i // 2 % 4, i % 2
            y, x = (y, (x + by) % 4) if core == 0 else ((y + by) % 4, x)
            pairs.append((i, (y * 4 + x) * 2 + core))
        return lax.ppermute(piece, "loc", pairs)

    lines = [piece] + [along(by) for by in (2, 1, 3)]
    oa, ob = far_call(key_a, key_b, xbuf, ybuf)
    return merge_call(
        oa, ob, near_o, near_st, ent_rows, w_out, mlp_gain.reshape(1, WIDTH), lines
    )


def solution(mesh):
    return jax.shard_map(
        on_device,
        mesh=mesh,
        in_specs=(
            P("loc", "head"),
            P(),
            P(None, None, "head"),
            P("head", None),
            P(),
            P(None, "head"),
            P("head", None),
            P("loc", None),
            P("loc", None),
            P("loc", None),
        ),
        out_specs=P("loc", "head"),
        check_vma=False,
    )
```

```python
import functools

import jax
import jax.numpy as jnp
from jax import lax
from jax.experimental import pallas as pl
from jax.experimental.pallas import tpu as pltpu
from jax.sharding import PartitionSpec as P

MESH = pl.DeviceIdType.MESH
F32 = jnp.float32
BF16 = jnp.bfloat16
BLK = 128
HD = 64
NB = 8
SIDE = 4
CHUNKS = 4
ROWS = NB * BLK
GROUP = ROWS // SIDE
WIDTH = 1024
PART = WIDTH // SIDE
NEG = -1e30
MB = 2**20
TALL = BLK + 16
UNITS = 32


def coords():
    loc = lax.axis_index("loc")
    return loc // 8, (loc // 2) % 4, loc % 2, lax.axis_index("head")


def device(y, x, core, z):
    return ((y % 4 * 4 + x % 4) * 2 + core, z % 4)


def shifted(axis, by):
    y, x, core, z = coords()
    if axis == "y":
        return device(y + by + 4, x, core, z)
    if axis == "x":
        return device(y, x + by + 4, core, z)
    if axis == "z":
        return device(y, x, core, z + by + 4)
    return device(y, x, 1 - core, z)


def loc_shifted(by):
    return ((lax.axis_index("loc") + by + 32) % 32, lax.axis_index("head"))


def greet(peers):
    barrier = pltpu.get_barrier_semaphore()
    for peer in peers:
        pl.semaphore_signal(barrier, inc=1, device_id=peer, device_id_type=MESH)


def greeted(peers):
    pl.semaphore_wait(pltpu.get_barrier_semaphore(), len(peers))


def remote(src, dst, send, recv, to):
    return pltpu.make_async_remote_copy(
        src_ref=src, dst_ref=dst, send_sem=send, recv_sem=recv, device_id=to, device_id_type=MESH
    )


def norm_rows(values, gain):
    center = values - jnp.mean(values, axis=-1, keepdims=True)
    spread = jnp.mean(center * center, axis=-1, keepdims=True)
    return center * lax.rsqrt(spread + 1e-05) * gain


def split_heads(query):
    zero = jnp.zeros((HD, BLK), query.dtype)
    top = jnp.concatenate([query[:HD], zero], axis=1)
    low = jnp.concatenate([zero, query[HD:]], axis=1)
    return jnp.concatenate([top, low], axis=0)


ORDER = (
    ("zs", 0), ("zs", 1), ("ts", 0), ("pp", 0), ("zf", 0), ("zs", 2), ("zf", 1), ("zs", 3),
    ("pr", 0), ("hf", 0), ("zf", 2), ("pr", 1), ("zf", 3), ("ws", 0), ("pf", 0), ("pr", 2),
    ("pf", 1), ("pr", 3), ("hl", 0), ("pf", 2), ("wf", 0), ("pf", 3), ("ro", 0),
    ("pe", 0), ("n", 1), ("n", 2), ("n", 3), ("n", 4), ("n", 5), ("pe", 1), ("n", 6), ("hw", 0),
    ("n", 7), ("n", 0), ("ko", 0), ("pe", 2), ("pe", 3), ("we", 0),
)


def gather_kernel(
    ent_hbm, gain, wqkv_hbm, tab, up_hbm, down_hbm,
    xbuf, ybuf, near_o, near_st, ent_rows, key_a, key_b, wz,
    ent, wqkv, zbuf, xown, yown, halo_low, halo_high, tab_y, tab_x, up_cols, up_rows, piece,
    zs, zr, xs, xr, ys, yr, cs, cr, hs, hr, ls, ts, tr, ws, wr, wl,
):
    y, x, core, z = coords()
    loc = lax.axis_index("loc")
    z_up, z_dn = shifted("z", 1), shifted("z", -1)
    x_up, x_dn = shifted("x", 1), shifted("x", -1)
    y_up, y_dn = shifted("y", 1), shifted("y", -1)
    sib = shifted("c", 0)
    nxt, prv = loc_shifted(1), loc_shifted(-1)
    y_opp, x_opp = shifted("y", 2), shifted("x", 2)
    peers = [z_up, z_dn, x_up, x_dn, y_up, y_dn, sib, nxt, prv, y_opp, x_opp]
    greet(peers)
    load_up = pltpu.make_async_copy(
        up_hbm.at[:, pl.ds(pl.multiple_of(loc // 4 * BLK, BLK), BLK)], up_cols, wl.at[0]
    )
    load_down = pltpu.make_async_copy(
        down_hbm.at[pl.ds(pl.multiple_of(loc * UNITS, UNITS), UNITS)],
        piece.at[pl.ds(UNITS, UNITS)],
        wl.at[1],
    )
    load_ent = pltpu.make_async_copy(ent_hbm, ent, wl.at[4])
    load_qkv = pltpu.make_async_copy(wqkv_hbm, wqkv, wl.at[5])
    load_ent.start()
    load_up.start()
    load_down.start()
    load_qkv.start()
    tab_y[y] = tab[...]
    tab_x[x] = tab[...]
    load_ent.wait()
    greeted(peers)
    rows = ROWS // CHUNKS
    blocks = NB // CHUNKS
    pending = []

    def go(copy):
        copy.start()
        pending.append(copy)
        return copy

    z_near = []

    def z_start(r):
        at = pl.ds(r * rows, rows)
        z_near.append(
            (
                go(remote(ent.at[at], zbuf.at[z, at], zs.at[r, 0], zr.at[r, 0], z_up)),
                go(remote(ent.at[at], zbuf.at[z, at], zs.at[r, 1], zr.at[r, 1], z_dn)),
            )
        )

    tab_copies = []

    def tab_start(_):
        for k, (dst, place, to) in enumerate(
            ((tab_y, y, (y_up, y_dn, y_opp)), (tab_x, x, (x_up, x_dn, x_opp)))
        ):
            for n, peer in enumerate(to):
                tab_copies.append(go(remote(tab, dst.at[place], ts.at[k, n], tr.at[k, n], peer)))

    lines = {}
    place_copies = []

    def weights_start(_):
        load_up.wait()
        load_down.wait()
        up_rows[...] = up_cols[...].astype(F32).T
        piece[0:UNITS] = up_rows[pl.ds(pl.multiple_of(loc % 4 * UNITS, UNITS), UNITS)].astype(BF16)
        lines["z"] = (
            go(remote(piece, wz.at[z], ws.at[0], wr.at[0], z_up)),
            go(remote(piece, wz.at[z], ws.at[1], wr.at[1], z_dn)),
        )
        local = pltpu.make_async_copy(piece, wz.at[z], wl.at[2])
        local.start()
        place_copies.append(local)

    def line_pass(name, buf, place, sem, up, dn, half):
        a, b = lines[name]
        a.wait_recv()
        view = buf.at[(place + 3) % 4, pl.ds(0, half)]
        c = go(remote(view, view, ws.at[sem], wr.at[sem], up))
        b.wait_recv()
        view = buf.at[(place + 1) % 4, pl.ds(half, half)]
        d = go(remote(view, view, ws.at[sem + 1], wr.at[sem + 1], dn))
        lines[name] = (c, d)

    def weights_forward(_):
        line_pass("z", wz, z, 2, z_up, z_dn, UNITS)

    def weights_finish(_):
        for copy in lines["z"]:
            copy.wait_recv()
        place_copies.pop().wait()

    def prepare(_):
        zbuf[z] = ent[...]
        load_qkv.wait()

    z_far = []

    def z_forward(r):
        a, b = z_near[r]
        low = pl.ds(r * rows, rows // 2)
        high = pl.ds(r * rows + rows // 2, rows // 2)
        a.wait_recv()
        s = (z + 3) % 4
        c = go(remote(zbuf.at[s, low], zbuf.at[s, low], zs.at[r, 2], zr.at[r, 2], z_up))
        b.wait_recv()
        s = (z + 1) % 4
        d = go(remote(zbuf.at[s, high], zbuf.at[s, high], zs.at[r, 3], zr.at[r, 3], z_dn))
        z_far.append((c, d))

    plane = {}
    core_copies = []
    local_copies = []

    def to_sibling(buf, place, blks, sem, src=None):
        view = buf.at[core, place, blks, pl.ds(0, 2)]
        core_copies.append(go(remote(view if src is None else src, view, cs.at[sem], cr.at[sem], sib)))

    def project(r):
        for copy in z_far[r]:
            copy.wait_recv()
        at = pl.ds(r * rows, rows)
        full = jnp.concatenate([zbuf[s, at, :] for s in range(SIDE)], axis=1).astype(F32)
        normed = norm_rows(full, gain[...]).astype(BF16)
        queries = jnp.dot(normed, wqkv[0], preferred_element_type=F32)
        keys = jnp.dot(normed, wqkv[1], preferred_element_type=F32).astype(BF16)
        values = jnp.dot(normed, wqkv[2], preferred_element_type=F32)
        q_t = (queries.T.astype(BF16).astype(F32) * 0.125).astype(BF16)
        v_t = values.T.astype(BF16)
        for i in range(blocks):
            b = r * blocks + i
            cut = slice(i * BLK, (i + 1) * BLK)
            xown[b, 0] = keys[cut, :BLK]
            yown[b, 0] = keys[cut, BLK:]
            xown[b, 1] = v_t[:BLK, cut]
            yown[b, 1] = v_t[BLK:, cut]
            yown[b, 2] = q_t[:BLK, cut]
            xown[b, 2] = q_t[BLK:, cut]
        blks = pl.ds(r * blocks, blocks)
        for name, own, buf, place, send, recv, up, dn, k in (
            ("x", xown, xbuf, x, xs, xr, x_up, x_dn, 0),
            ("y", yown, ybuf, y, ys, yr, y_up, y_dn, 1),
        ):
            src, dst = own.at[blks], buf.at[core, place, blks]
            plane[name, r] = (
                go(remote(src, dst, send.at[r, 0], recv.at[r, 0], up)),
                go(remote(src, dst, send.at[r, 1], recv.at[r, 1], dn)),
            )
            local = pltpu.make_async_copy(src, dst, ls.at[r * 2 + k])
            local.start()
            local_copies.append(local)
            to_sibling(buf, place, blks, r * 10 + k * 5, own.at[blks, pl.ds(0, 2)])

    def plane_forward(r):
        blks = pl.ds(r * blocks, blocks)
        low = pl.ds(r * blocks, blocks // 2)
        high = pl.ds(r * blocks + blocks // 2, blocks // 2)
        for name, buf, place, send, recv, up, dn, k in (
            ("x", xbuf, x, xs, xr, x_up, x_dn, 0),
            ("y", ybuf, y, ys, yr, y_up, y_dn, 1),
        ):
            a, b = plane[name, r]
            a.wait_recv()
            s = (place + 3) % 4
            view = buf.at[core, s, low]
            c = go(remote(view, view, send.at[r, 2], recv.at[r, 2], up))
            to_sibling(buf, s, blks, r * 10 + k * 5 + 1)
            b.wait_recv()
            s = (place + 1) % 4
            view = buf.at[core, s, high]
            d = go(remote(view, view, send.at[r, 3], recv.at[r, 3], dn))
            to_sibling(buf, s, blks, r * 10 + k * 5 + 2)
            plane[name, r] = (c, d)

    def plane_finish(r):
        low = pl.ds(r * blocks, blocks // 2)
        high = pl.ds(r * blocks + blocks // 2, blocks // 2)
        for name, buf, place, k in (("x", xbuf, x, 0), ("y", ybuf, y, 1)):
            c, d = plane[name, r]
            s = (place + 2) % 4
            c.wait_recv()
            to_sibling(buf, s, low, r * 10 + k * 5 + 3)
            d.wait_recv()
            to_sibling(buf, s, high, r * 10 + k * 5 + 4)

    def near(b):
        for p, (own, other) in enumerate(((xown, yown), (yown, xown))):
            query = split_heads(other[b, 2])
            parts = []
            for step in (-1, 0, 1):
                if b + step < 0:
                    key, val, ok = halo_low[p, 0], halo_low[p, 1], loc > 0
                elif b + step >= NB:
                    key, val, ok = halo_high[p, 0], halo_high[p, 1], loc < 31
                else:
                    key, val, ok = own[b + step, 0], own[b + step, 1], None
                score = jnp.dot(key, query, preferred_element_type=F32)
                if ok is not None:
                    score = jnp.where(ok, score, NEG)
                parts.append((score, val))
            top = functools.reduce(
                jnp.maximum, [jnp.max(score, axis=0, keepdims=True) for score, _ in parts]
            )
            total = jnp.zeros((1, 2 * BLK), F32)
            out = jnp.zeros((BLK, 2 * BLK), F32)
            for score, val in parts:
                weight = jnp.exp(score - top)
                total = total + jnp.sum(weight, axis=0, keepdims=True)
                out = out + jnp.dot(val, weight.astype(BF16), preferred_element_type=F32)
            near_o[b, p] = jnp.concatenate(
                [out[:HD, :BLK] / total[:, :BLK], out[HD:, BLK:] / total[:, BLK:]], axis=0
            )
            near_st[b, p, 0:1] = top[:, :BLK]
            near_st[b, p, 1:2] = top[:, BLK:]
            near_st[b, p, 2:3] = total[:, :BLK]
            near_st[b, p, 3:4] = total[:, BLK:]
            near_st[b, p, 4:8] = jnp.zeros((4, BLK), F32)

    halos = []

    def halo_first(_):
        for p, own in enumerate((xown, yown)):
            halos.append(go(remote(own.at[0, pl.ds(0, 2)], halo_high.at[p], hs.at[p], hr.at[p], prv)))

    def halo_last(_):
        for p, own in enumerate((xown, yown)):
            src = own.at[NB - 1, pl.ds(0, 2)]
            halos.append(go(remote(src, halo_low.at[p], hs.at[2 + p], hr.at[2 + p], nxt)))

    def halo_wait(_):
        for copy in halos:
            copy.wait_recv()

    def rows_out(_):
        mine = pl.ds(pl.multiple_of(z * GROUP, GROUP), GROUP)
        ent_rows[...] = jnp.concatenate([zbuf[s, mine, :] for s in range(SIDE)], axis=1)

    def keys_out(_):
        for copy in tab_copies:
            copy.wait_recv()
        code = jnp.concatenate([tab_y[s][:, :NB] for s in range(SIDE)], axis=1)
        at_key = code // 16 % 2 * 32 + code // 32 % 4 * NB + code // 2 % NB
        key_a[...] = jnp.where((code % 2 == 1) & (code // 128 == y), at_key, -1)
        code = jnp.concatenate([tab_x[s][:, :NB] for s in range(SIDE)], axis=1)
        at_key = code // 16 % 2 * 32 + code // 128 * NB + code // 2 % NB
        key_b[...] = jnp.where((code % 2 == 1) & (code // 32 % 4 == x), at_key, -1)

    steps = {
        "zs": z_start, "zf": z_forward, "pr": project, "pf": plane_forward, "pe": plane_finish,
        "n": near, "ts": tab_start, "ws": weights_start, "wf": weights_forward, "we": weights_finish,
        "hf": halo_first, "hl": halo_last, "hw": halo_wait,
        "ro": rows_out, "ko": keys_out, "pp": prepare,
    }
    for name, place in ORDER:
        steps[name](place)
    for copy in core_copies:
        copy.wait_recv()
    for copy in local_copies:
        copy.wait()
    for copy in pending:
        copy.wait_send()


def gather_call(ent, gain, wqkv, tab, w_up, w_down):
    vmem = pl.BlockSpec(memory_space=pltpu.VMEM)
    hbm = pl.BlockSpec(memory_space=pl.ANY)
    pinned = pl.BlockSpec(memory_space=pltpu.HBM)
    dma = pltpu.SemaphoreType.DMA
    plane_shape = (2, SIDE, NB, 3, BLK, BLK)
    return pl.pallas_call(
        gather_kernel,
        out_shape=(
            jax.ShapeDtypeStruct(plane_shape, BF16),
            jax.ShapeDtypeStruct(plane_shape, BF16),
            jax.ShapeDtypeStruct((NB, 2, BLK, BLK), F32),
            jax.ShapeDtypeStruct((NB, 2, 8, BLK), F32),
            jax.ShapeDtypeStruct((GROUP, WIDTH), BF16),
            jax.ShapeDtypeStruct((8, SIDE * NB), jnp.int32),
            jax.ShapeDtypeStruct((8, SIDE * NB), jnp.int32),
            jax.ShapeDtypeStruct((SIDE, 2 * UNITS, WIDTH), BF16),
        ),
        in_specs=[pinned, vmem, pinned, vmem, pinned, pinned],
        out_specs=(hbm, hbm) + (vmem,) * 5 + (hbm,),
        scratch_shapes=[
            pltpu.VMEM((ROWS, PART), BF16),
            pltpu.VMEM((3, WIDTH, PART), BF16),
            pltpu.VMEM((SIDE, ROWS, PART), BF16),
            pltpu.VMEM((NB, 3, BLK, BLK), BF16),
            pltpu.VMEM((NB, 3, BLK, BLK), BF16),
            pltpu.VMEM((2, 2, BLK, BLK), BF16),
            pltpu.VMEM((2, 2, BLK, BLK), BF16),
            pltpu.VMEM((SIDE, NB, BLK), jnp.int32),
            pltpu.VMEM((SIDE, NB, BLK), jnp.int32),
            pltpu.VMEM((WIDTH, BLK), BF16),
            pltpu.VMEM((BLK, WIDTH), F32),
            pltpu.VMEM((2 * UNITS, WIDTH), BF16),
            dma((CHUNKS, 4)), dma((CHUNKS, 4)),
            dma((CHUNKS, 4)), dma((CHUNKS, 4)),
            dma((CHUNKS, 4)), dma((CHUNKS, 4)),
            dma((CHUNKS * 10,)), dma((CHUNKS * 10,)),
            dma((4,)), dma((4,)),
            dma((CHUNKS * 2,)),
            dma((2, 3)), dma((2, 3)),
            dma((8,)), dma((8,)),
            dma((6,)),
        ],
        compiler_params=pltpu.CompilerParams(
            collective_id=0, has_side_effects=True, vmem_limit_bytes=60 * MB
        ),
        name="gather_project",
    )(ent, gain, wqkv, tab, w_up, w_down)


def far_kernel(
    key_a, key_b, x_hbm, y_hbm, oa, ob, query, pairs, acc, state, hits_a, hits_b, qs, ks
):
    core = lax.axis_index("loc") % 2
    live_q = SIDE * NB
    mine = pl.ds(core * live_q, live_q)
    loads = []
    for pair, (keys_hbm, query_hbm) in enumerate(((x_hbm, y_hbm), (y_hbm, x_hbm))):
        loads.append(
            (
                pltpu.make_async_copy(query_hbm.at[mine, 2], query.at[pair], qs.at[pair]),
                pltpu.make_async_copy(keys_hbm.at[:, pl.ds(0, 2)], pairs.at[pair], ks.at[pair]),
            )
        )
    for pair in loads:
        for load in pair:
            load.start()

    def find(s, counts):
        counts = list(counts)
        for b in range(NB):
            for j in range(4):
                for pair, (keys, hits) in enumerate(((key_a, hits_a), (key_b, hits_b))):
                    key = keys[j, s * NB + b]
                    hits[counts[pair]] = (s * NB + b) * 1024 + key
                    counts[pair] = counts[pair] + jnp.where(key >= 0, 1, 0)
        return tuple(counts)

    counts = lax.fori_loop(0, SIDE, find, (0, 0))
    for hits, count in zip((hits_a, hits_b), counts):
        for extra in range(8):
            hits[count + extra] = live_q * 1024

    def clear(i, carry):
        acc[i] = jnp.zeros((BLK, BLK), F32)
        state[i, 0:2] = jnp.full((2, BLK), NEG, F32)
        state[i, 2:8] = jnp.zeros((6, BLK), F32)
        return carry

    lax.fori_loop(0, 2 * (live_q + 1), clear, 0)

    for pair in range(2):
        hits, count = (hits_a, counts[0]) if pair == 0 else (hits_b, counts[1])
        o_ref = oa if pair == 0 else ob
        base = pair * (live_q + 1)
        for load in loads[pair]:
            load.wait()

        def eight(step, carry):
            work = []
            for u in range(8):
                code = hits[step * 8 + u]
                q, k = lax.shift_right_logical(code, 10), code & 1023
                asked = split_heads(query[pair, jnp.minimum(q, live_q - 1)])
                key = pairs[pair, k, 0]
                val = pairs[pair, k, 1]
                score = jnp.dot(key, asked, preferred_element_type=F32)
                top = jnp.max(score, axis=0, keepdims=True)
                weight = jnp.exp(score - top)
                total = jnp.sum(weight, axis=0, keepdims=True)
                out = jnp.dot(val, weight.astype(BF16), preferred_element_type=F32)
                work.append((q + base, top, total, out))
            for q, top, total, out in work:
                for h in range(2):
                    cut = slice(h * BLK, (h + 1) * BLK)
                    feat = pl.ds(h * HD, HD)
                    old_top = state[q, h : h + 1]
                    new_top = jnp.maximum(old_top, top[:, cut])
                    keep = jnp.exp(old_top - new_top)
                    add = jnp.exp(top[:, cut] - new_top)
                    acc[q, feat] = acc[q, feat] * keep + out[h * HD : (h + 1) * HD, cut] * add
                    state[q, h : h + 1] = new_top
                    state[q, 2 + h : 3 + h] = state[q, 2 + h : 3 + h] * keep + total[:, cut] * add
            return carry

        lax.fori_loop(0, lax.shift_right_logical(count + 7, 3), eight, 0)

        def finish(i, carry):
            st = state[base + i]
            left, terms = st[0:4], []
            for _ in range(3):
                terms.append(left.astype(BF16).astype(F32))
                left = left - terms[-1]
            terms.append(jnp.zeros((4, BLK), F32))
            o_ref[i, BLK:] = jnp.concatenate(terms, axis=0).astype(BF16)
            for h in range(2):
                total = st[2 + h : 3 + h]
                scale = 1.0 / jnp.where(total > 0, total, 1.0)
                feat = pl.ds(h * HD, HD)
                o_ref[i, feat] = (acc[base + i, feat] * scale).astype(BF16)
            return carry

        lax.fori_loop(0, live_q, finish, 0)


def far_call(key_a, key_b, xbuf, ybuf):
    vmem = pl.BlockSpec(memory_space=pltpu.VMEM)
    smem = pl.BlockSpec(memory_space=pltpu.SMEM)
    hbm = pl.BlockSpec(memory_space=pltpu.HBM)
    dma = pltpu.SemaphoreType.DMA
    live_q = SIDE * NB
    o_shape = jax.ShapeDtypeStruct((live_q, TALL, BLK), BF16)
    flat = (2 * live_q, 3, BLK, BLK)
    oa, ob = pl.pallas_call(
        far_kernel,
        out_shape=(o_shape, o_shape),
        in_specs=[smem, smem, hbm, hbm],
        out_specs=(vmem, vmem),
        scratch_shapes=[
            pltpu.VMEM((2, live_q, BLK, BLK), BF16),
            pltpu.VMEM((2, 2 * live_q, 2, BLK, BLK), BF16),
            pltpu.VMEM((2 * (live_q + 1), BLK, BLK), F32),
            pltpu.VMEM((2 * (live_q + 1), 8, BLK), F32),
            pltpu.SMEM((live_q * 4 + 8,), jnp.int32),
            pltpu.SMEM((live_q * 4 + 8,), jnp.int32),
            dma((2,)),
            dma((2,)),
        ],
        compiler_params=pltpu.CompilerParams(vmem_limit_bytes=58 * MB),
        cost_estimate=pl.CostEstimate(
            flops=8 * 10**9, bytes_accessed=30 * MB, transcendentals=3 * 10**6
        ),
        name="far_partials",
    )(key_a, key_b, xbuf.reshape(flat), ybuf.reshape(flat))
    shape = (SIDE, NB, TALL, BLK)
    return oa.reshape(shape), ob.reshape(shape)


def merge_kernel(
    oa, ob, near_o_hbm, near_st_hbm, ent_rows_hbm, w_out_hbm, gain, line_0, line_1, line_2, line_3, result,
    ra, rb, relay, att, part, got_half, got,
    weights, inner, acc, send_sib, got_sib, res, landed, near_o, near_st, ent_rows, w_out,
    os, orr, fs, fr, zs, zr, ws, wr, wl, ss, sr, es, er, ls,
):
    y, x, core, z = coords()
    z_up, z_dn = shifted("z", 1), shifted("z", -1)
    z_opp, sib = shifted("z", 2), shifted("c", 0)
    peers = [shifted("y", 1), shifted("y", -1), shifted("x", 1), shifted("x", -1), z_up, z_dn]
    w_place = y * (1 - core) + x * core
    w_up_to = device(y + 1 - core, x + core, core, z)
    w_dn_to = device(y + 3 * (1 - core), x + 3 * core, core, z)
    peers = peers + [z_opp, sib]
    greet(peers)
    loads = [
        pltpu.make_async_copy(src, dst, ls.at[n])
        for n, (src, dst) in enumerate(
            (
                (oa.at[y], ra.at[y]),
                (ob.at[x], rb.at[x]),
                (near_o_hbm, near_o),
                (near_st_hbm, near_st),
                (w_out_hbm, w_out),
                (ent_rows_hbm, ent_rows),
            )
        )
    ]
    for load in loads:
        load.start()
    line = (line_0, line_1, line_2, line_3)
    w_local = [
        pltpu.make_async_copy(line[n], weights.at[w_place, n], wl.at[n]) for n in range(SIDE)
    ]
    for copy in w_local:
        copy.start()
    greeted(peers)
    pending = []

    def go(copy):
        copy.start()
        pending.append(copy)
        return copy

    groups = [(z + by) % 4 for by in (2, 1, 3, 0)]
    per = NB // SIDE
    lanes = ((y, peers[0], peers[1], oa, ra), (x, peers[2], peers[3], ob, rb))
    relays, arrivals = {}, {}
    for n, g in enumerate(groups):
        arrivals[n] = []
        for k, (place, up, dn, o, ro) in enumerate(lanes):
            send, recv = os.at[k, n], orr.at[k, n]
            far_to, up_to, dn_to = (place + 2) % 4, (place + 1) % 4, (place + 3) % 4
            relays[k, n] = (
                go(remote(o.at[far_to, g * per], relay.at[k, n, 0], send.at[0], recv.at[0], up)),
                go(remote(o.at[far_to, g * per + 1], relay.at[k, n, 1], send.at[1], recv.at[1], dn)),
            )
            both = pl.ds(g * per, per)
            arrivals[n] += [
                go(remote(o.at[up_to, both], ro.at[place, both], send.at[2], recv.at[2], up)),
                go(remote(o.at[dn_to, both], ro.at[place, both], send.at[3], recv.at[3], dn)),
            ]

    def pass_on(n):
        g = groups[n]
        for k, (place, up, dn, o, ro) in enumerate(lanes):
            a, b = relays[k, n]
            a.wait_recv()
            dst = ro.at[(place + 3) % 4, g * per]
            arrivals[n].append(go(remote(relay.at[k, n, 0], dst, fs.at[k, n, 0], fr.at[k, n, 0], up)))
            b.wait_recv()
            dst = ro.at[(place + 1) % 4, g * per + 1]
            arrivals[n].append(go(remote(relay.at[k, n, 1], dst, fs.at[k, n, 1], fr.at[k, n, 1], dn)))

    pass_on(0)
    pass_on(1)
    w_up_copies, w_dn_copies = [None] * 4, [None] * 4

    def weights_start():
        for n in range(SIDE):
            u, d = n, (n + 2) % 4
            dst = weights.at[w_place]
            w_up_copies[u] = go(remote(line[u], dst.at[u], ws.at[0, u], wr.at[0, u], w_up_to))
            w_dn_copies[d] = go(remote(line[d], dst.at[d], ws.at[1, d], wr.at[1, d], w_dn_to))

    pass_on(2)
    pass_on(3)
    weights_start()
    w_far = []

    def weights_forward(n):
        w_up_copies[n].wait_recv()
        view = weights.at[(w_place + 3) % 4, n]
        w_far.append(go(remote(view, view, ws.at[2, n], wr.at[2, n], w_up_to)))
        w_dn_copies[n + 2].wait_recv()
        view = weights.at[(w_place + 1) % 4, n + 2]
        w_far.append(go(remote(view, view, ws.at[2, n + 2], wr.at[2, n + 2], w_dn_to)))

    for load in loads:
        load.wait()

    def merge(b, carry):
        for p, ro in enumerate((ra, rb)):
            stats, outs = [near_st[b, p]], [near_o[b, p]]
            for s in range(SIDE):
                tail = ro[s, b, BLK:].astype(F32)
                stats.append(tail[0:4] + tail[4:8] + tail[8:12])
                outs.append(ro[s, b, :BLK].astype(F32))
            halves = []
            for h in range(2):
                top = functools.reduce(jnp.maximum, [st[h : h + 1] for st in stats])
                scale = [st[2 + h : 3 + h] * jnp.exp(st[h : h + 1] - top) for st in stats]
                inv = 1.0 / functools.reduce(jnp.add, scale)
                halves.append(
                    functools.reduce(
                        jnp.add,
                        [o[h * HD : (h + 1) * HD] * (w * inv) for o, w in zip(outs, scale)],
                    )
                )
            tile = jnp.concatenate(halves, axis=0).T.astype(BF16)
            att[pl.ds(pl.multiple_of(b * BLK, BLK), BLK), p * BLK : (p + 1) * BLK] = tile
        return carry

    def project(n):
        for copy in arrivals[n]:
            copy.wait_recv()
        lax.fori_loop(groups[n] * per, groups[n] * per + per, merge, 0)
        rows = att[pl.ds(pl.multiple_of(groups[n] * GROUP, GROUP), GROUP), :]
        return jnp.dot(rows, w_out[...], preferred_element_type=F32)

    h = GROUP // 2
    part[0] = project(0).astype(BF16)
    f_up = go(remote(part.at[0, pl.ds(0, h)], got_half.at[0], zs.at[0], zr.at[0], z_up))
    f_dn = go(remote(part.at[0, pl.ds(h, h)], got_half.at[1], zs.at[1], zr.at[1], z_dn))
    to_up = project(1)
    part[1, h:] = to_up[h:].astype(BF16)
    f_up.wait_recv()
    part[1, :h] = (to_up[:h] + got_half[0].astype(F32)).astype(BF16)
    s_up = go(remote(part.at[1], got.at[0], zs.at[2], zr.at[2], z_up))
    weights_forward(0)
    to_dn = project(2)
    part[2, :h] = to_dn[:h].astype(BF16)
    f_dn.wait_recv()
    part[2, h:] = (to_dn[h:] + got_half[1].astype(F32)).astype(BF16)
    s_dn = go(remote(part.at[2], got.at[1], zs.at[3], zr.at[3], z_dn))
    mine = project(3) + ent_rows[...].astype(F32)
    weights_forward(1)
    s_up.wait_recv()
    s_dn.wait_recv()
    mixed = mine + got[0].astype(F32) + got[1].astype(F32)
    inner[core] = norm_rows(mixed, gain[...]).astype(BF16)
    to_sib = go(remote(inner.at[core], inner.at[core], ss.at[0], sr.at[0], sib))
    acc[core] = mixed
    acc[1 - core] = jnp.zeros((GROUP, WIDTH), F32)
    for copy in w_local:
        copy.wait()

    def mlp(slot, who):
        w_up = weights[slot, :, :, 0:UNITS].reshape(SIDE * SIDE * UNITS, WIDTH)
        w_down = weights[slot, :, :, UNITS:].reshape(SIDE * SIDE * UNITS, WIDTH)
        hidden = lax.dot_general(
            inner[who], w_up, (((1,), (1,)), ((), ())), preferred_element_type=F32
        )
        acc[who] += jnp.dot(gelu(hidden).astype(BF16), w_down, preferred_element_type=F32)

    def mlp_both(slot):
        def body(t, carry):
            mlp(slot, (core + 1 + t) % 2)
            return carry

        lax.fori_loop(0, 2, body, 0)

    to_sib.wait_recv()
    mlp_both(w_place)
    w_up_copies[2].wait_recv()
    w_up_copies[3].wait_recv()
    mlp_both((w_place + 3) % 4)
    w_dn_copies[0].wait_recv()
    w_dn_copies[1].wait_recv()
    mlp_both((w_place + 1) % 4)
    for copy in w_far:
        copy.wait_recv()
    mlp((w_place + 2) % 4, 1 - core)
    send_sib[...] = acc[1 - core].astype(BF16)
    back = go(remote(send_sib, got_sib, ss.at[1], sr.at[1], sib))
    mlp((w_place + 2) % 4, core)
    back.wait_recv()
    final = (acc[core] + got_sib[...].astype(F32)).astype(BF16)
    for s in range(SIDE):
        res[s] = final[:, s * PART : (s + 1) * PART]
    copies = []
    for n, to in ((2, z_opp), (1, z_up), (3, z_dn)):
        copies.append(go(remote(res.at[(z + n) % 4], landed.at[z], es.at[n], er.at[n], to)))
    result[pl.ds(pl.multiple_of(z * GROUP, GROUP), GROUP), :] = res[z]
    for copy in copies:
        copy.wait_recv()
    for n in range(1, SIDE):
        s = (z + n) % 4
        result[pl.ds(pl.multiple_of(s * GROUP, GROUP), GROUP), :] = landed[s]
    for copy in pending:
        copy.wait_send()


def gelu(v):
    return 0.5 * v * (1.0 + lax.erf(v * 0.7071067811865476))


def merge_call(oa, ob, near_o, near_st, ent_rows, w_out, gain, lines):
    vmem = pl.BlockSpec(memory_space=pltpu.VMEM)
    hbm = pl.BlockSpec(memory_space=pltpu.HBM)
    dma = pltpu.SemaphoreType.DMA
    return pl.pallas_call(
        merge_kernel,
        out_shape=jax.ShapeDtypeStruct((ROWS, PART), BF16),
        in_specs=[hbm] * 6 + [vmem] + [pl.BlockSpec(memory_space=pl.ANY)] * 4,
        out_specs=vmem,
        scratch_shapes=[
            pltpu.VMEM((SIDE, NB, TALL, BLK), BF16),
            pltpu.VMEM((SIDE, NB, TALL, BLK), BF16),
            pltpu.VMEM((2, SIDE, 2, TALL, BLK), BF16),
            pltpu.VMEM((ROWS, 2 * BLK), BF16),
            pltpu.VMEM((3, GROUP, WIDTH), BF16),
            pltpu.VMEM((2, GROUP // 2, WIDTH), BF16),
            pltpu.VMEM((2, GROUP, WIDTH), BF16),
            pltpu.VMEM((SIDE, SIDE, SIDE, 2 * UNITS, WIDTH), BF16),
            pltpu.VMEM((2, GROUP, WIDTH), BF16),
            pltpu.VMEM((2, GROUP, WIDTH), F32),
            pltpu.VMEM((GROUP, WIDTH), BF16),
            pltpu.VMEM((GROUP, WIDTH), BF16),
            pltpu.VMEM((SIDE, GROUP, PART), BF16),
            pltpu.VMEM((SIDE, GROUP, PART), BF16),
            pltpu.VMEM((NB, 2, BLK, BLK), F32),
            pltpu.VMEM((NB, 2, 8, BLK), F32),
            pltpu.VMEM((GROUP, WIDTH), BF16),
            pltpu.VMEM((PART, WIDTH), BF16),
            dma((2, 4, 4)), dma((2, 4, 4)),
            dma((2, 4, 2)), dma((2, 4, 2)),
            dma((4,)), dma((4,)),
            dma((3, 4)), dma((3, 4)), dma((4,)),
            dma((2,)), dma((2,)),
            dma((4,)), dma((4,)),
            dma((8,)),
        ],
        compiler_params=pltpu.CompilerParams(
            collective_id=1, has_side_effects=True, vmem_limit_bytes=50 * MB
        ),
        name="merge_project",
    )(oa, ob, near_o, near_st, ent_rows, w_out, gain, *lines)


def on_device(
    entities, attn_gain, w_qkv, w_out, mlp_gain, w_up, w_down, far_owner, far_local, far_live
):
    xbuf, ybuf, near_o, near_st, ent_rows, key_a, key_b, piece = gather_call(
        entities,
        attn_gain.reshape(1, WIDTH),
        w_qkv,
        jnp.pad(((far_owner * NB + far_local) * 2 + far_live).T, ((0, 4), (0, BLK - NB))),
        w_up,
        w_down,
    )
    def along(by):
        pairs = []
        for i in range(lax.axis_size("loc")):
            y, x, core = i // 8, i // 2 % 4, i % 2
            y, x = (y, (x + by) % 4) if core == 0 else ((y + by) % 4, x)
            pairs.append((i, (y * 4 + x) * 2 + core))
        return lax.ppermute(piece, "loc", pairs)

    lines = [piece] + [along(by) for by in (3, 1, 2)]
    oa, ob = far_call(key_a, key_b, xbuf, ybuf)
    return merge_call(
        oa, ob, near_o, near_st, ent_rows, w_out, mlp_gain.reshape(1, WIDTH), lines
    )


def solution(mesh):
    return jax.shard_map(
        on_device,
        mesh=mesh,
        in_specs=(
            P("loc", "head"),
            P(),
            P(None, None, "head"),
            P("head", None),
            P(),
            P(None, "head"),
            P("head", None),
            P("loc", None),
            P("loc", None),
            P("loc", None),
        ),
        out_specs=P("loc", "head"),
        check_vma=False,
    )
```

```python
import functools

import jax
import jax.numpy as jnp
from jax import lax
from jax.experimental import pallas as pl
from jax.experimental.pallas import tpu as pltpu
from jax.sharding import PartitionSpec as P

MESH = pl.DeviceIdType.MESH
F32 = jnp.float32
BF16 = jnp.bfloat16
BLK = 128
HD = 64
NB = 8
SIDE = 4
CHUNKS = 4
ROWS = NB * BLK
GROUP = ROWS // SIDE
WIDTH = 1024
PART = WIDTH // SIDE
NEG = -1e30
MB = 2**20
TALL = BLK + 16
UNITS = 32


def coords():
    loc = lax.axis_index("loc")
    return loc // 8, (loc // 2) % 4, loc % 2, lax.axis_index("head")


def device(y, x, core, z):
    return ((y % 4 * 4 + x % 4) * 2 + core, z % 4)


def shifted(axis, by):
    y, x, core, z = coords()
    if axis == "y":
        return device(y + by + 4, x, core, z)
    if axis == "x":
        return device(y, x + by + 4, core, z)
    if axis == "z":
        return device(y, x, core, z + by + 4)
    return device(y, x, 1 - core, z)


def loc_shifted(by):
    return ((lax.axis_index("loc") + by + 32) % 32, lax.axis_index("head"))


def greet(peers):
    barrier = pltpu.get_barrier_semaphore()
    for peer in peers:
        pl.semaphore_signal(barrier, inc=1, device_id=peer, device_id_type=MESH)


def greeted(peers):
    pl.semaphore_wait(pltpu.get_barrier_semaphore(), len(peers))


def remote(src, dst, send, recv, to):
    return pltpu.make_async_remote_copy(
        src_ref=src, dst_ref=dst, send_sem=send, recv_sem=recv, device_id=to, device_id_type=MESH
    )


def norm_rows(values, gain):
    center = values - jnp.mean(values, axis=-1, keepdims=True)
    spread = jnp.mean(center * center, axis=-1, keepdims=True)
    return center * lax.rsqrt(spread + 1e-05) * gain


def split_heads(query):
    zero = jnp.zeros((HD, BLK), query.dtype)
    top = jnp.concatenate([query[:HD], zero], axis=1)
    low = jnp.concatenate([zero, query[HD:]], axis=1)
    return jnp.concatenate([top, low], axis=0)


ORDER = (
    ("zs", 0), ("zs", 1), ("ts", 0), ("pp", 0), ("zf", 0), ("zs", 2), ("zf", 1), ("zs", 3),
    ("pr", 0), ("hf", 0), ("zf", 2), ("pr", 1), ("zf", 3), ("ws", 0), ("pf", 0), ("pr", 2),
    ("pf", 1), ("pr", 3), ("hl", 0), ("pf", 2), ("wf", 0), ("pf", 3), ("ro", 0),
    ("pe", 0), ("n", 1), ("n", 2), ("n", 3), ("n", 4), ("n", 5), ("pe", 1), ("n", 6), ("hw", 0),
    ("n", 7), ("n", 0), ("ko", 0), ("pe", 2), ("pe", 3), ("we", 0),
)


def gather_kernel(
    ent_hbm, gain, wqkv_hbm, tab, up_hbm, down_hbm,
    xbuf, ybuf, near_o, near_st, ent_rows, key_a, key_b, wz,
    ent, wqkv, zbuf, xown, yown, halo_low, halo_high, tab_y, tab_x, up_cols, up_rows, piece,
    zs, zr, xs, xr, ys, yr, cs, cr, hs, hr, ls, ts, tr, ws, wr, wl,
):
    y, x, core, z = coords()
    loc = lax.axis_index("loc")
    z_up, z_dn = shifted("z", 1), shifted("z", -1)
    x_up, x_dn = shifted("x", 1), shifted("x", -1)
    y_up, y_dn = shifted("y", 1), shifted("y", -1)
    sib = shifted("c", 0)
    nxt, prv = loc_shifted(1), loc_shifted(-1)
    y_opp, x_opp = shifted("y", 2), shifted("x", 2)
    peers = [z_up, z_dn, x_up, x_dn, y_up, y_dn, sib, nxt, prv, y_opp, x_opp]
    greet(peers)
    load_up = pltpu.make_async_copy(
        up_hbm.at[:, pl.ds(pl.multiple_of(loc // 4 * BLK, BLK), BLK)], up_cols, wl.at[0]
    )
    load_down = pltpu.make_async_copy(
        down_hbm.at[pl.ds(pl.multiple_of(loc * UNITS, UNITS), UNITS)],
        piece.at[pl.ds(UNITS, UNITS)],
        wl.at[1],
    )
    load_ent = pltpu.make_async_copy(ent_hbm, ent, wl.at[4])
    load_qkv = pltpu.make_async_copy(wqkv_hbm, wqkv, wl.at[5])
    load_ent.start()
    load_up.start()
    load_down.start()
    load_qkv.start()
    tab_y[y] = tab[...]
    tab_x[x] = tab[...]
    load_ent.wait()
    greeted(peers)
    rows = ROWS // CHUNKS
    blocks = NB // CHUNKS
    pending = []

    def go(copy):
        copy.start()
        pending.append(copy)
        return copy

    z_near = []

    def z_start(r):
        at = pl.ds(r * rows, rows)
        z_near.append(
            (
                go(remote(ent.at[at], zbuf.at[z, at], zs.at[r, 0], zr.at[r, 0], z_up)),
                go(remote(ent.at[at], zbuf.at[z, at], zs.at[r, 1], zr.at[r, 1], z_dn)),
            )
        )

    tab_copies = []

    def tab_start(_):
        for k, (dst, place, to) in enumerate(
            ((tab_y, y, (y_up, y_dn, y_opp)), (tab_x, x, (x_up, x_dn, x_opp)))
        ):
            for n, peer in enumerate(to):
                tab_copies.append(go(remote(tab, dst.at[place], ts.at[k, n], tr.at[k, n], peer)))

    lines = {}
    place_copies = []

    def weights_start(_):
        load_up.wait()
        load_down.wait()
        up_rows[...] = up_cols[...].astype(F32).T
        piece[0:UNITS] = up_rows[pl.ds(pl.multiple_of(loc % 4 * UNITS, UNITS), UNITS)].astype(BF16)
        lines["z"] = (
            go(remote(piece, wz.at[z], ws.at[0], wr.at[0], z_up)),
            go(remote(piece, wz.at[z], ws.at[1], wr.at[1], z_dn)),
        )
        local = pltpu.make_async_copy(piece, wz.at[z], wl.at[2])
        local.start()
        place_copies.append(local)

    def line_pass(name, buf, place, sem, up, dn, half):
        a, b = lines[name]
        a.wait_recv()
        view = buf.at[(place + 3) % 4, pl.ds(0, half)]
        c = go(remote(view, view, ws.at[sem], wr.at[sem], up))
        b.wait_recv()
        view = buf.at[(place + 1) % 4, pl.ds(half, half)]
        d = go(remote(view, view, ws.at[sem + 1], wr.at[sem + 1], dn))
        lines[name] = (c, d)

    def weights_forward(_):
        line_pass("z", wz, z, 2, z_up, z_dn, UNITS)

    def weights_finish(_):
        for copy in lines["z"]:
            copy.wait_recv()
        place_copies.pop().wait()

    def prepare(_):
        zbuf[z] = ent[...]
        load_qkv.wait()

    z_far = []

    def z_forward(r):
        a, b = z_near[r]
        low = pl.ds(r * rows, rows // 2)
        high = pl.ds(r * rows + rows // 2, rows // 2)
        a.wait_recv()
        s = (z + 3) % 4
        c = go(remote(zbuf.at[s, low], zbuf.at[s, low], zs.at[r, 2], zr.at[r, 2], z_up))
        b.wait_recv()
        s = (z + 1) % 4
        d = go(remote(zbuf.at[s, high], zbuf.at[s, high], zs.at[r, 3], zr.at[r, 3], z_dn))
        z_far.append((c, d))

    plane = {}
    core_copies = []
    local_copies = []

    def to_sibling(buf, place, blks, sem, src=None):
        view = buf.at[core, place, blks, pl.ds(0, 2)]
        core_copies.append(go(remote(view if src is None else src, view, cs.at[sem], cr.at[sem], sib)))

    def project(r):
        for copy in z_far[r]:
            copy.wait_recv()
        at = pl.ds(r * rows, rows)
        full = jnp.concatenate([zbuf[s, at, :] for s in range(SIDE)], axis=1).astype(F32)
        normed = norm_rows(full, gain[...]).astype(BF16)
        queries = jnp.dot(normed, wqkv[0], preferred_element_type=F32)
        keys = jnp.dot(normed, wqkv[1], preferred_element_type=F32).astype(BF16)
        values = jnp.dot(normed, wqkv[2], preferred_element_type=F32)
        q_t = (queries.T.astype(BF16).astype(F32) * 0.125).astype(BF16)
        v_t = values.T.astype(BF16)
        for i in range(blocks):
            b = r * blocks + i
            cut = slice(i * BLK, (i + 1) * BLK)
            xown[b, 0] = keys[cut, :BLK]
            yown[b, 0] = keys[cut, BLK:]
            xown[b, 1] = v_t[:BLK, cut]
            yown[b, 1] = v_t[BLK:, cut]
            yown[b, 2] = q_t[:BLK, cut]
            xown[b, 2] = q_t[BLK:, cut]
        blks = pl.ds(r * blocks, blocks)
        for name, own, buf, place, send, recv, up, dn, k in (
            ("x", xown, xbuf, x, xs, xr, x_up, x_dn, 0),
            ("y", yown, ybuf, y, ys, yr, y_up, y_dn, 1),
        ):
            src, dst = own.at[blks], buf.at[core, place, blks]
            plane[name, r] = (
                go(remote(src, dst, send.at[r, 0], recv.at[r, 0], up)),
                go(remote(src, dst, send.at[r, 1], recv.at[r, 1], dn)),
            )
            local = pltpu.make_async_copy(src, dst, ls.at[r * 2 + k])
            local.start()
            local_copies.append(local)
            to_sibling(buf, place, blks, r * 10 + k * 5, own.at[blks, pl.ds(0, 2)])

    def plane_forward(r):
        blks = pl.ds(r * blocks, blocks)
        low = pl.ds(r * blocks, blocks // 2)
        high = pl.ds(r * blocks + blocks // 2, blocks // 2)
        for name, buf, place, send, recv, up, dn, k in (
            ("x", xbuf, x, xs, xr, x_up, x_dn, 0),
            ("y", ybuf, y, ys, yr, y_up, y_dn, 1),
        ):
            a, b = plane[name, r]
            a.wait_recv()
            s = (place + 3) % 4
            view = buf.at[core, s, low]
            c = go(remote(view, view, send.at[r, 2], recv.at[r, 2], up))
            to_sibling(buf, s, blks, r * 10 + k * 5 + 1)
            b.wait_recv()
            s = (place + 1) % 4
            view = buf.at[core, s, high]
            d = go(remote(view, view, send.at[r, 3], recv.at[r, 3], dn))
            to_sibling(buf, s, blks, r * 10 + k * 5 + 2)
            plane[name, r] = (c, d)

    def plane_finish(r):
        low = pl.ds(r * blocks, blocks // 2)
        high = pl.ds(r * blocks + blocks // 2, blocks // 2)
        for name, buf, place, k in (("x", xbuf, x, 0), ("y", ybuf, y, 1)):
            c, d = plane[name, r]
            s = (place + 2) % 4
            c.wait_recv()
            to_sibling(buf, s, low, r * 10 + k * 5 + 3)
            d.wait_recv()
            to_sibling(buf, s, high, r * 10 + k * 5 + 4)

    def near(b):
        for p, (own, other) in enumerate(((xown, yown), (yown, xown))):
            query = split_heads(other[b, 2])
            parts = []
            for step in (-1, 0, 1):
                if b + step < 0:
                    key, val, ok = halo_low[p, 0], halo_low[p, 1], loc > 0
                elif b + step >= NB:
                    key, val, ok = halo_high[p, 0], halo_high[p, 1], loc < 31
                else:
                    key, val, ok = own[b + step, 0], own[b + step, 1], None
                score = jnp.dot(key, query, preferred_element_type=F32)
                if ok is not None:
                    score = jnp.where(ok, score, NEG)
                parts.append((score, val))
            top = functools.reduce(
                jnp.maximum, [jnp.max(score, axis=0, keepdims=True) for score, _ in parts]
            )
            total = jnp.zeros((1, 2 * BLK), F32)
            out = jnp.zeros((BLK, 2 * BLK), F32)
            for score, val in parts:
                weight = jnp.exp(score - top)
                total = total + jnp.sum(weight, axis=0, keepdims=True)
                out = out + jnp.dot(val, weight.astype(BF16), preferred_element_type=F32)
            near_o[b, p] = jnp.concatenate(
                [out[:HD, :BLK] / total[:, :BLK], out[HD:, BLK:] / total[:, BLK:]], axis=0
            )
            near_st[b, p, 0:1] = top[:, :BLK]
            near_st[b, p, 1:2] = top[:, BLK:]
            near_st[b, p, 2:3] = total[:, :BLK]
            near_st[b, p, 3:4] = total[:, BLK:]
            near_st[b, p, 4:8] = jnp.zeros((4, BLK), F32)

    halos = []

    def halo_first(_):
        for p, own in enumerate((xown, yown)):
            halos.append(go(remote(own.at[0, pl.ds(0, 2)], halo_high.at[p], hs.at[p], hr.at[p], prv)))

    def halo_last(_):
        for p, own in enumerate((xown, yown)):
            src = own.at[NB - 1, pl.ds(0, 2)]
            halos.append(go(remote(src, halo_low.at[p], hs.at[2 + p], hr.at[2 + p], nxt)))

    def halo_wait(_):
        for copy in halos:
            copy.wait_recv()

    def rows_out(_):
        mine = pl.ds(pl.multiple_of(z * GROUP, GROUP), GROUP)
        ent_rows[...] = jnp.concatenate([zbuf[s, mine, :] for s in range(SIDE)], axis=1)

    def keys_out(_):
        for copy in tab_copies:
            copy.wait_recv()
        code = jnp.concatenate([tab_y[s][:, :NB] for s in range(SIDE)], axis=1)
        at_key = code // 16 % 2 * 32 + code // 32 % 4 * NB + code // 2 % NB
        key_a[...] = jnp.where((code % 2 == 1) & (code // 128 == y), at_key, -1)
        code = jnp.concatenate([tab_x[s][:, :NB] for s in range(SIDE)], axis=1)
        at_key = code // 16 % 2 * 32 + code // 128 * NB + code // 2 % NB
        key_b[...] = jnp.where((code % 2 == 1) & (code // 32 % 4 == x), at_key, -1)

    steps = {
        "zs": z_start, "zf": z_forward, "pr": project, "pf": plane_forward, "pe": plane_finish,
        "n": near, "ts": tab_start, "ws": weights_start, "wf": weights_forward, "we": weights_finish,
        "hf": halo_first, "hl": halo_last, "hw": halo_wait,
        "ro": rows_out, "ko": keys_out, "pp": prepare,
    }
    for name, place in ORDER:
        steps[name](place)
    for copy in core_copies:
        copy.wait_recv()
    for copy in local_copies:
        copy.wait()
    for copy in pending:
        copy.wait_send()


def gather_call(ent, gain, wqkv, tab, w_up, w_down):
    vmem = pl.BlockSpec(memory_space=pltpu.VMEM)
    hbm = pl.BlockSpec(memory_space=pl.ANY)
    pinned = pl.BlockSpec(memory_space=pltpu.HBM)
    dma = pltpu.SemaphoreType.DMA
    plane_shape = (2, SIDE, NB, 3, BLK, BLK)
    return pl.pallas_call(
        gather_kernel,
        out_shape=(
            jax.ShapeDtypeStruct(plane_shape, BF16),
            jax.ShapeDtypeStruct(plane_shape, BF16),
            jax.ShapeDtypeStruct((NB, 2, BLK, BLK), F32),
            jax.ShapeDtypeStruct((NB, 2, 8, BLK), F32),
            jax.ShapeDtypeStruct((GROUP, WIDTH), BF16),
            jax.ShapeDtypeStruct((8, SIDE * NB), jnp.int32),
            jax.ShapeDtypeStruct((8, SIDE * NB), jnp.int32),
            jax.ShapeDtypeStruct((SIDE, 2 * UNITS, WIDTH), BF16),
        ),
        in_specs=[pinned, vmem, pinned, vmem, pinned, pinned],
        out_specs=(hbm, hbm) + (vmem,) * 5 + (hbm,),
        scratch_shapes=[
            pltpu.VMEM((ROWS, PART), BF16),
            pltpu.VMEM((3, WIDTH, PART), BF16),
            pltpu.VMEM((SIDE, ROWS, PART), BF16),
            pltpu.VMEM((NB, 3, BLK, BLK), BF16),
            pltpu.VMEM((NB, 3, BLK, BLK), BF16),
            pltpu.VMEM((2, 2, BLK, BLK), BF16),
            pltpu.VMEM((2, 2, BLK, BLK), BF16),
            pltpu.VMEM((SIDE, NB, BLK), jnp.int32),
            pltpu.VMEM((SIDE, NB, BLK), jnp.int32),
            pltpu.VMEM((WIDTH, BLK), BF16),
            pltpu.VMEM((BLK, WIDTH), F32),
            pltpu.VMEM((2 * UNITS, WIDTH), BF16),
            dma((CHUNKS, 4)), dma((CHUNKS, 4)),
            dma((CHUNKS, 4)), dma((CHUNKS, 4)),
            dma((CHUNKS, 4)), dma((CHUNKS, 4)),
            dma((CHUNKS * 10,)), dma((CHUNKS * 10,)),
            dma((4,)), dma((4,)),
            dma((CHUNKS * 2,)),
            dma((2, 3)), dma((2, 3)),
            dma((8,)), dma((8,)),
            dma((6,)),
        ],
        compiler_params=pltpu.CompilerParams(
            collective_id=0, has_side_effects=True, vmem_limit_bytes=60 * MB
        ),
        name="gather_project",
    )(ent, gain, wqkv, tab, w_up, w_down)


def far_kernel(
    key_a, key_b, x_hbm, y_hbm, oa, ob, query, pairs, acc, state, hits_a, hits_b, qs, ks
):
    core = lax.axis_index("loc") % 2
    live_q = SIDE * NB
    mine = pl.ds(core * live_q, live_q)
    loads = []
    for pair, (keys_hbm, query_hbm) in enumerate(((x_hbm, y_hbm), (y_hbm, x_hbm))):
        loads.append(
            (
                pltpu.make_async_copy(query_hbm.at[mine, 2], query.at[pair], qs.at[pair]),
                pltpu.make_async_copy(keys_hbm.at[:, pl.ds(0, 2)], pairs.at[pair], ks.at[pair]),
            )
        )
    for pair in loads:
        for load in pair:
            load.start()

    def find(s, counts):
        counts = list(counts)
        for b in range(NB):
            for j in range(4):
                for pair, (keys, hits) in enumerate(((key_a, hits_a), (key_b, hits_b))):
                    key = keys[j, s * NB + b]
                    hits[counts[pair]] = (s * NB + b) * 1024 + key
                    counts[pair] = counts[pair] + jnp.where(key >= 0, 1, 0)
        return tuple(counts)

    counts = lax.fori_loop(0, SIDE, find, (0, 0))
    for hits, count in zip((hits_a, hits_b), counts):
        for extra in range(8):
            hits[count + extra] = live_q * 1024

    def clear(i, carry):
        acc[i] = jnp.zeros((BLK, BLK), F32)
        state[i, 0:2] = jnp.full((2, BLK), NEG, F32)
        state[i, 2:8] = jnp.zeros((6, BLK), F32)
        return carry

    lax.fori_loop(0, 2 * (live_q + 1), clear, 0)

    for pair in range(2):
        hits, count = (hits_a, counts[0]) if pair == 0 else (hits_b, counts[1])
        o_ref = oa if pair == 0 else ob
        base = pair * (live_q + 1)
        for load in loads[pair]:
            load.wait()

        def eight(step, carry):
            work = []
            for u in range(8):
                code = hits[step * 8 + u]
                q, k = lax.shift_right_logical(code, 10), code & 1023
                asked = split_heads(query[pair, jnp.minimum(q, live_q - 1)])
                key = pairs[pair, k, 0]
                val = pairs[pair, k, 1]
                score = jnp.dot(key, asked, preferred_element_type=F32)
                top = jnp.max(score, axis=0, keepdims=True)
                weight = jnp.exp(score - top)
                total = jnp.sum(weight, axis=0, keepdims=True)
                out = jnp.dot(val, weight.astype(BF16), preferred_element_type=F32)
                work.append((q + base, top, total, out))
            for q, top, total, out in work:
                for h in range(2):
                    cut = slice(h * BLK, (h + 1) * BLK)
                    feat = pl.ds(h * HD, HD)
                    old_top = state[q, h : h + 1]
                    new_top = jnp.maximum(old_top, top[:, cut])
                    keep = jnp.exp(old_top - new_top)
                    add = jnp.exp(top[:, cut] - new_top)
                    acc[q, feat] = acc[q, feat] * keep + out[h * HD : (h + 1) * HD, cut] * add
                    state[q, h : h + 1] = new_top
                    state[q, 2 + h : 3 + h] = state[q, 2 + h : 3 + h] * keep + total[:, cut] * add
            return carry

        lax.fori_loop(0, lax.shift_right_logical(count + 7, 3), eight, 0)

        def finish(i, carry):
            st = state[base + i]
            left, terms = st[0:4], []
            for _ in range(3):
                terms.append(left.astype(BF16).astype(F32))
                left = left - terms[-1]
            terms.append(jnp.zeros((4, BLK), F32))
            o_ref[i, BLK:] = jnp.concatenate(terms, axis=0).astype(BF16)
            for h in range(2):
                total = st[2 + h : 3 + h]
                scale = 1.0 / jnp.where(total > 0, total, 1.0)
                feat = pl.ds(h * HD, HD)
                o_ref[i, feat] = (acc[base + i, feat] * scale).astype(BF16)
            return carry

        lax.fori_loop(0, live_q, finish, 0)


def far_call(key_a, key_b, xbuf, ybuf):
    vmem = pl.BlockSpec(memory_space=pltpu.VMEM)
    smem = pl.BlockSpec(memory_space=pltpu.SMEM)
    hbm = pl.BlockSpec(memory_space=pltpu.HBM)
    dma = pltpu.SemaphoreType.DMA
    live_q = SIDE * NB
    o_shape = jax.ShapeDtypeStruct((live_q, TALL, BLK), BF16)
    flat = (2 * live_q, 3, BLK, BLK)
    oa, ob = pl.pallas_call(
        far_kernel,
        out_shape=(o_shape, o_shape),
        in_specs=[smem, smem, hbm, hbm],
        out_specs=(vmem, vmem),
        scratch_shapes=[
            pltpu.VMEM((2, live_q, BLK, BLK), BF16),
            pltpu.VMEM((2, 2 * live_q, 2, BLK, BLK), BF16),
            pltpu.VMEM((2 * (live_q + 1), BLK, BLK), F32),
            pltpu.VMEM((2 * (live_q + 1), 8, BLK), F32),
            pltpu.SMEM((live_q * 4 + 8,), jnp.int32),
            pltpu.SMEM((live_q * 4 + 8,), jnp.int32),
            dma((2,)),
            dma((2,)),
        ],
        compiler_params=pltpu.CompilerParams(vmem_limit_bytes=58 * MB),
        cost_estimate=pl.CostEstimate(
            flops=8 * 10**9, bytes_accessed=30 * MB, transcendentals=3 * 10**6
        ),
        name="far_partials",
    )(key_a, key_b, xbuf.reshape(flat), ybuf.reshape(flat))
    shape = (SIDE, NB, TALL, BLK)
    return oa.reshape(shape), ob.reshape(shape)


def merge_kernel(
    oa, ob, near_o_hbm, near_st_hbm, ent_rows_hbm, w_out_hbm, gain, line_0, line_1, line_2, line_3, side_dn, side_up, result,
    ra, rb, relay, att, part, got_half, got,
    weights, inner, acc, send_sib, got_sib, res, landed, near_o, near_st, ent_rows, w_out,
    os, orr, fs, fr, zs, zr, ws, wr, wl, ss, sr, es, er, ls,
):
    y, x, core, z = coords()
    z_up, z_dn = shifted("z", 1), shifted("z", -1)
    z_opp, sib = shifted("z", 2), shifted("c", 0)
    peers = [shifted("y", 1), shifted("y", -1), shifted("x", 1), shifted("x", -1), z_up, z_dn]
    w_place = y * (1 - core) + x * core
    w_up_to = device(y + 1 - core, x + core, core, z)
    w_dn_to = device(y + 3 * (1 - core), x + 3 * core, core, z)
    peers = peers + [z_opp, sib]
    greet(peers)
    loads = [
        pltpu.make_async_copy(src, dst, ls.at[n])
        for n, (src, dst) in enumerate(
            (
                (oa.at[y], ra.at[y]),
                (ob.at[x], rb.at[x]),
                (near_o_hbm, near_o),
                (near_st_hbm, near_st),
                (w_out_hbm, w_out),
                (ent_rows_hbm, ent_rows),
            )
        )
    ]
    for load in loads:
        load.start()
    line = (line_0, line_1, line_2, line_3)
    w_local = [
        pltpu.make_async_copy(line[n], weights.at[w_place, n], wl.at[n]) for n in range(SIDE)
    ]
    w_sides = [
        pltpu.make_async_copy(side_dn, weights.at[(w_place + 3) % 4, 0], wl.at[SIDE]),
        pltpu.make_async_copy(side_up, weights.at[(w_place + 1) % 4, 0], wl.at[SIDE + 1]),
    ]
    for copy in w_local + w_sides:
        copy.start()
    greeted(peers)
    pending = []

    def go(copy):
        copy.start()
        pending.append(copy)
        return copy

    groups = [(z + by) % 4 for by in (2, 1, 3, 0)]
    per = NB // SIDE
    lanes = ((y, peers[0], peers[1], oa, ra), (x, peers[2], peers[3], ob, rb))
    relays, arrivals = {}, {}
    for n, g in enumerate(groups):
        arrivals[n] = []
        for k, (place, up, dn, o, ro) in enumerate(lanes):
            send, recv = os.at[k, n], orr.at[k, n]
            far_to, up_to, dn_to = (place + 2) % 4, (place + 1) % 4, (place + 3) % 4
            relays[k, n] = (
                go(remote(o.at[far_to, g * per], relay.at[k, n, 0], send.at[0], recv.at[0], up)),
                go(remote(o.at[far_to, g * per + 1], relay.at[k, n, 1], send.at[1], recv.at[1], dn)),
            )
            both = pl.ds(g * per, per)
            arrivals[n] += [
                go(remote(o.at[up_to, both], ro.at[place, both], send.at[2], recv.at[2], up)),
                go(remote(o.at[dn_to, both], ro.at[place, both], send.at[3], recv.at[3], dn)),
            ]

    def pass_on(n):
        g = groups[n]
        for k, (place, up, dn, o, ro) in enumerate(lanes):
            a, b = relays[k, n]
            a.wait_recv()
            dst = ro.at[(place + 3) % 4, g * per]
            arrivals[n].append(go(remote(relay.at[k, n, 0], dst, fs.at[k, n, 0], fr.at[k, n, 0], up)))
            b.wait_recv()
            dst = ro.at[(place + 1) % 4, g * per + 1]
            arrivals[n].append(go(remote(relay.at[k, n, 1], dst, fs.at[k, n, 1], fr.at[k, n, 1], dn)))

    pass_on(0)
    pass_on(1)
    w_up_copies, w_dn_copies = [None] * 4, [None] * 4

    def weights_start():
        dst = weights.at[w_place]
        for u, d in ((1, 2), (2, 3), (3, 1)):
            w_up_copies[u] = go(remote(line[u], dst.at[u], ws.at[0, u], wr.at[0, u], w_up_to))
            w_dn_copies[d] = go(remote(line[d], dst.at[d], ws.at[1, d], wr.at[1, d], w_dn_to))

    pass_on(2)
    pass_on(3)
    weights_start()
    w_far = []

    def weights_forward(n):
        if n == 0:
            for copy in w_sides:
                copy.wait()
        else:
            w_up_copies[n].wait_recv()
        view = weights.at[(w_place + 3) % 4, n]
        w_far.append(go(remote(view, view, ws.at[2, n], wr.at[2, n], w_up_to)))
        w_dn_copies[n + 2].wait_recv()
        view = weights.at[(w_place + 1) % 4, n + 2]
        w_far.append(go(remote(view, view, ws.at[2, n + 2], wr.at[2, n + 2], w_dn_to)))

    for load in loads:
        load.wait()

    def merge(b, carry):
        for p, ro in enumerate((ra, rb)):
            stats, outs = [near_st[b, p]], [near_o[b, p]]
            for s in range(SIDE):
                tail = ro[s, b, BLK:].astype(F32)
                stats.append(tail[0:4] + tail[4:8] + tail[8:12])
                outs.append(ro[s, b, :BLK].astype(F32))
            halves = []
            for h in range(2):
                top = functools.reduce(jnp.maximum, [st[h : h + 1] for st in stats])
                scale = [st[2 + h : 3 + h] * jnp.exp(st[h : h + 1] - top) for st in stats]
                inv = 1.0 / functools.reduce(jnp.add, scale)
                halves.append(
                    functools.reduce(
                        jnp.add,
                        [o[h * HD : (h + 1) * HD] * (w * inv) for o, w in zip(outs, scale)],
                    )
                )
            tile = jnp.concatenate(halves, axis=0).T.astype(BF16)
            att[pl.ds(pl.multiple_of(b * BLK, BLK), BLK), p * BLK : (p + 1) * BLK] = tile
        return carry

    def project(n):
        for copy in arrivals[n]:
            copy.wait_recv()
        lax.fori_loop(groups[n] * per, groups[n] * per + per, merge, 0)
        rows = att[pl.ds(pl.multiple_of(groups[n] * GROUP, GROUP), GROUP), :]
        return jnp.dot(rows, w_out[...], preferred_element_type=F32)

    h = GROUP // 2
    part[0] = project(0).astype(BF16)
    f_up = go(remote(part.at[0, pl.ds(0, h)], got_half.at[0], zs.at[0], zr.at[0], z_up))
    f_dn = go(remote(part.at[0, pl.ds(h, h)], got_half.at[1], zs.at[1], zr.at[1], z_dn))
    to_up = project(1)
    part[1, h:] = to_up[h:].astype(BF16)
    f_up.wait_recv()
    part[1, :h] = (to_up[:h] + got_half[0].astype(F32)).astype(BF16)
    s_up = go(remote(part.at[1], got.at[0], zs.at[2], zr.at[2], z_up))
    weights_forward(0)
    to_dn = project(2)
    part[2, :h] = to_dn[:h].astype(BF16)
    f_dn.wait_recv()
    part[2, h:] = (to_dn[h:] + got_half[1].astype(F32)).astype(BF16)
    s_dn = go(remote(part.at[2], got.at[1], zs.at[3], zr.at[3], z_dn))
    mine = project(3) + ent_rows[...].astype(F32)
    weights_forward(1)
    s_up.wait_recv()
    s_dn.wait_recv()
    mixed = mine + got[0].astype(F32) + got[1].astype(F32)
    inner[core] = norm_rows(mixed, gain[...]).astype(BF16)
    to_sib = go(remote(inner.at[core], inner.at[core], ss.at[0], sr.at[0], sib))
    acc[core] = mixed
    acc[1 - core] = jnp.zeros((GROUP, WIDTH), F32)
    for copy in w_local:
        copy.wait()

    def mlp(slot, who):
        w_up = weights[slot, :, :, 0:UNITS].reshape(SIDE * SIDE * UNITS, WIDTH)
        w_down = weights[slot, :, :, UNITS:].reshape(SIDE * SIDE * UNITS, WIDTH)
        hidden = lax.dot_general(
            inner[who], w_up, (((1,), (1,)), ((), ())), preferred_element_type=F32
        )
        acc[who] += jnp.dot(gelu(hidden).astype(BF16), w_down, preferred_element_type=F32)

    def mlp_both(slot):
        def body(t, carry):
            mlp(slot, (core + 1 + t) % 2)
            return carry

        lax.fori_loop(0, 2, body, 0)

    to_sib.wait_recv()
    mlp_both(w_place)
    w_up_copies[2].wait_recv()
    w_up_copies[3].wait_recv()
    mlp_both((w_place + 3) % 4)
    w_dn_copies[1].wait_recv()
    mlp_both((w_place + 1) % 4)
    for copy in w_far:
        copy.wait_recv()
    mlp((w_place + 2) % 4, 1 - core)
    send_sib[...] = acc[1 - core].astype(BF16)
    back = go(remote(send_sib, got_sib, ss.at[1], sr.at[1], sib))
    mlp((w_place + 2) % 4, core)
    back.wait_recv()
    final = (acc[core] + got_sib[...].astype(F32)).astype(BF16)
    for s in range(SIDE):
        res[s] = final[:, s * PART : (s + 1) * PART]
    copies = []
    for n, to in ((2, z_opp), (1, z_up), (3, z_dn)):
        copies.append(go(remote(res.at[(z + n) % 4], landed.at[z], es.at[n], er.at[n], to)))
    result[pl.ds(pl.multiple_of(z * GROUP, GROUP), GROUP), :] = res[z]
    for copy in copies:
        copy.wait_recv()
    for n in range(1, SIDE):
        s = (z + n) % 4
        result[pl.ds(pl.multiple_of(s * GROUP, GROUP), GROUP), :] = landed[s]
    for copy in pending:
        copy.wait_send()


def gelu(v):
    return 0.5 * v * (1.0 + lax.erf(v * 0.7071067811865476))


def merge_call(oa, ob, near_o, near_st, ent_rows, w_out, gain, lines):
    vmem = pl.BlockSpec(memory_space=pltpu.VMEM)
    hbm = pl.BlockSpec(memory_space=pltpu.HBM)
    dma = pltpu.SemaphoreType.DMA
    return pl.pallas_call(
        merge_kernel,
        out_shape=jax.ShapeDtypeStruct((ROWS, PART), BF16),
        in_specs=[hbm] * 6 + [vmem] + [pl.BlockSpec(memory_space=pl.ANY)] * 6,
        out_specs=vmem,
        scratch_shapes=[
            pltpu.VMEM((SIDE, NB, TALL, BLK), BF16),
            pltpu.VMEM((SIDE, NB, TALL, BLK), BF16),
            pltpu.VMEM((2, SIDE, 2, TALL, BLK), BF16),
            pltpu.VMEM((ROWS, 2 * BLK), BF16),
            pltpu.VMEM((3, GROUP, WIDTH), BF16),
            pltpu.VMEM((2, GROUP // 2, WIDTH), BF16),
            pltpu.VMEM((2, GROUP, WIDTH), BF16),
            pltpu.VMEM((SIDE, SIDE, SIDE, 2 * UNITS, WIDTH), BF16),
            pltpu.VMEM((2, GROUP, WIDTH), BF16),
            pltpu.VMEM((2, GROUP, WIDTH), F32),
            pltpu.VMEM((GROUP, WIDTH), BF16),
            pltpu.VMEM((GROUP, WIDTH), BF16),
            pltpu.VMEM((SIDE, GROUP, PART), BF16),
            pltpu.VMEM((SIDE, GROUP, PART), BF16),
            pltpu.VMEM((NB, 2, BLK, BLK), F32),
            pltpu.VMEM((NB, 2, 8, BLK), F32),
            pltpu.VMEM((GROUP, WIDTH), BF16),
            pltpu.VMEM((PART, WIDTH), BF16),
            dma((2, 4, 4)), dma((2, 4, 4)),
            dma((2, 4, 2)), dma((2, 4, 2)),
            dma((4,)), dma((4,)),
            dma((3, 4)), dma((3, 4)), dma((6,)),
            dma((2,)), dma((2,)),
            dma((4,)), dma((4,)),
            dma((8,)),
        ],
        compiler_params=pltpu.CompilerParams(
            collective_id=1, has_side_effects=True, vmem_limit_bytes=50 * MB
        ),
        name="merge_project",
    )(oa, ob, near_o, near_st, ent_rows, w_out, gain, *lines)


def on_device(
    entities, attn_gain, w_qkv, w_out, mlp_gain, w_up, w_down, far_owner, far_local, far_live
):
    xbuf, ybuf, near_o, near_st, ent_rows, key_a, key_b, piece = gather_call(
        entities,
        attn_gain.reshape(1, WIDTH),
        w_qkv,
        jnp.pad(((far_owner * NB + far_local) * 2 + far_live).T, ((0, 4), (0, BLK - NB))),
        w_up,
        w_down,
    )
    def along(by, turn=0):
        pairs = []
        for i in range(lax.axis_size("loc")):
            y, x, core = i // 8, i // 2 % 4, i % 2
            y, x = (y, (x + by) % 4) if core == turn else ((y + by) % 4, x)
            pairs.append((i, (y * 4 + x) * 2 + core))
        return lax.ppermute(piece, "loc", pairs)

    lines = [piece] + [along(by) for by in (3, 1, 2)] + [along(by, 1) for by in (1, 3)]
    oa, ob = far_call(key_a, key_b, xbuf, ybuf)
    return merge_call(
        oa, ob, near_o, near_st, ent_rows, w_out, mlp_gain.reshape(1, WIDTH), lines
    )


def solution(mesh):
    return jax.shard_map(
        on_device,
        mesh=mesh,
        in_specs=(
            P("loc", "head"),
            P(),
            P(None, None, "head"),
            P("head", None),
            P(),
            P(None, "head"),
            P("head", None),
            P("loc", None),
            P("loc", None),
            P("loc", None),
        ),
        out_specs=P("loc", "head"),
        check_vma=False,
    )
```
